32 devices in a mesh: dp: 8 (over z, x), tp: 4 (over y, core).
Axes of the slice: x: 2, y: 2, z: 4, core: 2. Of those that a mesh axis runs over, the one named last changes fastest.
Arguments:
- hidden_in: bfloat16 [1024, 16, 768], P('tp', 'dp'), may hold values from -6 to 6
- segment_ids: int32 [16, 1024], P('dp'), may hold values from 0 to 4, as said below
- cotangent: bfloat16 [1024, 16, 768], P('tp', 'dp'), may hold values from -6 to 6
- norm1_gain: bfloat16 [768], replicated, may hold values from 0.099609375 to 1.8984375
- norm1_bias: bfloat16 [768], replicated, may hold values from -3 to 3
- qkv_weight: bfloat16 [3, 768, 768], P(None, None, 'tp'), may hold values from -0.21875 to 0.21875
- qkv_bias: bfloat16 [3, 768], P(None, 'tp'), may hold values from -3 to 3
- out_weight: bfloat16 [768, 768], P('tp'), may hold values from -0.875 to 0.875
- out_bias: bfloat16 [768], replicated, may hold values from -3 to 3
- norm2_gain: bfloat16 [768], replicated, may hold values from 0.099609375 to 1.8984375
- norm2_bias: bfloat16 [768], replicated, may hold values from -3 to 3
- ffn_in_weight: bfloat16 [768, 3072], P(None, 'tp'), may hold values from -0.21875 to 0.21875
- ffn_in_bias: bfloat16 [3072], P('tp'), may hold values from -3 to 3
- ffn_out_weight: bfloat16 [3072, 768], P('tp'), may hold values from -0.15625 to 0.15625
- ffn_out_bias: bfloat16 [768], replicated, may hold values from -3 to 3
Outputs:
- block_out: bfloat16 [1024, 16, 768], P('tp', 'dp')
- input_grad: float32 [1024, 16, 768], P('tp', 'dp')
- norm1_gain_grad: float32 [768], replicated
- norm1_bias_grad: float32 [768], replicated
- qkv_weight_grad: float32 [3, 768, 768], P(None, None, 'tp')
- qkv_bias_grad: float32 [3, 768], P(None, 'tp')
- out_weight_grad: float32 [768, 768], P('tp')
- out_bias_grad: float32 [768], replicated
- norm2_gain_grad: float32 [768], replicated
- norm2_bias_grad: float32 [768], replicated
- ffn_in_weight_grad: float32 [768, 3072], P(None, 'tp')
- ffn_in_bias_grad: float32 [3072], P('tp')
- ffn_out_weight_grad: float32 [3072, 768], P('tp')
- ffn_out_bias_grad: float32 [768], replicated
The draws below stay inside these ranges and needn't reach their ends.
Inputs may be any that keep to these rules, and one draw needn't show every extreme that they name: `segment_ids`: along each row the ids never fall, begin at 0 and end at 4: every row holds five genes. Codons with equal ids form one gene, and attention stays within a gene.
All inputs are finite; a program needn't handle non-finite values.
Results may differ from the reference program's by a relative error of at most 0.018.
Values may be sent and summed in bfloat16 or wider, within the bound.
No kernel may reach another device: no remote copies, remote signals or barrier semaphores. Data moves between devices by JAX's collectives and lax.ppermute only.
A program may use at most 128 MiB of HBM per device.

```python
import jax
import jax.numpy as jnp
from jax import lax

D = 768
HEADS = 12
HEAD_DIM = 64
FF = 3072
LEN = 1024
ROWS = 2
BATCH = 16


def draw_segment_ids(key, part):
    key = jax.random.fold_in(key, 7)
    cut_key, pick_key = jax.random.split(key)
    places = jnp.arange(LEN, dtype=jnp.int32)
    quarter = LEN // 4
    eighth = LEN // 8
    drawn_low = jnp.array([1, quarter + 1, 2 * quarter + 1, 3 * quarter + 1], dtype=jnp.int32)
    drawn_high = jnp.array([quarter, 2 * quarter, 3 * quarter, LEN], dtype=jnp.int32)
    long_low = jnp.array([1, eighth, 3 * quarter + 1, 7 * eighth], dtype=jnp.int32)
    long_high = jnp.array([eighth, quarter, 7 * eighth, LEN], dtype=jnp.int32)
    picked = jax.random.randint(pick_key, (BATCH // ROWS,), 0, ROWS)
    chosen = jnp.arange(BATCH, dtype=jnp.int32) % ROWS == jnp.repeat(picked, ROWS)
    lows = jnp.where(chosen[:, None], long_low[None, :], drawn_low[None, :])
    highs = jnp.where(chosen[:, None], long_high[None, :], drawn_high[None, :])
    raw = jax.random.randint(cut_key, (BATCH, 4), 0, 1048576)
    cuts = lows + raw % (highs - lows)
    return jnp.sum((places[None, None, :] >= cuts[:, :, None]).astype(jnp.int32), axis=1).astype(jnp.int32)


def steps_of(key, dims, cuts, least, high):
    level, own = 1.0, jax.random.fold_in(key, 6)
    for axis_at, parts in cuts:
        steps = jnp.exp(jax.random.uniform(jax.random.fold_in(own, axis_at), (parts,), jnp.float32, least / len(cuts), high / len(cuts)))
        level = level * jnp.repeat(steps, dims[axis_at] // parts).reshape([-1 if axis == axis_at else 1 for axis in range(len(dims))])
    return level


def scatter_about(key, dims, scale, most, shards=(), kind=jnp.bfloat16):
    entries = jax.random.normal(key, dims, jnp.float32) * scale
    if len(shards) > 0:
        entries = steps_of(key, dims, shards, -0.22, 0.18) * entries
    return jnp.clip(entries, min=-most, max=most).astype(kind)


def setup_inputs(seed: int = 0) -> dict:
    splits = jax.random.split(jax.random.key(seed), 16)
    hidden_in = scatter_about(splits[0], (LEN, BATCH, D), 1.0, 6.0, ((0, 4), (1, 8)))
    segment_ids = draw_segment_ids(jax.random.fold_in(splits[15], 71), 0)
    cotangent = scatter_about(splits[2], (LEN, BATCH, D), 1.0, 6.0, ((0, 4), (1, 8)))
    norm1_gain = jnp.clip(1.0 + 0.18 * jax.random.normal(splits[3], (D,), jnp.float32), 0.099609375, 1.8984375).astype(jnp.bfloat16)
    norm1_bias = scatter_about(splits[4], (D,), 0.5, 3.0)
    qkv_weight = scatter_about(splits[5], (3, D, D), D ** -0.5, 0.21875, ((2, 4),))
    qkv_bias = scatter_about(splits[6], (3, D), 0.5, 3.0, ((1, 4),))
    out_weight = scatter_about(splits[7], (D, D), (D // 16) ** -0.5, 0.875, ((0, 4),))
    out_bias = scatter_about(splits[8], (D,), 0.5, 3.0)
    norm2_gain = jnp.clip(1.0 + 0.18 * jax.random.normal(splits[9], (D,), jnp.float32), 0.099609375, 1.8984375).astype(jnp.bfloat16)
    norm2_bias = scatter_about(splits[10], (D,), 0.5, 3.0)
    ffn_in_weight = scatter_about(splits[11], (D, FF), D ** -0.5, 0.21875, ((1, 4),))
    ffn_in_bias = scatter_about(splits[12], (FF,), 0.5, 3.0, ((0, 4),))
    ffn_out_weight = scatter_about(splits[13], (FF, D), (FF // 2) ** -0.5, 0.15625, ((0, 4),))
    ffn_out_bias = scatter_about(splits[14], (D,), 0.5, 3.0)
    return dict(hidden_in=hidden_in, segment_ids=segment_ids, cotangent=cotangent, norm1_gain=norm1_gain, norm1_bias=norm1_bias, qkv_weight=qkv_weight, qkv_bias=qkv_bias, out_weight=out_weight, out_bias=out_bias, norm2_gain=norm2_gain, norm2_bias=norm2_bias, ffn_in_weight=ffn_in_weight, ffn_in_bias=ffn_in_bias, ffn_out_weight=ffn_out_weight, ffn_out_bias=ffn_out_bias)


EPSILON = 1e-05
MASKED = -1000000000.0
HIGHEST = lax.Precision.HIGHEST

@jax.custom_vjp
def low(v):
    return lax.optimization_barrier(v.astype(jnp.bfloat16)).astype(jnp.float32)

@jax.custom_vjp
def low_back(v):
    return v

def low_keep(v):
    return (low(v), None)

def low_pass(kept, grad):
    return (grad,)

def back_keep(v):
    return (v, None)

def back_low(kept, grad):
    return (low(grad),)
low.defvjp(low_keep, low_pass)
low_back.defvjp(back_keep, back_low)

def layer_norm(values, norm_gain, norm_bias):
    average = lax.optimization_barrier(jnp.mean(values, axis=-1, keepdims=True))
    centered = values - average
    variance = lax.optimization_barrier(jnp.mean(centered * centered, axis=-1, keepdims=True))
    return centered * lax.rsqrt(variance + EPSILON) * norm_gain + norm_bias

def frequencies(head_size):
    indices = jnp.arange(head_size // 2, dtype=jnp.float32)
    return jnp.power(10000.0, -2.0 * indices / head_size)

def positions(segments):
    length = segments.shape[-1]
    indices = jnp.arange(length, dtype=jnp.int32)
    change = segments[..., 1:] != segments[..., :-1]
    opening = jnp.concatenate([jnp.ones(segments.shape[:-1] + (1,), dtype=bool), change], axis=-1)
    begins = lax.cummax(jnp.where(opening, indices, 0), axis=segments.ndim - 1)
    return (indices - begins).astype(jnp.float32)

def rotate(values, cosine, sine_vals):
    half_width = values.shape[-1] // 2
    lower_part = values[..., :half_width]
    upper_part = values[..., half_width:]
    return jnp.concatenate([lower_part * cosine - upper_part * sine_vals, upper_part * cosine + lower_part * sine_vals], axis=-1)

def attend_block(query_block, segment_block, key_heads, value_heads, row_seg):
    scores = jnp.einsum('qhd,khd->hqk', query_block, key_heads, precision=HIGHEST) * HEAD_DIM ** (-0.5)
    scores = low_back(scores)
    allowed = segment_block[:, None] == row_seg[None, :]
    scores = jnp.where(allowed[None], scores, MASKED)
    row_peak = lax.optimization_barrier(jnp.max(scores, axis=-1, keepdims=True))
    exponent = jnp.exp(scores - row_peak)
    probabilities = low(exponent / lax.optimization_barrier(jnp.sum(exponent, axis=-1, keepdims=True)))
    return jnp.einsum('hqk,khd->qhd', probabilities, value_heads, precision=HIGHEST)

def row_forward(weights, activations, row_seg):
    gain_one, bias_one, qkv_w, qkv_b, out_w, out_b, gain_two, bias_two, in_w, in_b, down_w, down_b = weights
    length = activations.shape[0]
    first_norm = low(layer_norm(activations, gain_one, bias_one))
    projected = jnp.einsum('ld,cde->cle', first_norm, qkv_w, precision=HIGHEST) + qkv_b[:, None, :]
    projected = low_back(projected)
    head_cols = projected.reshape(3, length, HEADS, HEAD_DIM)
    angles = positions(row_seg)[:, None, None] * frequencies(HEAD_DIM)
    cosine = jnp.cos(angles)
    sine_vals = jnp.sin(angles)
    query_heads = low(rotate(head_cols[0], cosine, sine_vals))
    key_heads = low(rotate(head_cols[1], cosine, sine_vals))
    value_heads = low(head_cols[2])
    block_size = min(512, length)
    blocks = length // block_size
    query_blocks = query_heads.reshape(blocks, block_size, HEADS, HEAD_DIM)
    segment_blocks = row_seg.reshape(blocks, block_size)
    checked = jax.checkpoint(attend_block)
    attended = lax.map(lambda inputs: checked(inputs[0], inputs[1], key_heads, value_heads, row_seg), (query_blocks, segment_blocks))
    attended = attended.reshape(length, HEADS * HEAD_DIM)
    attended = low(low_back(attended))
    branch = low_back(jnp.dot(attended, out_w, precision=HIGHEST) + out_b)
    middle = activations + branch
    second_norm = low(layer_norm(middle, gain_two, bias_two))
    pre_gelu = low_back(jnp.dot(second_norm, in_w, precision=HIGHEST) + in_b)
    activated = low(jax.nn.gelu(pre_gelu, approximate=False))
    feed_out = low_back(jnp.dot(activated, down_w, precision=HIGHEST) + down_b)
    return middle + feed_out

def reference(hidden_in, segment_ids, cotangent, norm1_gain, norm1_bias, qkv_weight, qkv_bias, out_weight, out_bias, norm2_gain, norm2_bias, ffn_in_weight, ffn_in_bias, ffn_out_weight, ffn_out_bias):
    params = tuple((item.astype(jnp.float32) for item in (norm1_gain, norm1_bias, qkv_weight, qkv_bias, out_weight, out_bias, norm2_gain, norm2_bias, ffn_in_weight, ffn_in_bias, ffn_out_weight, ffn_out_bias)))
    rows_in = jnp.transpose(hidden_in.astype(jnp.float32), (1, 0, 2))
    rows_cot = jnp.transpose(cotangent.astype(jnp.float32), (1, 0, 2))

    def one_row(totals, inputs):
        row_in, row_seg, row_cot = inputs

        def forward(weights, activations):
            return row_forward(weights, activations, row_seg)
        result, pullback = jax.vjp(forward, params, row_in)
        gradients, in_grad = pullback(row_cot)
        totals = jax.tree.map(lambda total_grad, new_grad: total_grad + new_grad, totals, gradients)
        return (totals, (result.astype(jnp.bfloat16), in_grad))
    zero_tree = jax.tree.map(jnp.zeros_like, params)
    totals, (outputs, in_grads) = lax.scan(one_row, zero_tree, (rows_in, segment_ids, rows_cot))
    return (jnp.transpose(outputs, (1, 0, 2)), jnp.transpose(in_grads, (1, 0, 2)), totals[0], totals[1], totals[2], totals[3], totals[4], totals[5], totals[6], totals[7], totals[8], totals[9], totals[10], totals[11])
```

```python
from functools import partial

import jax
import jax.numpy as jnp
from jax import lax
from jax.experimental import pallas as pl
from jax.experimental.pallas import tpu as pltpu
from jax.sharding import PartitionSpec as P

HEAD_DIM = 64
HALF = HEAD_DIM // 2
KEY_ROWS = 128
EPSILON = 1e-05
APART = -1e30
F32 = jnp.float32
BF16 = jnp.bfloat16

NN = (((1,), (0,)), ((), ()))
NT = (((1,), (1,)), ((), ()))
TN = (((0,), (0,)), ((), ()))


def dot(a, b, dims=NN):
    return lax.dot_general(a, b, dims, preferred_element_type=F32)


def shape(dims, dtype=BF16):
    return jax.ShapeDtypeStruct(dims, dtype)


def run(body, name, scalars, arrays, outs, scratch=(), flops=0, vmem=48):
    moved = sum(a.size * a.dtype.itemsize for a in arrays) + sum(
        o.size * jnp.dtype(o.dtype).itemsize for o in outs
    )
    return pl.pallas_call(
        body,
        out_shape=tuple(outs),
        in_specs=[pl.BlockSpec(memory_space=pltpu.SMEM)] * len(scalars)
        + [pl.BlockSpec(memory_space=pltpu.VMEM)] * len(arrays),
        out_specs=tuple(pl.BlockSpec(memory_space=pltpu.VMEM) for _ in outs),
        scratch_shapes=list(scratch),
        compiler_params=pltpu.CompilerParams(vmem_limit_bytes=vmem * 1024 * 1024),
        cost_estimate=pl.CostEstimate(flops=int(flops), bytes_accessed=int(moved), transcendentals=0),
        name=name,
    )(*scalars, *arrays)


def normalize(values):
    average = jnp.mean(values, axis=-1, keepdims=True)
    centered = values - average
    variance = jnp.mean(centered * centered, axis=-1, keepdims=True)
    inverse = lax.rsqrt(variance + EPSILON)
    return centered * inverse, inverse


def normalize_back(gradient, scaled, inverse, gain):
    grad_scaled = gradient * gain
    return inverse * (
        grad_scaled
        - jnp.mean(grad_scaled, axis=-1, keepdims=True)
        - scaled * jnp.mean(grad_scaled * scaled, axis=-1, keepdims=True)
    )


def first_norm_kernel(rows, width, hid, gain, bias, *outs):
    for r in range(rows):
        values = hid[:, r * width : (r + 1) * width].astype(F32)
        scaled, _ = normalize(values)
        outs[r][...] = (scaled * gain[...] + bias[...]).astype(BF16)


def project_kernel(far, place, one, two, weight, bias, cosine, sine, out):
    block = one.shape[0]
    local = weight.shape[0] // 3
    half = place[1] ^ far
    for k, tokens in enumerate((one, two)):
        spot = pl.multiple_of(((place[0] & 1) ^ k) * block, block)
        span = pl.ds(spot, block)
        table = pl.ds(pl.multiple_of(half * (2 * block) + spot, block), block)
        turned = dot(weight[...], tokens[...], NT) + bias[...]
        cs = cosine[:, table]
        sn = sine[:, table]
        for c in range(2):
            for base in range(c * local, (c + 1) * local, HEAD_DIM):
                a = turned[base : base + HALF]
                b = turned[base + HALF : base + HEAD_DIM]
                new_a = a * cs - b * sn
                new_b = b * cs + a * sn
                if c == 0:
                    new_a = new_a * HEAD_DIM**-0.5
                    new_b = new_b * HEAD_DIM**-0.5
                out[base : base + HALF, span] = new_a.astype(BF16)
                out[base + HALF : base + HEAD_DIM, span] = new_b.astype(BF16)
        out[2 * local :, span] = turned[2 * local :].astype(BF16)


def turn_over(values):
    return jnp.transpose(values.astype(F32)).astype(BF16)


def lay_out(place, near, far, mine, others, queries, keys):
    width = near.shape[1]
    local = near.shape[0] // 3
    heads = local // HEAD_DIM
    marks = mine.shape[0]
    for source, at in ((near, place[1] * width), (far, (1 - place[1]) * width)):
        at = pl.multiple_of(at, width)
        span = pl.ds(at, width)
        for h in range(heads):
            queries[h * KEY_ROWS : h * KEY_ROWS + HEAD_DIM, span] = source[
                h * HEAD_DIM : (h + 1) * HEAD_DIM, :
            ]
            column = jnp.concatenate(
                [
                    source[local + h * HEAD_DIM : local + (h + 1) * HEAD_DIM, :],
                    others[:, span],
                    jnp.zeros((KEY_ROWS - HEAD_DIM - marks, width), BF16),
                ],
                axis=0,
            )
            keys[h, span, :] = turn_over(column)
    for h in range(heads):
        queries[h * KEY_ROWS + HEAD_DIM : h * KEY_ROWS + HEAD_DIM + marks, :] = mine[...]
        queries[h * KEY_ROWS + HEAD_DIM + marks : (h + 1) * KEY_ROWS, :] = jnp.zeros(
            (KEY_ROWS - HEAD_DIM - marks, queries.shape[1]), BF16
        )


def attend_kernel(place, windows, near, far, mine, others, *rest):
    outs, (log_norm, queries, keys, values, attended) = rest[:4], rest[4:]
    width = near.shape[1]
    block = width // 2
    local = near.shape[0] // 3
    heads = local // HEAD_DIM
    lay_out(place, near, far, mine, others, queries, keys)
    for source, at in ((near, place[1] * width), (far, (1 - place[1]) * width)):
        values[:, pl.ds(pl.multiple_of(at, width), width)] = source[2 * local :, :]

    @pl.loop(0, 4)
    def _(quarter):
        span = pl.ds(pl.multiple_of(quarter * block, block), block)
        start = pl.multiple_of(windows[quarter], 128)
        count = windows[4 + quarter]

        def work(blocks):
            window = pl.ds(start, blocks * block)
            for h in range(heads):
                scores = dot(
                    keys[h, window, :], queries[h * KEY_ROWS : (h + 1) * KEY_ROWS, span]
                )
                peak = jnp.max(scores, axis=0, keepdims=True)
                weights = jnp.exp(scores - peak)
                total = jnp.sum(weights, axis=0, keepdims=True)
                out = dot(
                    values[h * HEAD_DIM : (h + 1) * HEAD_DIM, window], weights.astype(BF16)
                )
                attended[h * HEAD_DIM : (h + 1) * HEAD_DIM, span] = (
                    out * (1.0 / total)
                ).astype(BF16)
                log_norm[h : h + 1, span] = peak + jnp.log(total)

        for blocks in range(1, 5):
            pl.when(count == blocks)(partial(work, blocks))

    for s, out in enumerate(outs):
        out[...] = attended[:, pl.ds(pl.multiple_of((place[0] ^ s) * block, block), block)]


def attend_back_kernel(
    place, windows, near, far, mine, others, log_norm, cosine, sine, weight, *rest
):
    grads, outs, scratch = rest[:4], rest[4:9], rest[9:]
    grad_proj, partials = outs[0], outs[1:]
    queries, keys, key_rows, value_cols, query_cols, grad_rows, grad_cols, dk, dv, dq = scratch
    width = near.shape[1]
    block = width // 2
    local = near.shape[0] // 3
    heads = local // HEAD_DIM
    lay_out(place, near, far, mine, others, queries, keys)
    for source, at in ((near, place[1] * width), (far, (1 - place[1]) * width)):
        span = pl.ds(pl.multiple_of(at, width), width)
        key_rows[:, span] = source[local : 2 * local, :]
        for h in range(heads):
            query_cols[h, span, :] = turn_over(source[h * HEAD_DIM : (h + 1) * HEAD_DIM, :])
            value_cols[h, span, :] = turn_over(
                source[2 * local + h * HEAD_DIM : 2 * local + (h + 1) * HEAD_DIM, :]
            )
    for s, grad in enumerate(grads):
        span = pl.ds(pl.multiple_of((place[0] ^ s) * block, block), block)
        grad_rows[:, span] = grad[...]
        for h in range(heads):
            grad_cols[h, span, :] = turn_over(grad[h * HEAD_DIM : (h + 1) * HEAD_DIM, :])
    dk[...] = jnp.zeros_like(dk)
    dv[...] = jnp.zeros_like(dv)

    @pl.loop(0, 4)
    def _(quarter):
        span = pl.ds(pl.multiple_of(quarter * block, block), block)
        start = pl.multiple_of(windows[quarter], 128)
        count = windows[4 + quarter]

        def work(blocks):
            window = pl.ds(start, blocks * block)
            for h in range(heads):
                part = slice(h * HEAD_DIM, (h + 1) * HEAD_DIM)
                scores = dot(
                    keys[h, window, :], queries[h * KEY_ROWS : (h + 1) * KEY_ROWS, span]
                )
                probs = jnp.exp(scores - log_norm[h : h + 1, span])
                grad_probs = dot(value_cols[h, window, :], grad_rows[part, span])
                inner = jnp.sum(probs * grad_probs, axis=0, keepdims=True)
                grad_scores = (probs * (grad_probs - inner)).astype(BF16)
                dv[h, window, :] += dot(probs.astype(BF16), grad_cols[h, span, :])
                dk[h, window, :] += dot(grad_scores, query_cols[h, span, :])
                dq[part, span] = dot(key_rows[part, window], grad_scores)

        for blocks in range(1, 5):
            pl.when(count == blocks)(partial(work, blocks))

    cs = cosine[...]
    sn = sine[...]

    def turn_back(rows, base):
        a = rows[:HALF]
        b = rows[HALF:]
        grad_proj[base : base + HALF, :] = (a * cs + b * sn).astype(BF16)
        grad_proj[base + HALF : base + HEAD_DIM, :] = (b * cs - a * sn).astype(BF16)

    for h in range(heads):
        turn_back(dq[h * HEAD_DIM : (h + 1) * HEAD_DIM, :] * HEAD_DIM**-0.5, h * HEAD_DIM)
        turn_back(jnp.transpose(dk[h]), local + h * HEAD_DIM)
        base = 2 * local + h * HEAD_DIM
        grad_proj[base : base + HEAD_DIM, :] = jnp.transpose(dv[h]).astype(BF16)
    for s, partial_out in enumerate(partials):
        span = pl.ds(pl.multiple_of((place[0] ^ s) * block, block), block)
        partial_out[...] = dot(grad_proj[:, span], weight[...], TN).astype(BF16)


def middle_kernel(row, hid, *rest):
    attended, weights = rest[:4], rest[4:8]
    out_bias, gain, bias, second, middle = rest[8:]
    width = gain.shape[1]
    branch = out_bias[...]
    for a, w in zip(attended, weights):
        branch = branch + dot(a[...], w[...], TN)
    values = hid[:, row * width : (row + 1) * width].astype(F32) + branch
    middle[...] = values
    scaled, _ = normalize(values)
    second[...] = (scaled * gain[...] + bias[...]).astype(BF16)


def gelu_parts(h):
    size = jnp.abs(h)
    t = 1.0 / (1.0 + size * (0.3275911 * 0.5**0.5))
    density = jnp.exp(h * h * -0.5)
    poly = t * (
        0.254829592
        + t * (-0.284496736 + t * (1.421413741 + t * (-1.453152027 + t * 1.061405429)))
    )
    tail = 0.5 * poly * density
    below = jnp.where(h < 0, tail, 1.0 - tail)
    return below, density * 0.3989422804014327


def feed_kernel(second_a, second_b, cot_a, cot_b, w_in, b_in, w_out, *outs):
    out_a, out_b, grad_a, grad_b, act, grad_pre = outs
    block = second_a.shape[0]
    units = w_in.shape[1]
    step = 256
    for k, (second, cot, out, grad) in enumerate(
        ((second_a, cot_a, out_a, grad_a), (second_b, cot_b, out_b, grad_b))
    ):
        tokens = second[...]
        portion = cot[...]
        rows = slice(k * block, (k + 1) * block)
        for u in range(0, units, step):
            cols = slice(u, u + step)
            pre = dot(tokens, w_in[:, cols]) + b_in[:, cols]
            below, density = gelu_parts(pre)
            act[rows, cols] = (pre * below).astype(BF16)
            grad_act = dot(portion, w_out[cols, :], NT)
            grad_pre[rows, cols] = (grad_act * (below + pre * density)).astype(BF16)
        out[...] = dot(act[rows, :], w_out[...]).astype(BF16)
        grad[...] = dot(grad_pre[rows, :], w_in[...], NT).astype(BF16)


def feed_weights_kernel(place, *refs):
    count = (len(refs) - 11) // 3
    seconds, cots = refs[:count], refs[count : 2 * count]
    acts, pres = refs[2 * count : 2 * count + count // 2], refs[2 * count + count // 2 : 3 * count]
    outs, ins, bias, total_out, total_in = (
        refs[3 * count : 3 * count + 4],
        refs[3 * count + 4 : 3 * count + 8],
        refs[3 * count + 8],
        refs[3 * count + 9],
        refs[3 * count + 10],
    )
    block = seconds[0].shape[0]
    piece = outs[0].shape[0]
    added = None
    for k in range(count):
        rows = slice((k % 2) * block, (k % 2 + 1) * block)
        act = acts[k // 2][rows, :]
        pre = pres[k // 2][rows, :]
        down = dot(act, cots[k][...], TN)
        up = dot(seconds[k][...], pre, TN)
        sums = jnp.sum(pre.astype(F32), axis=0, keepdims=True)
        added = sums if added is None else added + sums
        if k == 0:
            total_out[...] = down
            total_in[...] = up
        else:
            total_out[...] += down
            total_in[...] += up
    bias[...] = added
    for s in range(4):
        span = pl.ds(pl.multiple_of((place[2] ^ s) * piece, piece), piece)
        outs[s][...] = total_out[span, :].astype(BF16)
        ins[s][...] = total_in[span, :].astype(BF16)


def middle_back_kernel(own, core, chip, middle, cot, gain, *rest):
    weights, outs = rest[:4], rest[4:]
    grad_middle, grad_branch, heads, sums = outs[0], outs[1], outs[2:6], outs[6]
    grad_second = own[...].astype(F32) + core[...].astype(F32) + chip[...].astype(F32)
    scaled, inverse = normalize(middle[...])
    grad_out = cot[...].astype(F32)
    total = grad_out + normalize_back(grad_second, scaled, inverse, gain[...])
    low = total.astype(BF16)
    grad_middle[...] = total
    grad_branch[...] = low
    for w, out in zip(weights, heads):
        out[...] = dot(w[...], low, NT).astype(BF16)
    sums[0:1, :] = jnp.sum(grad_second * scaled, axis=0, keepdims=True)
    sums[1:2, :] = jnp.sum(grad_second, axis=0, keepdims=True)
    sums[2:3, :] = jnp.sum(grad_out, axis=0, keepdims=True)
    sums[3:4, :] = jnp.sum(low.astype(F32), axis=0, keepdims=True)
    sums[4:, :] = jnp.zeros((4, sums.shape[1]), F32)


def out_weight_kernel(rows, *refs):
    attended, grads, outs = refs[: 4 * rows], refs[4 * rows : 5 * rows], refs[5 * rows :]
    for s, out in enumerate(outs):
        total = dot(attended[s][...], grads[0][...])
        for r in range(1, rows):
            total = total + dot(attended[4 * r + s][...], grads[r][...])
        out[...] = total.astype(BF16)


def project_weights_kernel(rows, place, *refs):
    projs, tokens = refs[:rows], refs[rows : 5 * rows]
    own, core, chip = refs[5 * rows : 5 * rows + 3]
    outs = refs[5 * rows + 3 : 5 * rows + 7]
    bias, total, small = refs[5 * rows + 7 :]
    block = tokens[0].shape[0]
    added = None
    for r in range(rows):
        sums = jnp.sum(projs[r][...].astype(F32), axis=1, keepdims=True)
        added = sums if added is None else added + sums
        for s in range(4):
            span = pl.ds(pl.multiple_of((place[0] ^ s) * block, block), block)
            product = dot(projs[r][:, span], tokens[4 * r + s][...])
            if r + s == 0:
                total[...] = product
            else:
                total[...] += product
    bias[...] = added
    small[...] = own[...].astype(F32) + core[...].astype(F32) + chip[...].astype(F32)
    big_piece, small_piece = total.shape[0] // 4, small.shape[0] // 4
    for s, out in enumerate(outs):
        at = place[2] ^ s
        big_at = pl.multiple_of(at * big_piece, big_piece)
        small_at = pl.multiple_of(at * small_piece, small_piece)
        out[:big_piece, :] = total[pl.ds(big_at, big_piece), :].astype(BF16)
        out[big_piece:, :] = small[pl.ds(small_at, small_piece), :].astype(BF16)


def finish_kernel(place, *refs):
    slots, outs = refs[:-2], refs[-2:]
    for k, out in enumerate(outs):
        for s in range(4):
            slot = slots[4 * k + s]
            piece = slot.shape[0]
            out[pl.ds(pl.multiple_of((place[2] ^ s) * piece, piece), piece), :] = slot[
                ...
            ].astype(F32)


def finish_project_kernel(place, *refs):
    slots, (big, small, total) = refs[:4], refs[4:]
    big_piece, small_piece = total.shape[0] // 4, small.shape[0] // 4
    for s, slot in enumerate(slots):
        at = place[2] ^ s
        big_at = pl.multiple_of(at * big_piece, big_piece)
        small_at = pl.multiple_of(at * small_piece, small_piece)
        total[pl.ds(big_at, big_piece), :] = slot[:big_piece, :].astype(F32)
        small[pl.ds(small_at, small_piece), :] = slot[big_piece:, :].astype(F32)
    local = big.shape[2]
    for c in range(3):
        big[c] = jnp.transpose(total[c * local : (c + 1) * local, :])


def first_back_kernel(row, own, core, chip, hid, grad_middle, gain, grad_in, sums):
    width = gain.shape[1]
    grad_first = own[...].astype(F32) + core[...].astype(F32) + chip[...].astype(F32)
    scaled, inverse = normalize(hid[:, row * width : (row + 1) * width].astype(F32))
    grad_in[...] = grad_middle[...] + normalize_back(grad_first, scaled, inverse, gain[...])
    sums[0:1, :] = jnp.sum(grad_first * scaled, axis=0, keepdims=True)
    sums[1:2, :] = jnp.sum(grad_first, axis=0, keepdims=True)
    sums[2:, :] = jnp.zeros((6, width), F32)


def swap(values, axis, size, bit):
    return lax.ppermute(values, axis, [(i, i ^ bit) for i in range(size)])


def core_swap(values):
    return swap(values, "tp", 4, 1)


def chip_swap(values):
    return swap(values, "tp", 4, 2)


def gather(values):
    across = chip_swap(values)
    return [values, core_swap(values), across, core_swap(across)]


def exchange(parts):
    far_core = chip_swap(parts[3])
    far = chip_swap(parts[2])
    return [parts[0], core_swap(parts[1]), far, core_swap(far_core)]


def plus(a, b):
    return (a.astype(F32) + b.astype(F32)).astype(BF16)


def scatter(parts):
    beside = core_swap(parts[1])
    across = chip_swap(plus(parts[2], core_swap(parts[3])))
    return [parts[0], beside, across]


def sum_rows(slots, size):
    two = plus(slots[2], swap(slots[3], "dp", size, 1))
    one = plus(slots[0], swap(slots[1], "dp", size, 1))
    one = plus(one, swap(two, "dp", size, 2))
    bit = 4
    while bit < size:
        one = plus(one, swap(one, "dp", size, bit))
        bit *= 2
    two = swap(one, "dp", size, 2)
    return [one, swap(one, "dp", size, 1), two, swap(two, "dp", size, 1)]


def sum_small(values, size, over_tp):
    if over_tp:
        values = values + core_swap(values)
        values = values + chip_swap(values)
    bit = 1
    while bit < size:
        values = values + swap(values, "dp", size, bit)
        bit *= 2
    return values


def on_device(
    size,
    hidden_in,
    segment_ids,
    cotangent,
    norm1_gain,
    norm1_bias,
    qkv_weight,
    qkv_bias,
    out_weight,
    out_bias,
    norm2_gain,
    norm2_bias,
    ffn_in_weight,
    ffn_in_bias,
    ffn_out_weight,
    ffn_out_bias,
):
    block, rows, width = hidden_in.shape
    length = segment_ids.shape[1]
    local = qkv_weight.shape[2]
    heads = local // HEAD_DIM
    units = ffn_in_weight.shape[1]
    me = lax.axis_index("tp").astype(jnp.int32)
    group = lax.axis_index("dp").astype(jnp.int32)
    place = jnp.stack([me, me // 2, group & 3, group])
    line = lambda v: v.astype(F32).reshape(1, -1)
    gain_one, bias_one = line(norm1_gain), line(norm1_bias)
    gain_two, bias_two = line(norm2_gain), line(norm2_bias)
    hid = hidden_in.reshape(block, rows * width)
    cots = [cotangent[:, r, :] for r in range(rows)]

    firsts = run(
        partial(first_norm_kernel, rows, width),
        "first_norm",
        [],
        [hid, gain_one, bias_one],
        [shape((block, width))] * rows,
    )
    first_slots = [gather(v) for v in firsts]
    out_slots = gather(out_weight)
    cot_slots = [gather(v) for v in cots]

    proj_weight = jnp.transpose(qkv_weight, (0, 2, 1)).reshape(3 * local, width)
    proj_bias = qkv_bias.astype(F32).reshape(3 * local, 1)
    ids = jnp.arange(16, dtype=jnp.int32)
    same = segment_ids[:, None, :] == ids[None, :, None]
    mine = same.astype(BF16)
    others = jnp.where(same | (ids >= 8)[None, :, None], 0.0, APART).astype(BF16)
    before = jnp.sum(
        (segment_ids[:, None, :] < ids[None, :8, None]).astype(jnp.int32), axis=-1
    )
    begins = jnp.sum(jnp.where(same[:, :8], before[:, :, None], 0), axis=1)
    where_in = (jnp.arange(length, dtype=jnp.int32)[None] - begins).astype(F32)
    rates = jnp.power(10000.0, -2.0 * jnp.arange(HALF, dtype=F32) / HEAD_DIM)
    angles = where_in[:, None, :] * rates[None, :, None]
    cosine, sine = jnp.cos(angles), jnp.sin(angles)
    opening = segment_ids[:, ::block]
    closing = segment_ids[:, block - 1 :: block]
    least = jnp.sum(
        (segment_ids[:, None, :] < opening[:, :, None]).astype(jnp.int32), axis=-1
    )
    past = jnp.sum(
        (segment_ids[:, None, :] <= closing[:, :, None]).astype(jnp.int32), axis=-1
    )
    start = least // 128 * 128
    count = (past - start + block - 1) // block
    start = jnp.minimum(start, length - count * block)
    windows = jnp.concatenate([start, count], axis=1)

    halves, attended, logs = [], [], []
    for r in range(rows):
        slots = first_slots[r]
        pair = []
        for far in range(2):
            pair += run(
                partial(project_kernel, far),
                "project",
                [place],
                [slots[2 * far], slots[2 * far + 1], proj_weight, proj_bias, cosine[r], sine[r]],
                [shape((3 * local, 2 * block))],
                flops=2 * 2 * block * width * 3 * local,
            )
        halves.append(pair)
        *outs, log_norm = run(
            attend_kernel,
            "attend",
            [place, windows[r]],
            [*pair, mine[r], others[r]],
            [shape((local, block))] * 4 + [shape((8, length), F32)],
            [
                pltpu.VMEM((heads * KEY_ROWS, length), BF16),
                pltpu.VMEM((heads, length, KEY_ROWS), BF16),
                pltpu.VMEM((local, length), BF16),
                pltpu.VMEM((local, length), BF16),
            ],
            flops=4 * 4 * local * length * length,
        )
        attended.append(exchange(outs))
        logs.append(log_norm)

    seconds, middles, second_slots = [], [], []
    for r in range(rows):
        second, middle = run(
            partial(middle_kernel, r),
            "middle",
            [],
            [hid, *attended[r], *out_slots, line(out_bias), gain_two, bias_two],
            [shape((block, width)), shape((block, width), F32)],
            flops=2 * block * width * width,
        )
        seconds.append(second)
        middles.append(middle)
        second_slots.append(gather(second))

    feeds, feed_grads, acts, pres = [], [], [], []
    for r in range(rows):
        outs_r, grads_r = [], []
        for far in range(2):
            s = slice(2 * far, 2 * far + 2)
            out_a, out_b, grad_a, grad_b, act, pre = run(
                feed_kernel,
                "feed",
                [],
                [
                    *second_slots[r][s],
                    *cot_slots[r][s],
                    ffn_in_weight,
                    line(ffn_in_bias),
                    ffn_out_weight,
                ],
                [shape((block, width))] * 4 + [shape((2 * block, units))] * 2,
                flops=8 * 2 * block * width * units,
            )
            outs_r += [out_a, out_b]
            grads_r += [grad_a, grad_b]
            acts.append(act)
            pres.append(pre)
        feed_grads.append(scatter(grads_r))
        feeds.append(outs_r)

    grad_middles, grad_branches, head_grads, norm_sums = [], [], [], []
    for r in range(rows):
        grad_middle, grad_branch, *parts, sums = run(
            middle_back_kernel,
            "middle_back",
            [],
            [*feed_grads[r], middles[r], cots[r], gain_two, *out_slots],
            [shape((block, width), F32), shape((block, width))]
            + [shape((local, block))] * 4
            + [shape((8, width), F32)],
            flops=2 * block * width * width,
        )
        grad_middles.append(grad_middle)
        grad_branches.append(grad_branch)
        head_grads.append(exchange(parts))
        norm_sums.append(sums)

    *slots, in_bias_sum = run(
        feed_weights_kernel,
        "feed_weights",
        [place],
        [*sum(second_slots, []), *sum(cot_slots, []), *acts, *pres],
        [shape((units // 4, width))] * 4
        + [shape((width // 4, units))] * 4
        + [shape((1, units), F32)],
        [pltpu.VMEM((units, width), F32), pltpu.VMEM((width, units), F32)],
        flops=2 * 8 * rows * block * width * units,
    )
    down_slots = sum_rows(slots[:4], size)
    up_slots = sum_rows(slots[4:], size)
    grad_down_weight, grad_in_weight = run(
        finish_kernel,
        "finish",
        [place],
        [*down_slots, *up_slots],
        [shape((units, width), F32), shape((width, units), F32)],
    )

    blocks_out = []
    for r in range(rows):
        own, beside, across = scatter(feeds[r])
        total = own.astype(F32) + beside.astype(F32) + across.astype(F32)
        blocks_out.append((middles[r] + (total + line(ffn_out_bias))).astype(BF16))
    block_out = jnp.stack(blocks_out, axis=1)

    projs, first_grads = [], []
    for r in range(rows):
        grad_proj, *parts = run(
            attend_back_kernel,
            "attend_back",
            [place, windows[r]],
            [
                *halves[r],
                mine[r],
                others[r],
                logs[r],
                cosine[r],
                sine[r],
                proj_weight,
                *head_grads[r],
            ],
            [shape((3 * local, length))] + [shape((block, width))] * 4,
            [
                pltpu.VMEM((heads * KEY_ROWS, length), BF16),
                pltpu.VMEM((heads, length, KEY_ROWS), BF16),
                pltpu.VMEM((local, length), BF16),
                pltpu.VMEM((heads, length, HEAD_DIM), BF16),
                pltpu.VMEM((heads, length, HEAD_DIM), BF16),
                pltpu.VMEM((local, length), BF16),
                pltpu.VMEM((heads, length, HEAD_DIM), BF16),
                pltpu.VMEM((heads, length, HEAD_DIM), F32),
                pltpu.VMEM((heads, length, HEAD_DIM), F32),
                pltpu.VMEM((local, length), F32),
            ],
            flops=10 * 4 * local * length * length,
        )
        projs.append(grad_proj)
        first_grads.append(scatter(parts))

    out_parts = run(
        partial(out_weight_kernel, rows),
        "out_weight",
        [],
        [*sum(attended, []), *grad_branches],
        [shape((local, width))] * 4,
        flops=2 * rows * block * width * width,
    )
    *slots, proj_bias_sum = run(
        partial(project_weights_kernel, rows),
        "project_weights",
        [place],
        [*projs, *sum(first_slots, []), *scatter(list(out_parts))],
        [shape((local, width))] * 4 + [shape((3 * local, 1), F32)],
        [pltpu.VMEM((3 * local, width), F32), pltpu.VMEM((local, width), F32)],
        flops=2 * rows * length * width * 3 * local,
    )
    slots = sum_rows(slots, size)
    grad_qkv_weight, grad_out_weight = run(
        finish_project_kernel,
        "finish_project",
        [place],
        slots,
        [shape((3, width, local), F32), shape((local, width), F32)],
        [pltpu.VMEM((3 * local, width), F32)],
    )

    grads_in, first_sums = [], []
    for r in range(rows):
        grad_in, sums = run(
            partial(first_back_kernel, r),
            "first_back",
            [],
            [*first_grads[r], hid, grad_middles[r], gain_one],
            [shape((block, width), F32), shape((8, width), F32)],
        )
        grads_in.append(grad_in)
        first_sums.append(sums)
    input_grad = jnp.stack(grads_in, axis=1)

    second_total = sum_small(sum(norm_sums), size, True)
    first_total = sum_small(sum(first_sums), size, True)
    in_bias_total = sum_small(in_bias_sum, size, False)
    proj_bias_total = sum_small(proj_bias_sum.reshape(3, local), size, False)
    return (
        block_out,
        input_grad,
        first_total[0],
        first_total[1],
        grad_qkv_weight,
        proj_bias_total,
        grad_out_weight,
        second_total[3],
        second_total[0],
        second_total[1],
        grad_in_weight,
        in_bias_total.reshape(units),
        grad_down_weight,
        second_total[2],
    )


def solution(mesh):
    sharded = P("tp", "dp", None)
    return jax.shard_map(
        partial(on_device, mesh.shape["dp"]),
        mesh=mesh,
        in_specs=(
            sharded,
            P("dp", None),
            sharded,
            P(),
            P(),
            P(None, None, "tp"),
            P(None, "tp"),
            P("tp", None),
            P(),
            P(),
            P(),
            P(None, "tp"),
            P("tp"),
            P("tp", None),
            P(),
        ),
        out_specs=(
            sharded,
            sharded,
            P(),
            P(),
            P(None, None, "tp"),
            P(None, "tp"),
            P("tp", None),
            P(),
            P(),
            P(),
            P(None, "tp"),
            P("tp"),
            P("tp", None),
            P(),
        ),
        check_vma=False,
    )
```

```python
from functools import partial

import jax
import jax.numpy as jnp
import numpy as np
from jax import lax
from jax.experimental import pallas as pl
from jax.experimental.pallas import tpu as pltpu
from jax.sharding import PartitionSpec as P

HEAD_DIM = 64
HALF = HEAD_DIM // 2
KEY_ROWS = 128
EPSILON = 1e-05
APART = -1e30
F32 = jnp.float32
BF16 = jnp.bfloat16

NN = (((1,), (0,)), ((), ()))
NT = (((1,), (1,)), ((), ()))
TN = (((0,), (0,)), ((), ()))


def dot(a, b, dims=NN):
    return lax.dot_general(a, b, dims, preferred_element_type=F32)


def shape(dims, dtype=BF16):
    return jax.ShapeDtypeStruct(dims, dtype)


class Line:
    def __init__(self):
        self.tile = None

    def run(self, body, name, scalars, arrays, outs, scratch=(), vmem=8):
        before = [] if self.tile is None else [self.tile]
        count, extra, made = len(scalars) + len(arrays), len(before), len(outs)

        def whole(*refs):
            tile = refs[count + extra + made]
            tile[...] = jnp.zeros_like(tile)
            body(
                *refs[:count],
                *refs[count + extra : count + extra + made],
                *refs[count + extra + made + 1 :],
            )

        outs = (*outs, shape((8, 128), F32))
        vector = pl.BlockSpec(memory_space=pltpu.VMEM)
        *results, self.tile = pl.pallas_call(
            whole,
            out_shape=outs,
            in_specs=[pl.BlockSpec(memory_space=pltpu.SMEM)] * len(scalars)
            + [vector] * (len(arrays) + extra),
            out_specs=(vector,) * len(outs),
            scratch_shapes=list(scratch),
            compiler_params=pltpu.CompilerParams(vmem_limit_bytes=vmem * 1024 * 1024),
            cost_estimate=pl.CostEstimate(flops=1, bytes_accessed=1, transcendentals=0),
            name=name,
        )(*scalars, *arrays, *before)
        return results

    def keep(self, *values, halves=False):
        parts = 3 if halves else 1
        outs = []
        for v in values:
            outs.append(shape(v.shape, v.dtype))
            outs += [shape((v.shape[0] // 2, *v.shape[1:]), v.dtype)] * (parts - 1)

        def body(*refs):
            for k in range(len(values)):
                mine = refs[len(values) + parts * k : len(values) + parts * (k + 1)]
                value = refs[k][...]
                mine[0][...] = value
                if halves:
                    write(value, None, mine[1:])

        return self.run(body, "keep", [], values, outs)

    def merge(self, whole, halves):
        def body(one, two, three, out):
            total = one[...].astype(F32) + read((two, three)).astype(F32)
            out[...] = total.astype(out.dtype)

        return self.run(body, "merge", [], [whole, *halves], [shape(whole.shape)])[0]

    def add(self, *sums):
        arrays = [term[0] for terms in sums for term in terms]
        parts = [[term[1:] for term in terms] for terms in sums]
        outs = []
        for terms in sums:
            first = terms[0][0]
            outs.append(shape(first.shape[len(terms[0]) - 1 :], first.dtype))

        def body(*refs):
            at = 0
            for k, terms in enumerate(parts):
                total = None
                for index in terms:
                    value = refs[at][index[0]] if index else refs[at][...]
                    value = value.astype(F32)
                    total = value if total is None else total + value
                    at += 1
                out = refs[len(arrays) + k]
                out[...] = total.astype(out.dtype)

        return self.run(body, "add", [], arrays, outs)


def normalize(values):
    average = jnp.mean(values, axis=-1, keepdims=True)
    centered = values - average
    variance = jnp.mean(centered * centered, axis=-1, keepdims=True)
    inverse = lax.rsqrt(variance + EPSILON)
    return centered * inverse, inverse


def normalize_back(gradient, scaled, inverse, gain):
    grad_scaled = gradient * gain
    return inverse * (
        grad_scaled
        - jnp.mean(grad_scaled, axis=-1, keepdims=True)
        - scaled * jnp.mean(grad_scaled * scaled, axis=-1, keepdims=True)
    )


def read(slot):
    if len(slot) == 1:
        return slot[0][...]
    return jnp.concatenate([part[...] for part in slot], axis=0)


def write(values, whole, parts):
    if whole is not None:
        whole[...] = values
    size = values.shape[0] // len(parts)
    for k, part in enumerate(parts):
        part[...] = values[k * size : (k + 1) * size]


def nest(refs, sizes):
    out, at = [], 0
    for size in sizes:
        out.append(refs[at : at + size])
        at += size
    return out


def first_norm_kernel(rows, width, hid, *refs):
    lines, vectors, outs = refs[:7], refs[7], refs[8:]
    for k, ref in enumerate(lines):
        vectors[k : k + 1, :] = ref[...].astype(F32).reshape(1, width)
    vectors[7:8, :] = jnp.zeros((1, width), F32)
    for r in range(rows):
        values = hid[:, r * width : (r + 1) * width].astype(F32)
        scaled, _ = normalize(values)
        low = (scaled * vectors[0:1, :] + vectors[1:2, :]).astype(BF16)
        write(low, outs[3 * r], outs[3 * r + 1 : 3 * r + 3])


def table_kernel(segments, rates, *outs):
    rows, length = segments.shape
    ids = lax.broadcasted_iota(jnp.int32, (16, length), 0)
    spots = lax.broadcasted_iota(jnp.int32, (1, length), 1)
    for r in range(rows):
        mine, others, cosine, sine = outs[4 * r : 4 * r + 4]
        row = segments[r : r + 1, :]
        same = row == ids
        before = jnp.sum((row < ids).astype(F32), axis=1, keepdims=True)
        begins = jnp.sum(jnp.where(same, before, 0.0), axis=0, keepdims=True)
        mine[...] = same.astype(F32).astype(BF16)
        others[...] = jnp.where(same | (ids >= 8), 0.0, APART).astype(BF16)
        angles = rates[...] * (spots.astype(F32) - begins)
        cosine[...] = jnp.cos(angles)
        sine[...] = jnp.sin(angles)


def split_kernel(width, whole, *outs):
    for r in range(len(outs) // 3):
        write(whole[:, r * width : (r + 1) * width], outs[3 * r], outs[3 * r + 1 : 3 * r + 3])


def project_kernel(far, place, one, two_a, two_b, weight, bias, cosine, sine, out):
    block = one.shape[0]
    local = weight.shape[0] // 3
    half = place[1] ^ far
    for k, tokens in enumerate(((one,), (two_a, two_b))):
        spot = pl.multiple_of(((place[0] & 1) ^ k) * block, block)
        span = pl.ds(spot, block)
        table = pl.ds(pl.multiple_of(half * (2 * block) + spot, block), block)
        turned = dot(weight[...], read(tokens), NT) + bias[...]
        cs = cosine[:, table]
        sn = sine[:, table]
        for c in range(2):
            for base in range(c * local, (c + 1) * local, HEAD_DIM):
                a = turned[base : base + HALF]
                b = turned[base + HALF : base + HEAD_DIM]
                new_a = a * cs - b * sn
                new_b = b * cs + a * sn
                if c == 0:
                    new_a = new_a * HEAD_DIM**-0.5
                    new_b = new_b * HEAD_DIM**-0.5
                out[base : base + HALF, span] = new_a.astype(BF16)
                out[base + HALF : base + HEAD_DIM, span] = new_b.astype(BF16)
        out[2 * local :, span] = turned[2 * local :].astype(BF16)


def turn_over(values):
    return jnp.transpose(values.astype(F32)).astype(BF16)


def lay_out(place, near, far, mine, others, queries, keys):
    width = near.shape[1]
    local = near.shape[0] // 3
    heads = local // HEAD_DIM
    marks = mine.shape[0]
    for source, at in ((near, place[1] * width), (far, (1 - place[1]) * width)):
        at = pl.multiple_of(at, width)
        span = pl.ds(at, width)
        for h in range(heads):
            queries[h * KEY_ROWS : h * KEY_ROWS + HEAD_DIM, span] = source[
                h * HEAD_DIM : (h + 1) * HEAD_DIM, :
            ]
            column = jnp.concatenate(
                [
                    source[local + h * HEAD_DIM : local + (h + 1) * HEAD_DIM, :],
                    others[:, span],
                    jnp.zeros((KEY_ROWS - HEAD_DIM - marks, width), BF16),
                ],
                axis=0,
            )
            keys[h, span, :] = turn_over(column)
    for h in range(heads):
        queries[h * KEY_ROWS + HEAD_DIM : h * KEY_ROWS + HEAD_DIM + marks, :] = mine[...]
        queries[h * KEY_ROWS + HEAD_DIM + marks : (h + 1) * KEY_ROWS, :] = jnp.zeros(
            (KEY_ROWS - HEAD_DIM - marks, queries.shape[1]), BF16
        )


def attend_kernel(place, windows, near, far, mine, others, *rest):
    outs, (log_norm, queries, keys, values, attended) = rest[:3], rest[3:]
    width = near.shape[1]
    block = width // 2
    local = near.shape[0] // 3
    heads = local // HEAD_DIM
    lay_out(place, near, far, mine, others, queries, keys)
    for source, at in ((near, place[1] * width), (far, (1 - place[1]) * width)):
        values[:, pl.ds(pl.multiple_of(at, width), width)] = source[2 * local :, :]

    @pl.loop(0, 4)
    def _(quarter):
        span = pl.ds(pl.multiple_of(quarter * block, block), block)
        start = pl.multiple_of(windows[quarter], 128)
        count = windows[4 + quarter]

        def work(blocks):
            window = pl.ds(start, blocks * block)
            for h in range(heads):
                scores = dot(
                    keys[h, window, :], queries[h * KEY_ROWS : (h + 1) * KEY_ROWS, span]
                )
                peak = jnp.max(scores, axis=0, keepdims=True)
                weights = jnp.exp(scores - peak)
                total = jnp.sum(weights, axis=0, keepdims=True)
                out = dot(
                    values[h * HEAD_DIM : (h + 1) * HEAD_DIM, window], weights.astype(BF16)
                )
                attended[h * HEAD_DIM : (h + 1) * HEAD_DIM, span] = (
                    out * (1.0 / total)
                ).astype(BF16)
                log_norm[h : h + 1, span] = peak + jnp.log(total)

        for blocks in range(1, 5):
            pl.when(count == blocks)(partial(work, blocks))

    for s, out in enumerate((outs[0], outs[1], outs[2].at[0], outs[2].at[1])):
        out[...] = attended[:, pl.ds(pl.multiple_of((place[0] ^ s) * block, block), block)]


def attend_back_kernel(
    place, windows, near, far, mine, others, log_norm, cosine, sine, weight, *rest
):
    grads, outs, scratch = four(rest[:4]), rest[4:11], rest[11:]
    grad_proj, partials = outs[0], nest(outs[1:], (1, 2, 1, 2))
    queries, keys, key_rows, value_cols, query_cols, grad_rows, grad_cols, dk, dv, dq = scratch
    width = near.shape[1]
    block = width // 2
    local = near.shape[0] // 3
    heads = local // HEAD_DIM
    lay_out(place, near, far, mine, others, queries, keys)
    for source, at in ((near, place[1] * width), (far, (1 - place[1]) * width)):
        span = pl.ds(pl.multiple_of(at, width), width)
        key_rows[:, span] = source[local : 2 * local, :]
        for h in range(heads):
            query_cols[h, span, :] = turn_over(source[h * HEAD_DIM : (h + 1) * HEAD_DIM, :])
            value_cols[h, span, :] = turn_over(
                source[2 * local + h * HEAD_DIM : 2 * local + (h + 1) * HEAD_DIM, :]
            )
    for s, grad in enumerate(grads):
        span = pl.ds(pl.multiple_of((place[0] ^ s) * block, block), block)
        grad_rows[:, span] = grad[...]
        for h in range(heads):
            grad_cols[h, span, :] = turn_over(grad[h * HEAD_DIM : (h + 1) * HEAD_DIM, :])
    dk[...] = jnp.zeros_like(dk)
    dv[...] = jnp.zeros_like(dv)

    @pl.loop(0, 4)
    def _(quarter):
        span = pl.ds(pl.multiple_of(quarter * block, block), block)
        start = pl.multiple_of(windows[quarter], 128)
        count = windows[4 + quarter]

        def work(blocks):
            window = pl.ds(start, blocks * block)
            for h in range(heads):
                part = slice(h * HEAD_DIM, (h + 1) * HEAD_DIM)
                scores = dot(
                    keys[h, window, :], queries[h * KEY_ROWS : (h + 1) * KEY_ROWS, span]
                )
                probs = jnp.exp(scores - log_norm[h : h + 1, span])
                grad_probs = dot(value_cols[h, window, :], grad_rows[part, span])
                inner = jnp.sum(probs * grad_probs, axis=0, keepdims=True)
                grad_scores = (probs * (grad_probs - inner)).astype(BF16)
                dv[h, window, :] += dot(probs.astype(BF16), grad_cols[h, span, :])
                dk[h, window, :] += dot(grad_scores, query_cols[h, span, :])
                dq[part, span] = dot(key_rows[part, window], grad_scores)

        for blocks in range(1, 5):
            pl.when(count == blocks)(partial(work, blocks))

    cs = cosine[...]
    sn = sine[...]

    def turn_back(rows, base):
        a = rows[:HALF]
        b = rows[HALF:]
        grad_proj[base : base + HALF, :] = (a * cs + b * sn).astype(BF16)
        grad_proj[base + HALF : base + HEAD_DIM, :] = (b * cs - a * sn).astype(BF16)

    for h in range(heads):
        turn_back(dq[h * HEAD_DIM : (h + 1) * HEAD_DIM, :] * HEAD_DIM**-0.5, h * HEAD_DIM)
        turn_back(jnp.transpose(dk[h]), local + h * HEAD_DIM)
        base = 2 * local + h * HEAD_DIM
        grad_proj[base : base + HEAD_DIM, :] = jnp.transpose(dv[h]).astype(BF16)
    for s, partial_out in enumerate(partials):
        span = pl.ds(pl.multiple_of((place[0] ^ s) * block, block), block)
        write(dot(grad_proj[:, span], weight[...], TN).astype(BF16), None, partial_out)


def four(parts):
    return [parts[0], parts[1], parts[2].at[0], parts[3].at[1]]


def middle_kernel(row, hid, *rest):
    attended, weights = four(rest[:4]), rest[4:8]
    vectors, second, second_a, second_b, middle = rest[8:]
    width = vectors.shape[1]
    branch = vectors[2:3, :]
    for a, w in zip(attended, weights):
        branch = branch + dot(a[...], w[...], TN)
    values = hid[:, row * width : (row + 1) * width].astype(F32) + branch
    middle[...] = values
    scaled, _ = normalize(values)
    low = (scaled * vectors[3:4, :] + vectors[4:5, :]).astype(BF16)
    write(low, second, (second_a, second_b))


def gelu_parts(h):
    size = jnp.abs(h)
    t = 1.0 / (1.0 + size * (0.3275911 * 0.5**0.5))
    density = jnp.exp(h * h * -0.5)
    poly = t * (
        0.254829592
        + t * (-0.284496736 + t * (1.421413741 + t * (-1.453152027 + t * 1.061405429)))
    )
    tail = 0.5 * poly * density
    below = jnp.where(h < 0, tail, 1.0 - tail)
    return below, density * 0.3989422804014327


def feed_kernel(*refs):
    seconds, cots, rest = nest(refs[:3], (1, 2)), nest(refs[3:6], (1, 2)), refs[6:]
    w_in, vectors, w_out, act, grad_pre = rest[:5]
    outs, grads = nest(rest[5:8], (1, 2)), nest(rest[8:11], (1, 2))
    block = seconds[0][0].shape[0]
    units = w_in.shape[1]
    step = 256
    for k in range(2):
        tokens = read(seconds[k])
        portion = read(cots[k])
        rows = slice(k * block, (k + 1) * block)
        for u in range(0, units, step):
            cols = slice(u, u + step)
            pre = dot(tokens, w_in[:, cols]) + vectors[6:7, cols]
            below, density = gelu_parts(pre)
            act[rows, cols] = (pre * below).astype(BF16)
            grad_act = dot(portion, w_out[cols, :], NT)
            grad_pre[rows, cols] = (grad_act * (below + pre * density)).astype(BF16)
        write(dot(act[rows, :], w_out[...]).astype(BF16), None, outs[k])
        write(dot(grad_pre[rows, :], w_in[...], NT).astype(BF16), None, grads[k])


def feed_weights_kernel(rows, place, *refs):
    count = 4 * rows
    seconds = nest(refs, (1, 2) * (2 * rows))
    cots = nest(refs[6 * rows :], (1, 2) * (2 * rows))
    acts, pres, refs = refs[12 * rows : 14 * rows], refs[14 * rows : 16 * rows], refs[16 * rows :]
    down_0, down_2, down_13, up_0, up_1, up_23, bias, total_out, total_in = refs
    outs = (down_0, down_13.at[0], down_2, down_13.at[1])
    ins = (up_0, up_1, up_23.at[0], up_23.at[1])
    block = seconds[0][0].shape[0]
    piece = outs[0].shape[0]
    added = None
    for k in range(count):
        rows = slice((k % 2) * block, (k % 2 + 1) * block)
        act = acts[k // 2][rows, :]
        pre = pres[k // 2][rows, :]
        down = dot(act, read(cots[k]), TN)
        up = dot(read(seconds[k]), pre, TN)
        sums = jnp.sum(pre.astype(F32), axis=0, keepdims=True)
        added = sums if added is None else added + sums
        if k == 0:
            total_out[...] = down
            total_in[...] = up
        else:
            total_out[...] += down
            total_in[...] += up
    bias[...] = added
    for s in range(4):
        span = pl.ds(pl.multiple_of((place[2] ^ s) * piece, piece), piece)
        outs[s][...] = total_out[span, :].astype(BF16)
        ins[s][...] = total_in[span, :].astype(BF16)


def middle_back_kernel(own, core_a, core_b, chip, middle, cot, vectors, *rest):
    weights, outs = rest[:4], rest[4:]
    grad_middle, grad_branch, sums = outs[0], outs[1], outs[5]
    heads = (outs[2], outs[3], outs[4].at[0], outs[4].at[1])
    core = read((core_a, core_b))
    grad_second = own[...].astype(F32) + core.astype(F32) + chip[...].astype(F32)
    scaled, inverse = normalize(middle[...])
    grad_out = cot[...].astype(F32)
    total = grad_out + normalize_back(grad_second, scaled, inverse, vectors[3:4, :])
    low = total.astype(BF16)
    grad_middle[...] = total
    grad_branch[...] = low
    for w, out in zip(weights, heads):
        out[...] = dot(w[...], low, NT).astype(BF16)
    sums[0:1, :] = jnp.sum(grad_second * scaled, axis=0, keepdims=True)
    sums[1:2, :] = jnp.sum(grad_second, axis=0, keepdims=True)
    sums[2:3, :] = jnp.sum(grad_out, axis=0, keepdims=True)
    sums[3:4, :] = jnp.sum(low.astype(F32), axis=0, keepdims=True)
    sums[4:, :] = jnp.zeros((4, sums.shape[1]), F32)


def out_weight_kernel(rows, *refs):
    attended, grads, outs = refs[: 4 * rows], refs[4 * rows : 5 * rows], refs[5 * rows :]
    attended = sum([four(attended[4 * r : 4 * r + 4]) for r in range(rows)], [])
    for s, out in enumerate(outs):
        total = dot(attended[s][...], grads[0][...])
        for r in range(1, rows):
            total = total + dot(attended[4 * r + s][...], grads[r][...])
        out[...] = total.astype(BF16)


def project_weights_kernel(rows, place, *refs):
    projs, tokens = refs[:rows], nest(refs[rows : 7 * rows], (1, 2) * (2 * rows))
    own, core, chip = refs[7 * rows : 7 * rows + 3]
    outs = refs[7 * rows + 3 : 7 * rows + 9]
    bias, total = refs[7 * rows + 9 :]
    block = tokens[0][0].shape[0]
    added = None
    size = projs[0].shape[0]
    for r in range(rows):
        sums = jnp.sum(projs[r][...].astype(F32), axis=1, keepdims=True)
        added = sums if added is None else added + sums
        for s in range(4):
            span = pl.ds(pl.multiple_of((place[0] ^ s) * block, block), block)
            product = dot(projs[r][:, span], read(tokens[4 * r + s]))
            if r + s == 0:
                total[:size, :] = product
            else:
                total[:size, :] += product
    bias[...] = added
    total[size:, :] = own[...].astype(F32) + core[...].astype(F32) + chip[...].astype(F32)
    piece = outs[0].shape[0]
    for bank in range(2):
        kept, other, pair = outs[3 * bank : 3 * bank + 3]
        bit = 1 + bank
        for slot, out in ((0, kept), (3 - bit, other), (bit, pair.at[0]), (3, pair.at[1])):
            at = 4 * bank + (place[2] ^ slot)
            out[...] = total[pl.ds(pl.multiple_of(at * piece, piece), piece), :].astype(BF16)


def finish_kernel(place, *refs):
    slots, outs = refs[:-2], refs[-2:]
    for k, out in enumerate(outs):
        for s in range(4):
            slot = slots[4 * k + s]
            piece = slot.shape[0]
            out[pl.ds(pl.multiple_of((place[2] ^ s) * piece, piece), piece), :] = slot[
                ...
            ].astype(F32)


def finish_project_kernel(place, *refs):
    slots, (big, small, total) = refs[:8], refs[8:]
    piece = slots[0].shape[0]
    for bank in range(2):
        for s in range(4):
            at = 4 * bank + (place[2] ^ s)
            total[pl.ds(pl.multiple_of(at * piece, piece), piece), :] = slots[4 * bank + s][
                ...
            ].astype(F32)
    size = big.shape[0]
    big[...] = total[:size, :]
    small[...] = total[size:, :]


def first_back_kernel(row, own, core_a, core_b, chip, hid, grad_middle, vectors, grad_in, sums):
    width = vectors.shape[1]
    core = read((core_a, core_b))
    grad_first = own[...].astype(F32) + core.astype(F32) + chip[...].astype(F32)
    scaled, inverse = normalize(hid[:, row * width : (row + 1) * width].astype(F32))
    grad_in[...] = grad_middle[...] + normalize_back(grad_first, scaled, inverse, vectors[0:1, :])
    sums[0:1, :] = jnp.sum(grad_first * scaled, axis=0, keepdims=True)
    sums[1:2, :] = jnp.sum(grad_first, axis=0, keepdims=True)
    sums[2:, :] = jnp.zeros((6, width), F32)


def pair_kernel(rows, *refs):
    parts = nest(refs[: 3 * rows], (1, 2) * rows)
    out = refs[3 * rows]
    for r in range(rows):
        one, two = read(parts[2 * r]), read(parts[2 * r + 1])
        out[r] = (one.astype(F32) + two.astype(F32)).astype(BF16)


def block_out_kernel(rows, *refs):
    parts = nest(refs[: 3 * rows], (1, 2) * rows)
    middles, across = refs[3 * rows : 4 * rows], refs[4 * rows]
    vectors, outs = refs[4 * rows + 1], refs[4 * rows + 2 :]
    for r in range(rows):
        own, core = read(parts[2 * r]), read(parts[2 * r + 1])
        total = own.astype(F32) + core.astype(F32) + across[r].astype(F32)
        outs[r][...] = (middles[r][...] + (total + vectors[5:6, :])).astype(BF16)


def swap(values, axis, size, bit):
    return lax.ppermute(values, axis, [(i, i ^ bit) for i in range(size)])


def core_swap(values):
    return swap(values, "tp", 4, 1)


def chip_swap(values):
    return swap(values, "tp", 4, 2)


class Bank:
    def __init__(self, own, other, pair, size, bit):
        self.own, self.other, self.size, self.bit, self.far = own, other, size, bit, 0
        self.moved = swap(pair, "dp", size, bit)

    def terms(self):
        if self.far == 0:
            return [[(self.other,), (self.moved, 1)], [(self.own,), (self.moved, 0)]]
        return [[(self.own,), (self.moved,)]]

    def take(self, results):
        near = 3 - self.bit
        if self.far == 0:
            self.other, self.own = results
            self.moved = swap(self.other, "dp", self.size, near)
            self.far = 2
            return
        (self.own,) = results
        self.far *= 2
        if self.far < self.size:
            self.moved = swap(self.own, "dp", self.size, self.far)
            return
        slots = [self.own, None, None, None]
        slots[near] = swap(self.own, "dp", self.size, near)
        slots[self.bit] = swap(self.own, "dp", self.size, self.bit)
        slots[3] = swap(slots[near], "dp", self.size, self.bit)
        self.slots = slots

    @property
    def done(self):
        return self.far >= self.size


def advance(line, *banks):
    terms = [bank.terms() for bank in banks]
    results = line.add(*sum(terms, []))
    for bank, own in zip(banks, terms):
        bank.take(results[: len(own)])
        results = results[len(own) :]


def on_device(
    size,
    hidden_in,
    segment_ids,
    cotangent,
    norm1_gain,
    norm1_bias,
    qkv_weight,
    qkv_bias,
    out_weight,
    out_bias,
    norm2_gain,
    norm2_bias,
    ffn_in_weight,
    ffn_in_bias,
    ffn_out_weight,
    ffn_out_bias,
):
    block, rows, width = hidden_in.shape
    length = segment_ids.shape[1]
    local = qkv_weight.shape[2]
    heads = local // HEAD_DIM
    units = ffn_in_weight.shape[1]
    me = lax.axis_index("tp").astype(jnp.int32)
    group = lax.axis_index("dp").astype(jnp.int32)
    place = jnp.stack([me, me // 2, group & 3, group])
    line = Line()
    each = range(rows)
    full, half = shape((block, width)), shape((block // 2, width))
    both = lambda pair: [core_swap(v) for v in pair]
    hid = hidden_in.reshape(block, rows * width)
    vectors, *firsts = line.run(
        partial(first_norm_kernel, rows, width),
        "first_norm",
        [],
        [hid, norm1_gain, norm1_bias, out_bias, norm2_gain, norm2_bias, ffn_out_bias, ffn_in_bias],
        [shape((8, width), F32)] + [full, half, half] * rows,
    )
    firsts_beside = [both(firsts[3 * r + 1 : 3 * r + 3]) for r in each]
    firsts = firsts[::3]
    firsts_across = [chip_swap(v) for v in firsts]

    rates = np.power(10000.0, -2.0 * np.arange(HALF) / HEAD_DIM).astype(np.float32)
    tables = line.run(
        table_kernel,
        "tables",
        [],
        [segment_ids, jnp.asarray(rates.reshape(HALF, 1))],
        [
            shape((16, length)),
            shape((16, length)),
            shape((HALF, length), F32),
            shape((HALF, length), F32),
        ]
        * rows,
    )
    mine, others, cosine, sine = (tables[k::4] for k in range(4))
    opening = segment_ids[:, ::block]
    closing = segment_ids[:, block - 1 :: block]
    least = jnp.sum(
        (segment_ids[:, None, :] < opening[:, :, None]).astype(jnp.int32), axis=-1
    )
    past = jnp.sum(
        (segment_ids[:, None, :] <= closing[:, :, None]).astype(jnp.int32), axis=-1
    )
    start = least // 128 * 128
    count = (past - start + block - 1) // block
    start = jnp.minimum(start, length - count * block)
    windows = jnp.concatenate([start, count], axis=1)
    proj_weight = jnp.transpose(qkv_weight, (0, 2, 1)).reshape(3 * local, width)
    proj_bias = qkv_bias.astype(F32).reshape(3 * local, 1)

    cots = line.run(
        partial(split_kernel, width),
        "split",
        [],
        [cotangent.reshape(block, rows * width)],
        [full, half, half] * rows,
    )
    cot_slots = [[cots[3 * r], *both(cots[3 * r + 1 : 3 * r + 3])] for r in each]
    cots = cots[::3]

    def project(far, r, slots):
        return line.run(
            partial(project_kernel, far),
            "project",
            [place],
            [*slots, proj_weight, proj_bias, cosine[r], sine[r]],
            [shape((3 * local, 2 * block))],
        )[0]

    def attend(r):
        *outs, log_norm = line.run(
            attend_kernel,
            "attend",
            [place, windows[r]],
            [near[r], far[r], mine[r], others[r]],
            [shape((local, block))] * 2
            + [shape((2, local, block)), shape((8, length), F32)],
            [
                pltpu.VMEM((heads * KEY_ROWS, length), BF16),
                pltpu.VMEM((heads, length, KEY_ROWS), BF16),
                pltpu.VMEM((local, length), BF16),
                pltpu.VMEM((local, length), BF16),
            ],
            vmem=14,
        )
        logs.append(log_norm)
        return [outs[0], core_swap(outs[1]), chip_swap(outs[2])]

    def feed(r, s):
        act, pre, *parts = line.run(
            feed_kernel,
            "feed",
            [],
            [
                *second_slots[r][s : s + 3],
                *cot_slots[r][s : s + 3],
                ffn_in_weight,
                vectors,
                ffn_out_weight,
            ],
            [shape((2 * block, units))] * 2 + [full, half, half] * 2,
        )
        acts[2 * r + s // 3], pres[2 * r + s // 3] = act, pre
        return parts

    near = [project(0, r, [firsts[r], *firsts_beside[r]]) for r in each]
    logs, far, attended, first_slots, cots_across = [], [], [], [], []
    for r in each:
        arrived, *halves = line.keep(firsts_across[r], halves=True)
        first_slots.append([firsts[r], *firsts_beside[r], arrived, *both(halves)])
        if r == 0:
            (ready,) = line.keep(out_weight)
            out_across = chip_swap(ready)
            out_beside = core_swap(ready)
        far.append(project(1, r, first_slots[r][3:]))
        attended.append(attend(r))
        cots_across.append(chip_swap(line.keep(cots[r])[0]))

    middles, second_slots = [], []
    acts, pres, feeds, feed_grads = [None] * (2 * rows), [None] * (2 * rows), [], []
    for r in each:
        if r == 0:
            arrived, out_far = line.keep(attended[r][2], out_across)
            out_slots = [out_weight, out_beside, out_far, core_swap(out_far)]
        else:
            (arrived,) = line.keep(attended[r][2])
        attended[r][2:] = [arrived, core_swap(arrived)]
        second, *halves, middle = line.run(
            partial(middle_kernel, r),
            "middle",
            [],
            [hid, *attended[r], *out_slots, vectors],
            [full, half, half, shape((block, width), F32)],
        )
        middles.append(middle)
        second_slots.append([second, *both(halves), chip_swap(second)])
        feeds.append(feed(r, 0))
    for r in each:
        seen, seen_a, seen_b, cot, cot_a, cot_b = line.keep(
            second_slots[r][3], cots_across[r], halves=True
        )
        second_slots[r][3:] = [seen, *both((seen_a, seen_b))]
        cot_slots[r] += [cot, *both((cot_a, cot_b))]
        if r > 0:
            back = line.merge(feeds[r - 1][9], halfway)
            feed_grads.append([feeds[r - 1][3], *both(feeds[r - 1][4:6]), chip_swap(back)])
        feeds[r] += feed(r, 3)
        halfway = both(feeds[r][10:12])
    back = line.merge(feeds[-1][9], halfway)
    feed_grads.append([feeds[-1][3], *both(feeds[-1][4:6]), chip_swap(back)])

    down_0, down_2, down_13, up_0, up_1, up_23, in_bias_sum = line.run(
        partial(feed_weights_kernel, rows),
        "feed_weights",
        [place],
        [*sum(second_slots, []), *sum(cot_slots, []), *acts, *pres],
        [shape((units // 4, width))] * 2
        + [shape((2, units // 4, width))]
        + [shape((width // 4, units))] * 2
        + [shape((2, width // 4, units)), shape((1, units), F32)],
        [pltpu.VMEM((units, width), F32), pltpu.VMEM((width, units), F32)],
        vmem=14,
    )
    down = Bank(down_0, down_2, down_13, size, 1)
    up = Bank(up_0, up_1, up_23, size, 2)

    grad_middles, grad_branches, head_grads, norm_sums = [], [], [], []
    for r in each:
        grad_middle, grad_branch, *parts, sums = line.run(
            middle_back_kernel,
            "middle_back",
            [],
            [*feed_grads[r], middles[r], cots[r], vectors, *out_slots],
            [shape((block, width), F32), shape((block, width))]
            + [shape((local, block))] * 2
            + [shape((2, local, block)), shape((8, width), F32)],
        )
        grad_middles.append(grad_middle)
        grad_branches.append(grad_branch)
        head_grads.append([parts[0], core_swap(parts[1]), chip_swap(parts[2])])
        norm_sums.append(sums)

    out_parts = line.run(
        partial(out_weight_kernel, rows),
        "out_weight",
        [],
        [*sum(attended, []), *grad_branches],
        [shape((local, width))] * 4,
    )
    out_half = core_swap(out_parts[3])
    out_beside = core_swap(out_parts[1])

    def attend_back(r):
        grad_proj, *parts = line.run(
            attend_back_kernel,
            "attend_back",
            [place, windows[r]],
            [
                near[r],
                far[r],
                mine[r],
                others[r],
                logs[r],
                cosine[r],
                sine[r],
                proj_weight,
                *head_grads[r],
            ],
            [shape((3 * local, length))] + [full, half, half] * 2,
            [
                pltpu.VMEM((heads * KEY_ROWS, length), BF16),
                pltpu.VMEM((heads, length, KEY_ROWS), BF16),
                pltpu.VMEM((local, length), BF16),
                pltpu.VMEM((heads, length, HEAD_DIM), BF16),
                pltpu.VMEM((heads, length, HEAD_DIM), BF16),
                pltpu.VMEM((local, length), BF16),
                pltpu.VMEM((heads, length, HEAD_DIM), BF16),
                pltpu.VMEM((heads, length, HEAD_DIM), F32),
                pltpu.VMEM((heads, length, HEAD_DIM), F32),
                pltpu.VMEM((local, length), F32),
            ],
            vmem=20,
        )
        projs.append(grad_proj)
        return [parts[0], *both(parts[1:3])], parts[3], both(parts[4:6])

    projs, first_grads = [], []
    feeds_beside = [both(feeds[r][1:3]) for r in each]
    feeds_half = [both(feeds[r][7:9]) for r in each]
    for r in each:
        (arrived,) = line.keep(head_grads[r][2])
        head_grads[r][2:] = [arrived, core_swap(arrived)]
    (back,) = line.add([(out_parts[2],), (out_half,)])
    out_sums = [out_parts[0], out_beside, chip_swap(back)]
    kept, partly, halfway = attend_back(0)
    ready = line.run(
        partial(pair_kernel, rows),
        "pair",
        [],
        sum([[feeds[r][6], *feeds_half[r]] for r in each], []),
        [shape((rows, block, width))],
    )
    blocks_across = chip_swap(ready[0])
    for r in range(1, rows):
        advance(line, down, up)
        back = line.merge(partly, halfway)
        first_grads.append([*kept, chip_swap(back)])
        kept, partly, halfway = attend_back(r)
    back = line.merge(partly, halfway)
    first_grads.append([*kept, chip_swap(back)])
    *slots, proj_bias_sum = line.run(
        partial(project_weights_kernel, rows),
        "project_weights",
        [place],
        [*projs, *sum(first_slots, []), *out_sums],
        [shape((local // 2, width)), shape((local // 2, width)), shape((2, local // 2, width))]
        * 2
        + [shape((3 * local, 1), F32)],
        [pltpu.VMEM((4 * local, width), F32)],
        vmem=10,
    )
    one = Bank(*slots[:3], size, 1)
    two = Bank(*slots[3:], size, 2)
    advance(line, down, up)

    blocks_out = line.run(
        partial(block_out_kernel, rows),
        "block_out",
        [],
        [
            *sum([[feeds[r][0], *feeds_beside[r]] for r in each], []),
            *middles,
            blocks_across,
            vectors,
        ],
        [shape((block, width))] * rows,
    )
    block_out = jnp.stack(blocks_out, axis=1)

    grads_in, first_sums = [], []
    for r in each:
        grad_in, sums = line.run(
            partial(first_back_kernel, r),
            "first_back",
            [],
            [*first_grads[r], hid, grad_middles[r], vectors],
            [shape((block, width), F32), shape((8, width), F32)],
        )
        grads_in.append(grad_in)
        first_sums.append(sums)
        if r == 0:
            advance(line, one, two)
    input_grad = jnp.stack(grads_in, axis=1)

    whole = jnp.concatenate([sum(first_sums)[:2], sum(norm_sums)[:4]], axis=0)
    (whole,) = line.add([(whole,), (core_swap(whole),)])
    advance(line, one, two)
    (whole,) = line.add([(whole,), (chip_swap(whole),)])
    extra = [in_bias_sum.reshape(units), jnp.pad(proj_bias_sum.reshape(-1), (0, units - 3 * local))]
    small = jnp.concatenate([whole, jnp.stack(extra)], axis=0)
    (small,) = line.add([(small,), (swap(small, "dp", size, 1),)])
    while not down.done:
        advance(line, down, up)
    (small,) = line.add([(small,), (swap(small, "dp", size, 2),)])
    while not one.done:
        advance(line, one, two)
    bit = 4
    while bit < size:
        (small,) = line.add([(small,), (swap(small, "dp", size, bit),)])
        bit *= 2
    grad_down_weight, grad_in_weight = line.run(
        finish_kernel,
        "finish",
        [place],
        [*down.slots, *up.slots],
        [shape((units, width), F32), shape((width, units), F32)],
    )
    grad_qkv_weight, grad_out_weight = line.run(
        finish_project_kernel,
        "finish_project",
        [place],
        [*one.slots, *two.slots],
        [shape((3 * local, width), F32), shape((local, width), F32)],
        [pltpu.VMEM((4 * local, width), F32)],
    )
    grad_qkv_weight = jnp.transpose(grad_qkv_weight.reshape(3, local, width), (0, 2, 1))
    return (
        block_out,
        input_grad,
        small[0],
        small[1],
        grad_qkv_weight,
        small[7, : 3 * local].reshape(3, local),
        grad_out_weight,
        small[5],
        small[2],
        small[3],
        grad_in_weight,
        small[6],
        grad_down_weight,
        small[4],
    )


def solution(mesh):
    sharded = P("tp", "dp", None)
    return jax.shard_map(
        partial(on_device, mesh.shape["dp"]),
        mesh=mesh,
        in_specs=(
            sharded,
            P("dp", None),
            sharded,
            P(),
            P(),
            P(None, None, "tp"),
            P(None, "tp"),
            P("tp", None),
            P(),
            P(),
            P(),
            P(None, "tp"),
            P("tp"),
            P("tp", None),
            P(),
        ),
        out_specs=(
            sharded,
            sharded,
            P(),
            P(),
            P(None, None, "tp"),
            P(None, "tp"),
            P("tp", None),
            P(),
            P(),
            P(),
            P(None, "tp"),
            P("tp"),
            P("tp", None),
            P(),
        ),
        check_vma=False,
    )
```

```python
from functools import partial

import jax
import jax.numpy as jnp
import numpy as np
from jax import lax
from jax.experimental import pallas as pl
from jax.experimental.pallas import tpu as pltpu
from jax.sharding import PartitionSpec as P

HEAD_DIM = 64
HALF = HEAD_DIM // 2
KEY_ROWS = 128
EPSILON = 1e-05
APART = -1e30
F32 = jnp.float32
BF16 = jnp.bfloat16

NN = (((1,), (0,)), ((), ()))
NT = (((1,), (1,)), ((), ()))
TN = (((0,), (0,)), ((), ()))


def dot(a, b, dims=NN):
    return lax.dot_general(a, b, dims, preferred_element_type=F32)


def shape(dims, dtype=BF16):
    return jax.ShapeDtypeStruct(dims, dtype)


class Line:
    def __init__(self):
        self.tile = None

    def run(
        self, body, name, scalars, arrays, outs, scratch=(), vmem=8, inputs=None, numbers=(), places=None
    ):
        before = [] if self.tile is None else [self.tile]
        count, extra, made = len(scalars) + len(arrays), len(before), len(outs)
        made += len(numbers)

        def whole(*refs):
            tile = refs[count + extra + made]
            tile[...] = jnp.zeros_like(tile)
            body(
                *refs[:count],
                *refs[count + extra : count + extra + made],
                *refs[count + extra + made + 1 :],
            )

        vector = pl.BlockSpec(memory_space=pltpu.VMEM)
        scalar = pl.BlockSpec(memory_space=pltpu.SMEM)
        *results, self.tile = pl.pallas_call(
            whole,
            out_shape=(*numbers, *outs, shape((8, 128), F32)),
            in_specs=[scalar] * len(scalars)
            + (inputs or [vector] * len(arrays))
            + [vector] * extra,
            out_specs=(scalar,) * len(numbers)
            + (tuple(places) if places else (vector,) * len(outs))
            + (vector,),
            scratch_shapes=list(scratch),
            compiler_params=pltpu.CompilerParams(vmem_limit_bytes=vmem * 1024 * 1024),
            cost_estimate=pl.CostEstimate(flops=1, bytes_accessed=1, transcendentals=0),
            name=name,
        )(*scalars, *arrays, *before)
        return results

    def keep(self, *arrays):
        def body(*refs):
            for k in range(len(arrays)):
                refs[len(arrays) + k][...] = refs[k][...]

        return self.run(body, "keep", [], arrays, [shape(v.shape, v.dtype) for v in arrays])

    def split(self, near, pair):
        def body(near, pair, one, two):
            one[...] = pair[0]
            two[0] = near[...]
            two[1] = pair[1]

        made = [shape(near.shape), shape((2, *near.shape))]
        one, two = self.run(body, "split", [], [near, pair], made)
        return [one, core_swap(two)]

    def merge(self, one, two, cuts):
        def body(one, two, *outs):
            total = one[...].astype(F32) + two[...].astype(F32)
            size = total.shape[0] // cuts
            for k, out in enumerate(outs):
                out[...] = total[k * size : (k + 1) * size].astype(out.dtype)

        made = [shape((one.shape[0] // cuts, *one.shape[1:]))] * cuts
        return self.run(body, "merge", [], [one, two], made)

    def join(self, *arrays):
        def body(*refs):
            for k in range(len(arrays)):
                refs[len(arrays)][k] = refs[k][...]

        first = arrays[0]
        made = [shape((len(arrays), *first.shape), first.dtype)]
        return self.run(body, "join", [], arrays, made, vmem=8)[0]

    def add_rows(self, ones, twos):
        count = len(ones)

        def body(*refs):
            for r in range(count):
                total = refs[r][...].astype(F32) + refs[count + r][1].astype(F32)
                refs[2 * count][r] = total.astype(BF16)

        made = [shape((count, *ones[0].shape))]
        return self.run(body, "add_rows", [], [*ones, *twos], made)[0]

    def add_pair(self, one, two):
        def body(a, b, c, d, out):
            out[0] = (a[...].astype(F32) + b[...].astype(F32)).astype(out.dtype)
            out[1] = (c[...].astype(F32) + d[...].astype(F32)).astype(out.dtype)

        made = [shape((2, *one[0].shape), one[0].dtype)]
        return self.run(body, "add_pair", [], [*one, *two], made)[0]

    def add(self, *sums):
        arrays = [term[0] for terms in sums for term in terms]
        parts = [[term[1:] for term in terms] for terms in sums]
        outs = []
        for terms in sums:
            first = terms[0][0]
            outs.append(shape(first.shape[len(terms[0]) - 1 :], first.dtype))

        def body(*refs):
            at = 0
            for k, terms in enumerate(parts):
                total = None
                for index in terms:
                    value = refs[at][index[0]] if index else refs[at][...]
                    value = value.astype(F32)
                    total = value if total is None else total + value
                    at += 1
                out = refs[len(arrays) + k]
                out[...] = total.astype(out.dtype)

        return self.run(body, "add", [], arrays, outs)


def normalize(values):
    average = jnp.mean(values, axis=-1, keepdims=True)
    centered = values - average
    variance = jnp.mean(centered * centered, axis=-1, keepdims=True)
    inverse = lax.rsqrt(variance + EPSILON)
    return centered * inverse, inverse


def normalize_back(gradient, scaled, inverse, gain):
    grad_scaled = gradient * gain
    return inverse * (
        grad_scaled
        - jnp.mean(grad_scaled, axis=-1, keepdims=True)
        - scaled * jnp.mean(grad_scaled * scaled, axis=-1, keepdims=True)
    )


def where_am_i():
    me = lax.axis_index("tp")
    return me, me // 2, lax.axis_index("dp") & 3


def first_norm_kernel(rows, width, hid, *refs):
    lines, (w_in, w_out, vectors, first, alone, joined) = refs[:7], refs[7:13]
    lands, sems = refs[13:20], refs[20]
    copies = [
        pltpu.make_async_copy(line, land, sems.at[k])
        for k, (line, land) in enumerate(zip(lines, lands))
    ]
    sends = [
        pltpu.make_async_copy(w_in, joined.at[0], sems.at[7]),
        pltpu.make_async_copy(w_out, joined.at[1], sems.at[8]),
    ]
    for copy in copies + sends:
        copy.start()
    normed = []
    for r in range(rows):
        values = hid[:, r * width : (r + 1) * width].astype(F32)
        normed.append(normalize(values)[0])
    for copy in copies:
        copy.wait()
    for k, land in enumerate(lands):
        vectors[k : k + 1, :] = land[...].astype(F32).reshape(1, width)
    vectors[7:8, :] = jnp.zeros((1, width), F32)
    for r in range(rows):
        low = (normed[r] * vectors[0:1, :] + vectors[1:2, :]).astype(BF16)
        first[r] = low
        if r == 0:
            alone[...] = low
    for copy in sends:
        copy.wait()


def table_kernel(block, segments, rates, bias, windows, marks, waves, column):
    rows, length = segments.shape
    ids = lax.broadcasted_iota(jnp.int32, (16, length), 0)
    spots = lax.broadcasted_iota(jnp.int32, (1, length), 1)
    for r in range(rows):
        row = segments[r : r + 1, :]
        same = row == ids
        before = jnp.sum((row < ids).astype(F32), axis=1, keepdims=True)
        begins = jnp.sum(jnp.where(same, before, 0.0), axis=0, keepdims=True)
        ends = jnp.sum((row <= ids).astype(F32), axis=1, keepdims=True)
        closes = jnp.sum(jnp.where(same, ends, 0.0), axis=0, keepdims=True)
        marks[r, 0] = same.astype(F32).astype(BF16)
        marks[r, 1] = jnp.where(same | (ids >= 8), 0.0, APART).astype(BF16)
        angles = rates[...] * (spots.astype(F32) - begins)
        waves[r, 0] = jnp.cos(angles)
        waves[r, 1] = jnp.sin(angles)
        blocks = length // block
        for q in range(blocks):
            inside = slice(q * block, (q + 1) * block)
            least = jnp.min(begins[:, inside]).astype(jnp.int32)
            past = jnp.max(closes[:, inside]).astype(jnp.int32)
            start = (least // 128) * 128
            count = (past - start + block - 1) // block
            windows[2 * blocks * r + q] = jnp.minimum(start, length - count * block)
            windows[2 * blocks * r + blocks + q] = count
    local = bias.shape[1]
    tall = jnp.concatenate([bias[...].astype(F32), jnp.zeros((5, local), F32)], axis=0)
    tall = jnp.transpose(tall)
    for c in range(3):
        column[c * local : (c + 1) * local, :] = tall[:, c : c + 1]


def split_kernel(width, whole, *outs):
    for r, out in enumerate(outs):
        out[...] = whole[:, r * width : (r + 1) * width]


def project_kernel(far, picked, one, two, weight, bias, waves, out):
    block = two.shape[-2]
    local = weight.shape[0] // 3
    me, chip, _ = where_am_i()
    half = chip ^ far
    for at, r in enumerate(picked):
        for k, tokens in enumerate((one, two)):
            spot = pl.multiple_of(((me & 1) ^ k) * block, block)
            span = pl.ds(spot, block)
            table = pl.ds(pl.multiple_of(half * (2 * block) + spot, block), block)
            values = tokens[at] if len(tokens.shape) == 3 else tokens[...]
            turned = dot(weight[...], values, NT) + bias[...]
            cs = waves[r, 0, :, table]
            sn = waves[r, 1, :, table]
            for c in range(2):
                for base in range(c * local, (c + 1) * local, HEAD_DIM):
                    a = turned[base : base + HALF]
                    b = turned[base + HALF : base + HEAD_DIM]
                    new_a = a * cs - b * sn
                    new_b = b * cs + a * sn
                    if c == 0:
                        new_a = new_a * HEAD_DIM**-0.5
                        new_b = new_b * HEAD_DIM**-0.5
                    out[at, base : base + HALF, span] = new_a.astype(BF16)
                    out[at, base + HALF : base + HEAD_DIM, span] = new_b.astype(BF16)
            out[at, 2 * local :, span] = turned[2 * local :].astype(BF16)


def turn_over(values):
    return jnp.transpose(values.astype(F32)).astype(BF16)


def sides(r, near, far):
    chip = where_am_i()[1]
    width = near.shape[-1]
    return [
        (source, pl.ds(pl.multiple_of(at, width), width))
        for source, at in ((near.at[r], chip * width), (far.at[0], (1 - chip) * width))
    ]


def lay_out(r, picked, near, far, marked, queries, keys):
    mine = marked[r, 0]
    width = near.shape[-1]
    local = near.shape[1] // 3
    marks = mine.shape[0]
    for source, span in sides(r, near, far):
        for at, h in enumerate(picked):
            queries[at * KEY_ROWS : at * KEY_ROWS + HEAD_DIM, span] = source[
                h * HEAD_DIM : (h + 1) * HEAD_DIM, :
            ]
            column = jnp.concatenate(
                [
                    source[local + h * HEAD_DIM : local + (h + 1) * HEAD_DIM, :],
                    marked[r, 1, :, span],
                    jnp.zeros((KEY_ROWS - HEAD_DIM - marks, width), BF16),
                ],
                axis=0,
            )
            keys[at, span, :] = turn_over(column)
    for at in range(len(picked)):
        base = at * KEY_ROWS + HEAD_DIM
        queries[base : base + marks, :] = mine
        queries[base + marks : (at + 1) * KEY_ROWS, :] = jnp.zeros(
            (KEY_ROWS - HEAD_DIM - marks, queries.shape[1]), BF16
        )


def attend_kernel(r, windows, near, far, marked, *rest):
    outs, (log_norm, queries, keys, values, attended) = rest[:3], rest[3:]
    block = near.shape[-1] // 2
    local = near.shape[1] // 3
    heads = local // HEAD_DIM
    me = where_am_i()[0]
    lay_out(r, range(heads), near, far, marked, queries, keys)
    for source, span in sides(r, near, far):
        values[:, span] = source[2 * local :, :]

    @pl.loop(0, 4)
    def _(quarter):
        span = pl.ds(pl.multiple_of(quarter * block, block), block)
        start = pl.multiple_of(windows[8 * r + quarter], 128)
        count = windows[8 * r + 4 + quarter]

        def work(blocks):
            window = pl.ds(start, blocks * block)
            for h in range(heads):
                scores = dot(
                    keys[h, window, :], queries[h * KEY_ROWS : (h + 1) * KEY_ROWS, span]
                )
                peak = jnp.max(scores, axis=0, keepdims=True)
                weights = jnp.exp(scores - peak)
                total = jnp.sum(weights, axis=0, keepdims=True)
                out = dot(
                    values[h * HEAD_DIM : (h + 1) * HEAD_DIM, window], weights.astype(BF16)
                )
                attended[h * HEAD_DIM : (h + 1) * HEAD_DIM, span] = (
                    out * (1.0 / total)
                ).astype(BF16)
                log_norm[h : h + 1, span] = peak + jnp.log(total)

        for blocks in range(1, 5):
            pl.when(count == blocks)(partial(work, blocks))

    for s, out in enumerate((outs[0], outs[1], outs[2].at[0], outs[2].at[1])):
        out[...] = attended[:, pl.ds(pl.multiple_of((me ^ s) * block, block), block)]


def attend_back_kernel(r, picked, windows, near, far, marked, log_norm, waves, *rest):
    grads = (rest[0], rest[2].at[0], rest[1], rest[2].at[1])
    scratch, rest = rest[-10:], rest[3:-10]
    queries, keys, key_rows, value_cols, query_cols, grad_rows, grad_cols, dk, dv, dq = scratch
    block = near.shape[-1] // 2
    local = near.shape[1] // 3
    heads = local // HEAD_DIM
    me = where_am_i()[0]
    if len(rest) == 1:
        before, weight, grad_proj, partials = None, None, rest[0], ()
    else:
        before = rest[0] if rest[0].shape[0] < rest[1].shape[0] else None
        weight, grad_proj, own, across, *sent = rest[1:] if before is not None else rest
        if len(sent) == 1:
            sent = (sent[0].at[0], sent[0].at[1])
        partials = (own, sent[0], across, sent[1])
    stride = grad_proj.shape[0] // 3
    first = picked[0] if weight is None else 0
    lay_out(r, picked, near, far, marked, queries, keys)
    for source, span in sides(r, near, far):
        for at, h in enumerate(picked):
            part = slice(at * HEAD_DIM, (at + 1) * HEAD_DIM)
            key_rows[part, span] = source[local + h * HEAD_DIM : local + (h + 1) * HEAD_DIM, :]
            query_cols[at, span, :] = turn_over(source[h * HEAD_DIM : (h + 1) * HEAD_DIM, :])
            value_cols[at, span, :] = turn_over(
                source[2 * local + h * HEAD_DIM : 2 * local + (h + 1) * HEAD_DIM, :]
            )
    for s, grad in enumerate(grads):
        span = pl.ds(pl.multiple_of((me ^ s) * block, block), block)
        for at, h in enumerate(picked):
            rows = grad[h * HEAD_DIM : (h + 1) * HEAD_DIM, :]
            grad_rows[at * HEAD_DIM : (at + 1) * HEAD_DIM, span] = rows
            grad_cols[at, span, :] = turn_over(rows)
    dk[...] = jnp.zeros_like(dk)
    dv[...] = jnp.zeros_like(dv)

    @pl.loop(0, 4)
    def _(quarter):
        span = pl.ds(pl.multiple_of(quarter * block, block), block)
        start = pl.multiple_of(windows[8 * r + quarter], 128)
        count = windows[8 * r + 4 + quarter]

        def work(blocks):
            window = pl.ds(start, blocks * block)
            for at, h in enumerate(picked):
                part = slice(at * HEAD_DIM, (at + 1) * HEAD_DIM)
                scores = dot(
                    keys[at, window, :], queries[at * KEY_ROWS : (at + 1) * KEY_ROWS, span]
                )
                probs = jnp.exp(scores - log_norm[h : h + 1, span])
                grad_probs = dot(value_cols[at, window, :], grad_rows[part, span])
                inner = jnp.sum(probs * grad_probs, axis=0, keepdims=True)
                grad_scores = (probs * (grad_probs - inner)).astype(BF16)
                dv[at, window, :] += dot(probs.astype(BF16), grad_cols[at, span, :])
                dk[at, window, :] += dot(grad_scores, query_cols[at, span, :])
                dq[part, span] = dot(key_rows[part, window], grad_scores)

        for blocks in range(1, 5):
            pl.when(count == blocks)(partial(work, blocks))

    cs = waves[r, 0]
    sn = waves[r, 1]

    def turn_back(rows, base):
        a = rows[:HALF]
        b = rows[HALF:]
        grad_proj[base : base + HALF, :] = (a * cs + b * sn).astype(BF16)
        grad_proj[base + HALF : base + HEAD_DIM, :] = (b * cs - a * sn).astype(BF16)

    for at, h in enumerate(picked):
        base = (h - first) * HEAD_DIM
        turn_back(dq[at * HEAD_DIM : (at + 1) * HEAD_DIM, :] * HEAD_DIM**-0.5, base)
        turn_back(jnp.transpose(dk[at]), stride + base)
        base += 2 * stride
        grad_proj[base : base + HEAD_DIM, :] = jnp.transpose(dv[at]).astype(BF16)
    if before is not None:
        had = before.shape[0] // 3
        for c in range(3):
            grad_proj[c * stride : c * stride + had, :] = before[c * had : (c + 1) * had, :]
    for s, partial_out in enumerate(partials):
        span = pl.ds(pl.multiple_of((me ^ s) * block, block), block)
        partial_out[...] = dot(grad_proj[:, span], weight[...], TN).astype(BF16)


def four(parts):
    return (parts[0], parts[2].at[0], parts[1], parts[2].at[1])


def middle_kernel(row, hid, *rest):
    attended, weights = four(rest[:3]), rest[3:7]
    vectors, cot, middle, second, pair = rest[7:12]
    width = vectors.shape[1]
    branch = vectors[2:3, :]
    for a, w in zip(attended, weights):
        branch = branch + dot(a[...], w[...], TN)
    values = hid[:, row * width : (row + 1) * width].astype(F32) + branch
    middle[...] = values
    scaled, _ = normalize(values)
    low = (scaled * vectors[3:4, :] + vectors[4:5, :]).astype(BF16)
    second[...] = low
    pair[0] = low
    pair[1] = cot[...]


def gelu_parts(h):
    size = jnp.abs(h)
    t = 1.0 / (1.0 + size * (0.3275911 * 0.5**0.5))
    density = jnp.exp(h * h * -0.5)
    poly = t * (
        0.254829592
        + t * (-0.284496736 + t * (1.421413741 + t * (-1.453152027 + t * 1.061405429)))
    )
    tail = 0.5 * poly * density
    below = jnp.where(h < 0, tail, 1.0 - tail)
    return below, density * 0.3989422804014327


def feed_kernel(second, cot, w_in, w_out, vectors, passed, passed_vectors, act, grad_pre, *outs):
    if cot is None:
        second, cot = second.at[0], second.at[1]
    units = w_in.shape[1]
    width = w_in.shape[0]
    step = 256
    tokens = second[...]
    portion = cot[...]
    for side, lines in enumerate((vectors, passed_vectors)):
        for u in range(0, units, step):
            cols = slice(u, u + step)
            spot = slice(side * units + u, side * units + u + step)
            into = passed[:width, cols] if side else w_in[:, cols]
            down = passed[width + u : width + u + step, :] if side else w_out[cols, :]
            pre = dot(tokens, into) + lines[6:7, cols]
            below, density = gelu_parts(pre)
            act[:, spot] = (pre * below).astype(BF16)
            grad_act = dot(portion, down, NT)
            grad_pre[:, spot] = (grad_act * (below + pre * density)).astype(BF16)
    out = dot(act[:, :units], w_out[...]) + dot(act[:, units:], passed[width:, :])
    grad = dot(grad_pre[:, :units], w_in[...], NT) + dot(
        grad_pre[:, units:], passed[:width, :], NT
    )
    half = out.shape[0] // 2
    outs[0][...] = out.astype(BF16)
    low = grad.astype(BF16)
    if len(outs) == 2:
        outs[1][...] = low
    else:
        outs[1][...] = low[:half]
        outs[2][...] = low[half:]


def feed_weights_kernel(count, *refs):
    near = count // 2
    seconds, cots, pairs = refs[:near], refs[near:count], refs[count : count + near]
    seconds = [*seconds, *(pair.at[0] for pair in pairs)]
    cots = [*cots, *(pair.at[1] for pair in pairs)]
    refs = refs[count + near :]
    acts, pres = refs[:count], refs[count : 2 * count]
    own, passed, own_bias, passed_bias, down, up = refs[2 * count :]
    units = own.shape[1]
    for k in range(count):
        pre = pres[k][...]
        part_down = dot(acts[k][...], cots[k][...], TN)
        part_up = dot(seconds[k][...], pre, TN)
        sums = jnp.sum(pre.astype(F32), axis=0, keepdims=True)
        if k == 0:
            down[...] = part_down
            up[...] = part_up
            added = sums
        else:
            down[...] += part_down
            up[...] += part_up
            added += sums
    own_bias[...] = added[:, :units]
    passed_bias[...] = jnp.broadcast_to(added[:, units:], passed_bias.shape)
    own[0] = down[:units, :].astype(BF16)
    own[1] = up[:, :units].astype(BF16)
    passed[0] = down[units:, :].astype(BF16)
    passed[1] = up[:, units:].astype(BF16)


def feed_slots_kernel(own, passed, own_bias, passed_bias, bias, *outs):
    piece = outs[0].shape[0] // 2
    spot = where_am_i()[2]
    bias[...] = own_bias[...] + passed_bias[0:1, :]
    for s, out in enumerate(outs):
        span = pl.ds(pl.multiple_of((spot ^ s) * piece, piece), piece)
        for bank in range(2):
            total = own[bank, span, :].astype(F32) + passed[bank, span, :].astype(F32)
            out[bank * piece : (bank + 1) * piece, :] = total.astype(BF16)


def middle_back_kernel(chips, own, *rest):
    chip, rest = rest[:chips], rest[chips:]
    middle, cot, vectors = rest[:3]
    weights, outs = rest[3:7], rest[7:]
    grad_middle, grad_branch, sums = outs[0], outs[1], outs[5]
    heads = (outs[2], outs[3], outs[4].at[0], outs[4].at[1])
    across = jnp.concatenate([part[...] for part in chip], axis=0) if chips > 1 else chip[0][...]
    grad_second = own[...].astype(F32) + across.astype(F32)
    scaled, inverse = normalize(middle[...])
    grad_out = cot[...].astype(F32)
    total = grad_out + normalize_back(grad_second, scaled, inverse, vectors[3:4, :])
    low = total.astype(BF16)
    grad_middle[...] = total
    grad_branch[...] = low
    for w, out in zip(weights, heads):
        out[...] = dot(w[...], low, NT).astype(BF16)
    sums[0:1, :] = jnp.sum(grad_second * scaled, axis=0, keepdims=True)
    sums[1:2, :] = jnp.sum(grad_second, axis=0, keepdims=True)
    sums[2:3, :] = jnp.sum(grad_out, axis=0, keepdims=True)
    sums[3:4, :] = jnp.sum(low.astype(F32), axis=0, keepdims=True)
    sums[4:, :] = jnp.zeros((4, sums.shape[1]), F32)


def out_weight_kernel(rows, *refs):
    attended, grads, outs = refs[: 3 * rows], refs[3 * rows : 4 * rows], refs[4 * rows :]
    attended = [four(attended[3 * r : 3 * r + 3]) for r in range(rows)]
    own, across, sent = outs
    for s, out in enumerate((own, sent.at[0], across, sent.at[1])):
        total = dot(attended[0][s][...], grads[0][...])
        for r in range(1, rows):
            total = total + dot(attended[r][s][...], grads[r][...])
        out[...] = total.astype(BF16)


def project_weights_kernel(rows, *refs):
    projs, near, far = refs[:rows], refs[rows : rows + 2], refs[rows + 2 : 3 * rows + 2]
    refs = refs[3 * rows + 2 :]
    own, swapped, chip = refs[:3]
    outs, (bias, total) = refs[3:7], refs[7:]
    block = near[0].shape[1]
    me, _, spot = where_am_i()
    size = projs[0].shape[0]
    local = size // 3
    ones = jnp.ones((8, projs[0].shape[1]), BF16)
    bias[...] = jnp.zeros_like(bias)
    for c in range(3):
        part = slice(c * local, (c + 1) * local)
        sums = dot(ones, projs[0][part, :], NT)
        for r in range(1, rows):
            sums += dot(ones, projs[r][part, :], NT)
        bias[:, 256 * c : 256 * c + local] = sums
    for r in range(rows):
        for s in range(4):
            span = pl.ds(pl.multiple_of((me ^ s) * block, block), block)
            tokens = near[s][r] if s < 2 else far[2 * r + s - 2][...]
            product = dot(projs[r][:, span], tokens)
            if r + s == 0:
                total[:size, :] = product
            else:
                total[:size, :] += product
    total[size:, :] = own[...].astype(F32) + swapped[0].astype(F32) + chip[...].astype(F32)
    piece = outs[0].shape[0]
    for s, out in enumerate(outs):
        at = pl.multiple_of((spot ^ s) * piece, piece)
        out[...] = total[pl.ds(at, piece), :].astype(BF16)


def finish_kernel(*refs):
    spot = where_am_i()[2]
    slots, outs = refs[:4], refs[4:]
    for s, slot in enumerate(slots):
        piece = slot.shape[0] // 2
        span = pl.ds(pl.multiple_of((spot ^ s) * piece, piece), piece)
        for k, out in enumerate(outs):
            out[span, :] = slot[k * piece : (k + 1) * piece, :].astype(F32)


def finish_project_kernel(*refs):
    spot = where_am_i()[2]
    slots, (big, small, total) = refs[:4], refs[4:]
    for s, slot in enumerate(slots):
        piece = slot.shape[0]
        at = pl.multiple_of((spot ^ s) * piece, piece)
        total[pl.ds(at, piece), :] = slot[...].astype(F32)
    size = big.shape[0]
    big[...] = total[:size, :]
    small[...] = total[size:, :]


def first_back_kernel(row, own, beside, chip, hid, grad_middle, vectors, grad_in, sums):
    width = vectors.shape[1]
    swapped = beside[0] if len(beside.shape) == 3 else beside[...]
    grad_first = own[...].astype(F32) + swapped.astype(F32) + chip[...].astype(F32)
    scaled, inverse = normalize(hid[:, row * width : (row + 1) * width].astype(F32))
    grad_in[...] = grad_middle[...] + normalize_back(grad_first, scaled, inverse, vectors[0:1, :])
    sums[0:1, :] = jnp.sum(grad_first * scaled, axis=0, keepdims=True)
    sums[1:2, :] = jnp.sum(grad_first, axis=0, keepdims=True)
    sums[2:, :] = jnp.zeros((6, width), F32)


def small_kernel(firsts, middles, out):
    rows = len(firsts)
    out[...] = jnp.zeros_like(out)
    out[0:2, :] = sum(ref[0:2, :] for ref in firsts)
    out[2:6, :] = sum(ref[0:4, :] for ref in middles)


def small_extra_kernel(one, two, in_bias, proj_bias, out):
    out[...] = one[...] + two[...]
    out[6:7, :] = in_bias[...]
    out[7:8, :] = proj_bias[0:1, :]


def finish_small_kernel(one, two, *outs):
    *lines, proj_bias, total = outs
    total[...] = one[...] + two[...]
    width = total.shape[1]
    for k, line in enumerate(lines):
        line[...] = total[k : k + 1, :].reshape(width)
    local = proj_bias.shape[1]
    for c in range(3):
        proj_bias[c : c + 1, :] = total[7:8, 256 * c : 256 * c + local]


def block_out_kernel(rows, *refs):
    owns, middles = refs[:rows], refs[rows : 2 * rows]
    across, vectors, outs = refs[2 * rows], refs[2 * rows + 1], refs[2 * rows + 2 :]
    for r in range(rows):
        total = owns[r][...].astype(F32) + across[r].astype(F32)
        outs[r][...] = (middles[r][...] + (total + vectors[5:6, :])).astype(BF16)


def swap(values, axis, size, bit):
    return lax.ppermute(values, axis, [(i, i ^ bit) for i in range(size)])


def core_swap(values):
    return swap(values, "tp", 4, 1)


def chip_swap(values):
    return swap(values, "tp", 4, 2)


class Bank:
    def __init__(self, line, slots, size):
        self.line, self.own, self.size = line, slots[0], size
        self.moved = [swap(slots[s], "dp", size, s) for s in range(1, 4)]
        self.bit = 2

    def advance(self):
        (self.own,) = self.line.add([(self.own,), *((v,) for v in self.moved)])
        self.bit *= 2
        if self.bit < self.size:
            self.moved = [swap(self.own, "dp", self.size, self.bit)]
            return
        self.slots = [self.own] + [swap(self.own, "dp", self.size, s) for s in range(1, 4)]

    @property
    def done(self):
        return self.bit >= self.size


def on_device(
    size,
    hidden_in,
    segment_ids,
    cotangent,
    norm1_gain,
    norm1_bias,
    qkv_weight,
    qkv_bias,
    out_weight,
    out_bias,
    norm2_gain,
    norm2_bias,
    ffn_in_weight,
    ffn_in_bias,
    ffn_out_weight,
    ffn_out_bias,
):
    block, rows, width = hidden_in.shape
    length = segment_ids.shape[1]
    local = qkv_weight.shape[2]
    heads = local // HEAD_DIM
    units = ffn_in_weight.shape[1]
    line = Line()
    each, last = range(rows), rows - 1
    full, half, both = shape((block, width)), shape((block // 2, width)), shape((rows, block, width))
    hid = hidden_in.reshape(block, rows * width)
    cots = cotangent.reshape(block, rows * width)
    vector, anywhere = pl.BlockSpec(memory_space=pltpu.VMEM), pl.BlockSpec(memory_space=pltpu.HBM)
    params = [norm1_gain, norm1_bias, out_bias, norm2_gain, norm2_bias, ffn_out_bias, ffn_in_bias]
    vectors, first, alone, joined = line.run(
        partial(first_norm_kernel, rows, width),
        "first_norm",
        [],
        [hid, *params, ffn_in_weight, ffn_out_weight],
        [shape((8, width), F32), both, full, shape((2, *ffn_in_weight.shape))],
        [pltpu.VMEM((width,), BF16)] * 7 + [pltpu.SemaphoreType.DMA((9,))],
        inputs=[vector] + [anywhere] * 9,
        places=[vector] * 3 + [anywhere],
    )
    first_across = [chip_swap(alone)]
    first_beside = core_swap(first)
    passed = core_swap(joined).reshape(2 * width, -1)
    passed_vectors = core_swap(vectors)

    rates = np.power(10000.0, -2.0 * np.arange(HALF) / HEAD_DIM).astype(np.float32)
    windows, marks, waves, proj_bias = line.run(
        partial(table_kernel, block),
        "tables",
        [],
        [segment_ids, jnp.asarray(rates.reshape(HALF, 1)), qkv_bias],
        [
            shape((rows, 2, 16, length)),
            shape((rows, 2, HALF, length), F32),
            shape((3 * local, 1), F32),
        ],
        numbers=[shape((rows * 2 * (length // block),), jnp.int32)],
    )
    proj_weight = jnp.transpose(qkv_weight, (0, 2, 1)).reshape(3 * local, width)

    def project(far, picked, one, two):
        return line.run(
            partial(project_kernel, far, picked),
            "project",
            [],
            [one, two, proj_weight, proj_bias, waves],
            [shape((len(picked), 3 * local, 2 * block))],
        )[0]

    def attend(r):
        *outs, log_norm = line.run(
            partial(attend_kernel, r),
            "attend",
            [windows],
            [near, far[r], marks],
            [shape((local, block))] * 2
            + [shape((2, local, block)), shape((8, length), F32)],
            [
                pltpu.VMEM((heads * KEY_ROWS, length), BF16),
                pltpu.VMEM((heads, length, KEY_ROWS), BF16),
                pltpu.VMEM((local, length), BF16),
                pltpu.VMEM((local, length), BF16),
            ],
            vmem=14,
        )
        logs.append(log_norm)
        return [outs[0], outs[1], chip_swap(outs[2])]

    def feed(*tokens):
        tokens = list(tokens)

        def body(*refs):
            feed_kernel(*(refs if len(tokens) == 2 else (refs[0], None, *refs[1:])))

        act, pre, *outs = line.run(
            body,
            "feed",
            [],
            tokens + [ffn_in_weight, ffn_out_weight, vectors, passed, passed_vectors],
            [shape((block, 2 * units))] * 2 + [full, full],
            vmem=12,
        )
        acts.append(act)
        pres.append(pre)
        return outs

    def pick(values, r):
        def body(values, out):
            out[...] = values[r]

        return line.run(body, "pick", [], [values], [shape(values.shape[1:])])[0]

    near = project(0, tuple(each), first, first_beside)
    cots = line.run(partial(split_kernel, width), "split", [], [cots], [full] * rows)
    far, far_slots = [], []
    logs, attended = [], []
    for r in each:
        (arrived,) = line.keep(first_across[r])
        far_slots += [arrived, core_swap(arrived)]
        if r < last:
            first_across.append(chip_swap(pick(first, r + 1)))
        if r == last:
            (ready,) = line.keep(out_weight)
            out_across = chip_swap(ready)
            out_beside = core_swap(ready)
        far.append(project(1, (r,), *far_slots[-2:]))
        attended.append(attend(r))

    middles, seconds, pairs = [], [], []
    acts, pres, feeds, feed_grads = [], [], [], []
    for r in each:
        if r == 0:
            (out_far,) = line.keep(out_across)
            out_slots = [out_weight, out_beside, out_far, core_swap(out_far)]
        one, two = line.split(attended[r][1], attended[r][2])
        attended[r][1:] = [one, two]
        middle, second, pair = line.run(
            partial(middle_kernel, r),
            "middle",
            [],
            [hid, *attended[r], *out_slots, vectors, cots[r]],
            [shape((block, width), F32), full, shape((2, block, width))],
        )
        middles.append(middle)
        seconds.append(second)
        pairs.append(chip_swap(pair))
        out, grad = feed(second, cots[r])
        feeds.append([out])
        feed_grads.append([grad])
    for r in each:
        out, grad = feed(pairs[r])
        feeds[r].append(out)
        feed_grads[r].append(chip_swap(grad))

    grad_middles, grad_branches, head_grads, norm_sums = [], [], [], []

    def middle_back(r):
        own, *across = feed_grads[r]
        grad_middle, grad_branch, *parts, sums = line.run(
            partial(middle_back_kernel, len(across)),
            "middle_back",
            [],
            [own, *across, middles[r], cots[r], vectors, *out_slots],
            [shape((block, width), F32), full]
            + [shape((local, block))] * 2
            + [shape((2, local, block)), shape((8, width), F32)],
        )
        grad_middles.append(grad_middle)
        grad_branches.append(grad_branch)
        head_grads.append([parts[0], parts[1], chip_swap(parts[2])])
        norm_sums.append(sums)

    for r in range(last):
        middle_back(r)
    own_sums, passed_sums, own_bias, passed_bias = line.run(
        partial(feed_weights_kernel, 2 * rows),
        "feed_weights",
        [],
        [*seconds, *cots, *pairs, *acts, *pres],
        [
            shape((2, units, width)),
            shape((2, units, width)),
            shape((1, units), F32),
            shape((8, units), F32),
        ],
        [pltpu.VMEM((2 * units, width), F32), pltpu.VMEM((width, 2 * units), F32)],
        vmem=22,
    )
    passed_sums = core_swap(passed_sums)
    passed_bias = core_swap(passed_bias)
    in_bias_sum, *slots = line.run(
        feed_slots_kernel,
        "feed_slots",
        [],
        [own_sums, passed_sums, own_bias, passed_bias],
        [shape((1, units), F32)] + [shape((units // 2, width))] * 4,
    )
    feed_bank = Bank(line, slots, size)
    middle_back(last)
    head_grads[0][1:] = line.split(*head_grads[0][1:])
    blocks_across = chip_swap(line.join(*(feeds[k][1] for k in each)))

    def attend_back(r, picked, before):
        final = picked[-1] == heads - 1
        some = len(picked)
        made = local if final else some * HEAD_DIM
        grad_proj, *parts = line.run(
            partial(attend_back_kernel, r, picked),
            "attend_back",
            [windows],
            [near, far[r], marks, logs[r], waves, *head_grads[r]]
            + before
            + ([proj_weight] if final else []),
            [shape((3 * made, length))]
            + ([full, full] if final else [])
            + ([full, full] if final and r == last else [])
            + ([shape((2, block, width))] if final and r < last else []),
            [
                pltpu.VMEM((some * KEY_ROWS, length), BF16),
                pltpu.VMEM((some, length, KEY_ROWS), BF16),
                pltpu.VMEM((some * HEAD_DIM, length), BF16),
                pltpu.VMEM((some, length, HEAD_DIM), BF16),
                pltpu.VMEM((some, length, HEAD_DIM), BF16),
                pltpu.VMEM((some * HEAD_DIM, length), BF16),
                pltpu.VMEM((some, length, HEAD_DIM), BF16),
                pltpu.VMEM((some, length, HEAD_DIM), F32),
                pltpu.VMEM((some, length, HEAD_DIM), F32),
                pltpu.VMEM((some * HEAD_DIM, length), F32),
            ],
            vmem=20,
        )
        if not final:
            return [grad_proj]
        projs.append(grad_proj)
        first_grads.append([parts[0], parts[1], *(core_swap(v) for v in parts[2:])])

    projs, first_grads = [], []
    for r in each:
        if r > 0:
            head_grads[r][1:] = line.split(*head_grads[r][1:])
        if r == last:
            feed_bank.advance()
            out_parts = line.run(
                partial(out_weight_kernel, rows),
                "out_weight",
                [],
                [*sum(attended, []), *grad_branches],
                [shape((local, width))] * 2 + [shape((2, local, width))],
            )
            out_beside = core_swap(out_parts[2])
            (back,) = line.add([(out_parts[1],), (out_beside, 1)])
            out_sums = [out_parts[0], out_beside, chip_swap(back)]
        attend_back(r, tuple(range(heads)), [])
    grads_in, first_sums = [], []

    def first_back(r):
        own, _, beside, *_ = first_grads[r]
        grad_in, sums = line.run(
            partial(first_back_kernel, r),
            "first_back",
            [],
            [own, beside, first_across_back[r], hid, grad_middles[r], vectors],
            [shape((block, width), F32), shape((8, width), F32)],
        )
        grads_in.append(grad_in)
        first_sums.append(sums)

    *slots, proj_bias_sum = line.run(
        partial(project_weights_kernel, rows),
        "project_weights",
        [],
        [*projs, first, first_beside, *far_slots, *out_sums],
        [shape((local, width))] * 4 + [shape((8, width), F32)],
        [pltpu.VMEM((4 * local, width), F32)],
        vmem=10,
    )
    head_bank = Bank(line, slots, size)
    first_across_back = []
    for r in each:
        far_part = [(first_grads[r][2], 1)] if r < last else [(first_grads[r][3],)]
        (back,) = line.add([(first_grads[r][1],), *far_part])
        first_across_back.append(chip_swap(back))
    blocks_out = line.run(
        partial(block_out_kernel, rows),
        "block_out",
        [],
        [*(feeds[r][0] for r in each), *middles, blocks_across, vectors],
        [full] * rows,
    )
    block_out = jnp.stack(blocks_out, axis=1)
    while not feed_bank.done:
        feed_bank.advance()
    head_bank.advance()
    for r in each:
        first_back(r)
    input_grad = jnp.stack(grads_in, axis=1)
    (small,) = line.run(
        lambda *refs: small_kernel(refs[:rows], refs[rows : 2 * rows], refs[2 * rows]),
        "small",
        [],
        [*first_sums, *norm_sums],
        [shape((8, width), F32)],
    )
    (small,) = line.add([(small,), (core_swap(small),)])
    (small,) = line.run(
        small_extra_kernel,
        "small_extra",
        [],
        [small, chip_swap(small), in_bias_sum, proj_bias_sum],
        [shape((8, width), F32)],
    )
    while not head_bank.done:
        head_bank.advance()
    bit = 1
    while 2 * bit < size:
        (small,) = line.add([(small,), (swap(small, "dp", size, bit),)])
        bit *= 2
    *lines, grad_proj_bias = line.run(
        finish_small_kernel,
        "finish_small",
        [],
        [small, swap(small, "dp", size, bit)],
        [shape((width,), F32)] * 7 + [shape((3, local), F32)],
        [pltpu.VMEM((8, width), F32)],
    )
    grad_down_weight, grad_in_weight = line.run(
        finish_kernel,
        "finish",
        [],
        feed_bank.slots,
        [shape((units, width), F32), shape((width, units), F32)],
    )
    grad_qkv_weight, grad_out_weight = line.run(
        finish_project_kernel,
        "finish_project",
        [],
        head_bank.slots,
        [shape((3 * local, width), F32), shape((local, width), F32)],
        [pltpu.VMEM((4 * local, width), F32)],
    )
    grad_qkv_weight = jnp.transpose(grad_qkv_weight.reshape(3, local, width), (0, 2, 1))
    return (
        block_out,
        input_grad,
        lines[0],
        lines[1],
        grad_qkv_weight,
        grad_proj_bias,
        grad_out_weight,
        lines[5],
        lines[2],
        lines[3],
        grad_in_weight,
        lines[6],
        grad_down_weight,
        lines[4],
    )


def solution(mesh):
    sharded = P("tp", "dp", None)
    return jax.shard_map(
        partial(on_device, mesh.shape["dp"]),
        mesh=mesh,
        in_specs=(
            sharded,
            P("dp", None),
            sharded,
            P(),
            P(),
            P(None, None, "tp"),
            P(None, "tp"),
            P("tp", None),
            P(),
            P(),
            P(),
            P(None, "tp"),
            P("tp"),
            P("tp", None),
            P(),
        ),
        out_specs=(
            sharded,
            sharded,
            P(),
            P(),
            P(None, None, "tp"),
            P(None, "tp"),
            P("tp", None),
            P(),
            P(),
            P(),
            P(None, "tp"),
            P("tp"),
            P("tp", None),
            P(),
        ),
        check_vma=False,
    )
```

```python
from functools import partial

import jax
import jax.numpy as jnp
import numpy as np
from jax import lax
from jax.experimental import pallas as pl
from jax.experimental.pallas import tpu as pltpu
from jax.sharding import PartitionSpec as P

HEAD_DIM = 64
HALF = HEAD_DIM // 2
KEY_ROWS = 128
EPSILON = 1e-05
APART = -1e30
F32 = jnp.float32
BF16 = jnp.bfloat16

NN = (((1,), (0,)), ((), ()))
NT = (((1,), (1,)), ((), ()))
TN = (((0,), (0,)), ((), ()))


def dot(a, b, dims=NN):
    return lax.dot_general(a, b, dims, preferred_element_type=F32)


def shape(dims, dtype=BF16):
    return jax.ShapeDtypeStruct(dims, dtype)


class Line:
    def __init__(self):
        self.tile = None

    def run(
        self, body, name, scalars, arrays, outs, scratch=(), vmem=8, inputs=None, numbers=(), places=None
    ):
        before = [] if self.tile is None else [self.tile]
        count, extra, made = len(scalars) + len(arrays), len(before), len(outs)
        made += len(numbers)

        def whole(*refs):
            tile = refs[count + extra + made]
            tile[...] = jnp.zeros_like(tile)
            body(
                *refs[:count],
                *refs[count + extra : count + extra + made],
                *refs[count + extra + made + 1 :],
            )

        vector = pl.BlockSpec(memory_space=pltpu.VMEM)
        scalar = pl.BlockSpec(memory_space=pltpu.SMEM)
        *results, self.tile = pl.pallas_call(
            whole,
            out_shape=(*numbers, *outs, shape((8, 128), F32)),
            in_specs=[scalar] * len(scalars)
            + (inputs or [vector] * len(arrays))
            + [vector] * extra,
            out_specs=(scalar,) * len(numbers)
            + (tuple(places) if places else (vector,) * len(outs))
            + (vector,),
            scratch_shapes=list(scratch),
            compiler_params=pltpu.CompilerParams(vmem_limit_bytes=vmem * 1024 * 1024),
            cost_estimate=pl.CostEstimate(flops=1, bytes_accessed=1, transcendentals=0),
            name=name,
        )(*scalars, *arrays, *before)
        return results

    def keep(self, *arrays):
        def body(*refs):
            for k in range(len(arrays)):
                refs[len(arrays) + k][...] = refs[k][...]

        return self.run(body, "keep", [], arrays, [shape(v.shape, v.dtype) for v in arrays])

    def split(self, near, pair):
        def body(near, pair, one, two):
            one[...] = pair[0]
            two[0] = near[...]
            two[1] = pair[1]

        made = [shape(near.shape), shape((2, *near.shape))]
        one, two = self.run(body, "split", [], [near, pair], made)
        return [one, core_swap(two)]

    def merge(self, one, two, cuts):
        def body(one, two, *outs):
            total = one[...].astype(F32) + two[...].astype(F32)
            size = total.shape[0] // cuts
            for k, out in enumerate(outs):
                out[...] = total[k * size : (k + 1) * size].astype(out.dtype)

        made = [shape((one.shape[0] // cuts, *one.shape[1:]))] * cuts
        return self.run(body, "merge", [], [one, two], made)

    def join(self, *arrays):
        def body(*refs):
            for k in range(len(arrays)):
                refs[len(arrays)][k] = refs[k][...]

        first = arrays[0]
        made = [shape((len(arrays), *first.shape), first.dtype)]
        return self.run(body, "join", [], arrays, made, vmem=8)[0]

    def add_rows(self, ones, twos):
        count = len(ones)

        def body(*refs):
            for r in range(count):
                total = refs[r][...].astype(F32) + refs[count + r][1].astype(F32)
                refs[2 * count][r] = total.astype(BF16)

        made = [shape((count, *ones[0].shape))]
        return self.run(body, "add_rows", [], [*ones, *twos], made)[0]

    def add_pair(self, one, two):
        def body(a, b, c, d, out):
            out[0] = (a[...].astype(F32) + b[...].astype(F32)).astype(out.dtype)
            out[1] = (c[...].astype(F32) + d[...].astype(F32)).astype(out.dtype)

        made = [shape((2, *one[0].shape), one[0].dtype)]
        return self.run(body, "add_pair", [], [*one, *two], made)[0]

    def add(self, *sums):
        arrays = [term[0] for terms in sums for term in terms]
        parts = [[term[1:] for term in terms] for terms in sums]
        outs = []
        for terms in sums:
            first = terms[0][0]
            outs.append(shape(first.shape[len(terms[0]) - 1 :], first.dtype))

        def body(*refs):
            at = 0
            for k, terms in enumerate(parts):
                total = None
                for index in terms:
                    value = refs[at][index[0]] if index else refs[at][...]
                    value = value.astype(F32)
                    total = value if total is None else total + value
                    at += 1
                out = refs[len(arrays) + k]
                out[...] = total.astype(out.dtype)

        return self.run(body, "add", [], arrays, outs)


def normalize(values):
    average = jnp.mean(values, axis=-1, keepdims=True)
    centered = values - average
    variance = jnp.mean(centered * centered, axis=-1, keepdims=True)
    inverse = lax.rsqrt(variance + EPSILON)
    return centered * inverse, inverse


def normalize_back(gradient, scaled, inverse, gain):
    grad_scaled = gradient * gain
    return inverse * (
        grad_scaled
        - jnp.mean(grad_scaled, axis=-1, keepdims=True)
        - scaled * jnp.mean(grad_scaled * scaled, axis=-1, keepdims=True)
    )


def where_am_i():
    me = lax.axis_index("tp")
    return me, me // 2, lax.axis_index("dp") & 3


def first_norm_kernel(rows, width, hid, *refs):
    lines, (w_in, w_out, vectors, first, alone, joined) = refs[:7], refs[7:13]
    lands, sems = refs[13:20], refs[20]
    copies = [
        pltpu.make_async_copy(line, land, sems.at[k])
        for k, (line, land) in enumerate(zip(lines, lands))
    ]
    sends = [
        pltpu.make_async_copy(w_in, joined.at[0], sems.at[7]),
        pltpu.make_async_copy(w_out, joined.at[1], sems.at[8]),
    ]
    for copy in copies + sends:
        copy.start()
    normed = []
    for r in range(rows):
        values = hid[:, r * width : (r + 1) * width].astype(F32)
        normed.append(normalize(values)[0])
    for copy in copies:
        copy.wait()
    for k, land in enumerate(lands):
        vectors[k : k + 1, :] = land[...].astype(F32).reshape(1, width)
    vectors[7:8, :] = jnp.zeros((1, width), F32)
    for r in range(rows):
        low = (normed[r] * vectors[0:1, :] + vectors[1:2, :]).astype(BF16)
        first[r] = low
        if r == 0:
            alone[...] = low
    for copy in sends:
        copy.wait()


def table_kernel(block, segments, rates, bias, windows, marks, waves, column):
    rows, length = segments.shape
    ids = lax.broadcasted_iota(jnp.int32, (16, length), 0)
    spots = lax.broadcasted_iota(jnp.int32, (1, length), 1)
    for r in range(rows):
        row = segments[r : r + 1, :]
        same = row == ids
        before = jnp.sum((row < ids).astype(F32), axis=1, keepdims=True)
        begins = jnp.sum(jnp.where(same, before, 0.0), axis=0, keepdims=True)
        ends = jnp.sum((row <= ids).astype(F32), axis=1, keepdims=True)
        closes = jnp.sum(jnp.where(same, ends, 0.0), axis=0, keepdims=True)
        marks[r, 0] = same.astype(F32).astype(BF16)
        marks[r, 1] = jnp.where(same | (ids >= 8), 0.0, APART).astype(BF16)
        angles = rates[...] * (spots.astype(F32) - begins)
        waves[r, 0] = jnp.cos(angles)
        waves[r, 1] = jnp.sin(angles)
        blocks = length // block
        for q in range(blocks):
            inside = slice(q * block, (q + 1) * block)
            least = jnp.min(begins[:, inside]).astype(jnp.int32)
            past = jnp.max(closes[:, inside]).astype(jnp.int32)
            start = (least // 128) * 128
            count = (past - start + block - 1) // block
            windows[2 * blocks * r + q] = jnp.minimum(start, length - count * block)
            windows[2 * blocks * r + blocks + q] = count
    local = bias.shape[1]
    tall = jnp.concatenate([bias[...].astype(F32), jnp.zeros((5, local), F32)], axis=0)
    tall = jnp.transpose(tall)
    for c in range(3):
        column[c * local : (c + 1) * local, :] = tall[:, c : c + 1]


def split_kernel(width, whole, *outs):
    for r, out in enumerate(outs):
        out[...] = whole[:, r * width : (r + 1) * width]


def project_kernel(far, picked, one, two, weight, bias, waves, out):
    block = two.shape[-2]
    local = weight.shape[0] // 3
    me, chip, _ = where_am_i()
    half = chip ^ far
    for at, r in enumerate(picked):
        for k, tokens in enumerate((one, two)):
            spot = pl.multiple_of(((me & 1) ^ k) * block, block)
            span = pl.ds(spot, block)
            table = pl.ds(pl.multiple_of(half * (2 * block) + spot, block), block)
            values = tokens[at] if len(tokens.shape) == 3 else tokens[...]
            turned = dot(weight[...], values, NT) + bias[...]
            cs = waves[r, 0, :, table]
            sn = waves[r, 1, :, table]
            for c in range(2):
                for base in range(c * local, (c + 1) * local, HEAD_DIM):
                    a = turned[base : base + HALF]
                    b = turned[base + HALF : base + HEAD_DIM]
                    new_a = a * cs - b * sn
                    new_b = b * cs + a * sn
                    if c == 0:
                        new_a = new_a * HEAD_DIM**-0.5
                        new_b = new_b * HEAD_DIM**-0.5
                    out[at, base : base + HALF, span] = new_a.astype(BF16)
                    out[at, base + HALF : base + HEAD_DIM, span] = new_b.astype(BF16)
            out[at, 2 * local :, span] = turned[2 * local :].astype(BF16)


def turn_over(values):
    return jnp.transpose(values.astype(F32)).astype(BF16)


def sides(r, near, far):
    chip = where_am_i()[1]
    width = near.shape[-1]
    return [
        (source, pl.ds(pl.multiple_of(at, width), width))
        for source, at in ((near.at[r], chip * width), (far.at[0], (1 - chip) * width))
    ]


def lay_out(r, picked, near, far, marked, queries, keys):
    mine = marked[r, 0]
    width = near.shape[-1]
    local = near.shape[1] // 3
    marks = mine.shape[0]
    for source, span in sides(r, near, far):
        for at, h in enumerate(picked):
            queries[at * KEY_ROWS : at * KEY_ROWS + HEAD_DIM, span] = source[
                h * HEAD_DIM : (h + 1) * HEAD_DIM, :
            ]
            column = jnp.concatenate(
                [
                    source[local + h * HEAD_DIM : local + (h + 1) * HEAD_DIM, :],
                    marked[r, 1, :, span],
                    jnp.zeros((KEY_ROWS - HEAD_DIM - marks, width), BF16),
                ],
                axis=0,
            )
            keys[at, span, :] = turn_over(column)
    for at in range(len(picked)):
        base = at * KEY_ROWS + HEAD_DIM
        queries[base : base + marks, :] = mine
        queries[base + marks : (at + 1) * KEY_ROWS, :] = jnp.zeros(
            (KEY_ROWS - HEAD_DIM - marks, queries.shape[1]), BF16
        )


def attend_kernel(r, windows, near, far, marked, *rest):
    outs, (log_norm, queries, keys, values, attended) = rest[:3], rest[3:]
    block = near.shape[-1] // 2
    local = near.shape[1] // 3
    heads = local // HEAD_DIM
    me = where_am_i()[0]
    lay_out(r, range(heads), near, far, marked, queries, keys)
    for source, span in sides(r, near, far):
        values[:, span] = source[2 * local :, :]

    @pl.loop(0, 4)
    def _(quarter):
        span = pl.ds(pl.multiple_of(quarter * block, block), block)
        start = pl.multiple_of(windows[8 * r + quarter], 128)
        count = windows[8 * r + 4 + quarter]

        def work(blocks):
            window = pl.ds(start, blocks * block)

            @pl.loop(0, heads)
            def _(h):
                part = pl.ds(pl.multiple_of(h * HEAD_DIM, HEAD_DIM), HEAD_DIM)
                rows = pl.ds(pl.multiple_of(h * KEY_ROWS, KEY_ROWS), KEY_ROWS)
                scores = dot(keys[h, window, :], queries[rows, span])
                peak = jnp.max(scores, axis=0, keepdims=True)
                weights = jnp.exp(scores - peak)
                total = jnp.sum(weights, axis=0, keepdims=True)
                out = dot(values[part, window], weights.astype(BF16))
                attended[part, span] = (out * (1.0 / total)).astype(BF16)
                log_norm[pl.ds(h, 1), span] = peak + jnp.log(total)

        for blocks in range(1, 5):
            pl.when(count == blocks)(partial(work, blocks))

    for s, out in enumerate((outs[0], outs[1], outs[2].at[0], outs[2].at[1])):
        out[...] = attended[:, pl.ds(pl.multiple_of((me ^ s) * block, block), block)]


def attend_back_kernel(r, picked, windows, near, far, marked, log_norm, waves, *rest):
    grads = (rest[0], rest[2].at[0], rest[1], rest[2].at[1])
    scratch, rest = rest[-10:], rest[3:-10]
    queries, keys, key_rows, value_cols, query_cols, grad_rows, grad_cols, dk, dv, dq = scratch
    block = near.shape[-1] // 2
    local = near.shape[1] // 3
    heads = local // HEAD_DIM
    me = where_am_i()[0]
    if len(rest) == 1:
        before, weight, grad_proj, partials = None, None, rest[0], ()
    else:
        before = rest[0] if rest[0].shape[0] < rest[1].shape[0] else None
        weight, grad_proj, own, across, *sent = rest[1:] if before is not None else rest
        if len(sent) == 1:
            sent = (sent[0].at[0], sent[0].at[1])
        partials = (own, sent[0], across, sent[1])
    stride = grad_proj.shape[0] // 3
    first = picked[0] if weight is None else 0
    lay_out(r, picked, near, far, marked, queries, keys)
    for source, span in sides(r, near, far):
        for at, h in enumerate(picked):
            part = slice(at * HEAD_DIM, (at + 1) * HEAD_DIM)
            key_rows[part, span] = source[local + h * HEAD_DIM : local + (h + 1) * HEAD_DIM, :]
            query_cols[at, span, :] = turn_over(source[h * HEAD_DIM : (h + 1) * HEAD_DIM, :])
            value_cols[at, span, :] = turn_over(
                source[2 * local + h * HEAD_DIM : 2 * local + (h + 1) * HEAD_DIM, :]
            )
    for s, grad in enumerate(grads):
        span = pl.ds(pl.multiple_of((me ^ s) * block, block), block)
        for at, h in enumerate(picked):
            rows = grad[h * HEAD_DIM : (h + 1) * HEAD_DIM, :]
            grad_rows[at * HEAD_DIM : (at + 1) * HEAD_DIM, span] = rows
            grad_cols[at, span, :] = turn_over(rows)
    dk[...] = jnp.zeros_like(dk)
    dv[...] = jnp.zeros_like(dv)

    @pl.loop(0, 4)
    def _(quarter):
        span = pl.ds(pl.multiple_of(quarter * block, block), block)
        start = pl.multiple_of(windows[8 * r + quarter], 128)
        count = windows[8 * r + 4 + quarter]

        def work(blocks):
            window = pl.ds(start, blocks * block)
            for at, h in enumerate(picked):
                part = slice(at * HEAD_DIM, (at + 1) * HEAD_DIM)
                scores = dot(
                    keys[at, window, :], queries[at * KEY_ROWS : (at + 1) * KEY_ROWS, span]
                )
                probs = jnp.exp(scores - log_norm[h : h + 1, span])
                grad_probs = dot(value_cols[at, window, :], grad_rows[part, span])
                inner = jnp.sum(probs * grad_probs, axis=0, keepdims=True)
                grad_scores = (probs * (grad_probs - inner)).astype(BF16)
                dv[at, window, :] += dot(probs.astype(BF16), grad_cols[at, span, :])
                dk[at, window, :] += dot(grad_scores, query_cols[at, span, :])
                dq[part, span] = dot(key_rows[part, window], grad_scores)

        for blocks in range(1, 5):
            pl.when(count == blocks)(partial(work, blocks))

    cs = waves[r, 0]
    sn = waves[r, 1]

    def turn_back(rows, base):
        a = rows[:HALF]
        b = rows[HALF:]
        grad_proj[base : base + HALF, :] = (a * cs + b * sn).astype(BF16)
        grad_proj[base + HALF : base + HEAD_DIM, :] = (b * cs - a * sn).astype(BF16)

    for at, h in enumerate(picked):
        base = (h - first) * HEAD_DIM
        turn_back(dq[at * HEAD_DIM : (at + 1) * HEAD_DIM, :] * HEAD_DIM**-0.5, base)
        turn_back(jnp.transpose(dk[at]), stride + base)
        base += 2 * stride
        grad_proj[base : base + HEAD_DIM, :] = jnp.transpose(dv[at]).astype(BF16)
    if before is not None:
        had = before.shape[0] // 3
        for c in range(3):
            grad_proj[c * stride : c * stride + had, :] = before[c * had : (c + 1) * had, :]
    for s, partial_out in enumerate(partials):
        span = pl.ds(pl.multiple_of((me ^ s) * block, block), block)
        partial_out[...] = dot(grad_proj[:, span], weight[...], TN).astype(BF16)


def four(parts):
    return (parts[0], parts[2].at[0], parts[1], parts[2].at[1])


def middle_kernel(row, hid, *rest):
    attended, weights = four(rest[:3]), rest[3:7]
    vectors, cot, middle, second, pair = rest[7:12]
    width = vectors.shape[1]
    branch = vectors[2:3, :]
    for a, w in zip(attended, weights):
        branch = branch + dot(a[...], w[...], TN)
    values = hid[:, row * width : (row + 1) * width].astype(F32) + branch
    middle[...] = values
    scaled, _ = normalize(values)
    low = (scaled * vectors[3:4, :] + vectors[4:5, :]).astype(BF16)
    second[...] = low
    pair[0] = low
    pair[1] = cot[...]


def gelu_parts(h):
    size = jnp.abs(h)
    t = 1.0 / (1.0 + size * (0.3275911 * 0.5**0.5))
    density = jnp.exp(h * h * -0.5)
    poly = t * (
        0.254829592
        + t * (-0.284496736 + t * (1.421413741 + t * (-1.453152027 + t * 1.061405429)))
    )
    tail = 0.5 * poly * density
    below = jnp.where(h < 0, tail, 1.0 - tail)
    return below, density * 0.3989422804014327


def feed_kernel(second, cot, w_in, w_out, vectors, passed, passed_vectors, act, grad_pre, *outs):
    if cot is None:
        second, cot = second.at[0], second.at[1]
    units = w_in.shape[1]
    width = w_in.shape[0]
    step = 256
    tokens = second[...]
    portion = cot[...]
    for side, lines in enumerate((vectors, passed_vectors)):
        for u in range(0, units, step):
            cols = slice(u, u + step)
            spot = slice(side * units + u, side * units + u + step)
            into = passed[:width, cols] if side else w_in[:, cols]
            down = passed[width + u : width + u + step, :] if side else w_out[cols, :]
            pre = dot(tokens, into) + lines[6:7, cols]
            below, density = gelu_parts(pre)
            act[:, spot] = (pre * below).astype(BF16)
            grad_act = dot(portion, down, NT)
            grad_pre[:, spot] = (grad_act * (below + pre * density)).astype(BF16)
    out = dot(act[:, :units], w_out[...]) + dot(act[:, units:], passed[width:, :])
    grad = dot(grad_pre[:, :units], w_in[...], NT) + dot(
        grad_pre[:, units:], passed[:width, :], NT
    )
    half = out.shape[0] // 2
    outs[0][...] = out.astype(BF16)
    low = grad.astype(BF16)
    if len(outs) == 2:
        outs[1][...] = low
    else:
        outs[1][...] = low[:half]
        outs[2][...] = low[half:]


def feed_weights_kernel(count, *refs):
    near = count // 2
    seconds, cots, pairs = refs[:near], refs[near:count], refs[count : count + near]
    seconds = [*seconds, *(pair.at[0] for pair in pairs)]
    cots = [*cots, *(pair.at[1] for pair in pairs)]
    refs = refs[count + near :]
    acts, pres = refs[:count], refs[count : 2 * count]
    own, passed, own_bias, passed_bias, down, up = refs[2 * count :]
    units = own.shape[1]
    for k in range(count):
        pre = pres[k][...]
        part_down = dot(acts[k][...], cots[k][...], TN)
        part_up = dot(seconds[k][...], pre, TN)
        sums = jnp.sum(pre.astype(F32), axis=0, keepdims=True)
        if k == 0:
            down[...] = part_down
            up[...] = part_up
            added = sums
        else:
            down[...] += part_down
            up[...] += part_up
            added += sums
    own_bias[...] = added[:, :units]
    passed_bias[...] = jnp.broadcast_to(added[:, units:], passed_bias.shape)
    own[0] = down[:units, :].astype(BF16)
    own[1] = up[:, :units].astype(BF16)
    passed[0] = down[units:, :].astype(BF16)
    passed[1] = up[:, units:].astype(BF16)


def feed_slots_kernel(own, passed, own_bias, passed_bias, bias, *outs):
    piece = outs[0].shape[0] // 2
    spot = where_am_i()[2]
    bias[...] = own_bias[...] + passed_bias[0:1, :]
    for s, out in enumerate(outs):
        span = pl.ds(pl.multiple_of((spot ^ s) * piece, piece), piece)
        for bank in range(2):
            total = own[bank, span, :].astype(F32) + passed[bank, span, :].astype(F32)
            out[bank * piece : (bank + 1) * piece, :] = total.astype(BF16)


def middle_back_kernel(chips, own, *rest):
    chip, rest = rest[:chips], rest[chips:]
    middle, cot, vectors = rest[:3]
    weights, outs = rest[3:7], rest[7:]
    grad_middle, grad_branch, sums = outs[0], outs[1], outs[5]
    heads = (outs[2], outs[3], outs[4].at[0], outs[4].at[1])
    across = jnp.concatenate([part[...] for part in chip], axis=0) if chips > 1 else chip[0][...]
    grad_second = own[...].astype(F32) + across.astype(F32)
    scaled, inverse = normalize(middle[...])
    grad_out = cot[...].astype(F32)
    total = grad_out + normalize_back(grad_second, scaled, inverse, vectors[3:4, :])
    low = total.astype(BF16)
    grad_middle[...] = total
    grad_branch[...] = low
    for w, out in zip(weights, heads):
        out[...] = dot(w[...], low, NT).astype(BF16)
    sums[0:1, :] = jnp.sum(grad_second * scaled, axis=0, keepdims=True)
    sums[1:2, :] = jnp.sum(grad_second, axis=0, keepdims=True)
    sums[2:3, :] = jnp.sum(grad_out, axis=0, keepdims=True)
    sums[3:4, :] = jnp.sum(low.astype(F32), axis=0, keepdims=True)
    sums[4:, :] = jnp.zeros((4, sums.shape[1]), F32)


def out_weight_kernel(rows, *refs):
    attended, grads, outs = refs[: 3 * rows], refs[3 * rows : 4 * rows], refs[4 * rows :]
    attended = [four(attended[3 * r : 3 * r + 3]) for r in range(rows)]
    own, across, sent = outs
    for s, out in enumerate((own, sent.at[0], across, sent.at[1])):
        total = dot(attended[0][s][...], grads[0][...])
        for r in range(1, rows):
            total = total + dot(attended[r][s][...], grads[r][...])
        out[...] = total.astype(BF16)


def project_weights_kernel(rows, *refs):
    projs, near, far = refs[:rows], refs[rows : rows + 2], refs[rows + 2 : 3 * rows + 2]
    refs = refs[3 * rows + 2 :]
    own, swapped, chip = refs[:3]
    outs, (bias, total) = refs[3:7], refs[7:]
    block = near[0].shape[1]
    me, _, spot = where_am_i()
    size = projs[0].shape[0]
    local = size // 3
    ones = jnp.ones((8, projs[0].shape[1]), BF16)
    bias[...] = jnp.zeros_like(bias)
    for c in range(3):
        part = slice(c * local, (c + 1) * local)
        sums = dot(ones, projs[0][part, :], NT)
        for r in range(1, rows):
            sums += dot(ones, projs[r][part, :], NT)
        bias[:, 256 * c : 256 * c + local] = sums
    for r in range(rows):
        for s in range(4):
            span = pl.ds(pl.multiple_of((me ^ s) * block, block), block)
            tokens = near[s][r] if s < 2 else far[2 * r + s - 2][...]
            product = dot(projs[r][:, span], tokens)
            if r + s == 0:
                total[:size, :] = product
            else:
                total[:size, :] += product
    total[size:, :] = own[...].astype(F32) + swapped[0].astype(F32) + chip[...].astype(F32)
    piece = outs[0].shape[0]
    for s, out in enumerate(outs):
        at = pl.multiple_of((spot ^ s) * piece, piece)
        out[...] = total[pl.ds(at, piece), :].astype(BF16)


def finish_kernel(*refs):
    spot = where_am_i()[2]
    slots, outs = refs[:4], refs[4:]
    for s, slot in enumerate(slots):
        piece = slot.shape[0] // 2
        span = pl.ds(pl.multiple_of((spot ^ s) * piece, piece), piece)
        for k, out in enumerate(outs):
            out[span, :] = slot[k * piece : (k + 1) * piece, :].astype(F32)


def finish_project_kernel(*refs):
    spot = where_am_i()[2]
    slots, (big, small, total) = refs[:4], refs[4:]
    for s, slot in enumerate(slots):
        piece = slot.shape[0]
        at = pl.multiple_of((spot ^ s) * piece, piece)
        total[pl.ds(at, piece), :] = slot[...].astype(F32)
    size = big.shape[0]
    big[...] = total[:size, :]
    small[...] = total[size:, :]


def first_back_kernel(row, own, beside, chip, hid, grad_middle, vectors, grad_in, sums):
    width = vectors.shape[1]
    swapped = beside[0] if len(beside.shape) == 3 else beside[...]
    grad_first = own[...].astype(F32) + swapped.astype(F32) + chip[...].astype(F32)
    scaled, inverse = normalize(hid[:, row * width : (row + 1) * width].astype(F32))
    grad_in[...] = grad_middle[...] + normalize_back(grad_first, scaled, inverse, vectors[0:1, :])
    sums[0:1, :] = jnp.sum(grad_first * scaled, axis=0, keepdims=True)
    sums[1:2, :] = jnp.sum(grad_first, axis=0, keepdims=True)
    sums[2:, :] = jnp.zeros((6, width), F32)


def small_kernel(firsts, middles, out):
    rows = len(firsts)
    out[...] = jnp.zeros_like(out)
    out[0:2, :] = sum(ref[0:2, :] for ref in firsts)
    out[2:6, :] = sum(ref[0:4, :] for ref in middles)


def small_extra_kernel(one, two, in_bias, proj_bias, out):
    out[...] = one[...] + two[...]
    out[6:7, :] = in_bias[...]
    out[7:8, :] = proj_bias[0:1, :]


def finish_small_kernel(one, two, *outs):
    *lines, proj_bias, total = outs
    total[...] = one[...] + two[...]
    width = total.shape[1]
    for k, line in enumerate(lines):
        line[...] = total[k : k + 1, :].reshape(width)
    local = proj_bias.shape[1]
    for c in range(3):
        proj_bias[c : c + 1, :] = total[7:8, 256 * c : 256 * c + local]


def block_out_kernel(own, middle, across, vectors, out):
    total = own[...].astype(F32) + across[...].astype(F32)
    out[...] = (middle[...] + (total + vectors[5:6, :])).astype(BF16)


def swap(values, axis, size, bit):
    return lax.ppermute(values, axis, [(i, i ^ bit) for i in range(size)])


def core_swap(values):
    return swap(values, "tp", 4, 1)


def chip_swap(values):
    return swap(values, "tp", 4, 2)


class Bank:
    def __init__(self, line, slots, size):
        self.line, self.own, self.size = line, slots[0], size
        self.moved = [swap(slots[s], "dp", size, s) for s in range(1, 4)]
        self.bit = 2

    def advance(self):
        (self.own,) = self.line.add([(self.own,), *((v,) for v in self.moved)])
        self.bit *= 2
        if self.bit < self.size:
            self.moved = [swap(self.own, "dp", self.size, self.bit)]
            return
        self.slots = [self.own] + [swap(self.own, "dp", self.size, s) for s in range(1, 4)]

    @property
    def done(self):
        return self.bit >= self.size


def on_device(
    size,
    hidden_in,
    segment_ids,
    cotangent,
    norm1_gain,
    norm1_bias,
    qkv_weight,
    qkv_bias,
    out_weight,
    out_bias,
    norm2_gain,
    norm2_bias,
    ffn_in_weight,
    ffn_in_bias,
    ffn_out_weight,
    ffn_out_bias,
):
    block, rows, width = hidden_in.shape
    length = segment_ids.shape[1]
    local = qkv_weight.shape[2]
    heads = local // HEAD_DIM
    units = ffn_in_weight.shape[1]
    line = Line()
    each, last = range(rows), rows - 1
    full, half, both = shape((block, width)), shape((block // 2, width)), shape((rows, block, width))
    hid = hidden_in.reshape(block, rows * width)
    cots = cotangent.reshape(block, rows * width)
    vector, anywhere = pl.BlockSpec(memory_space=pltpu.VMEM), pl.BlockSpec(memory_space=pltpu.HBM)
    params = [norm1_gain, norm1_bias, out_bias, norm2_gain, norm2_bias, ffn_out_bias, ffn_in_bias]
    vectors, first, alone, joined = line.run(
        partial(first_norm_kernel, rows, width),
        "first_norm",
        [],
        [hid, *params, ffn_in_weight, ffn_out_weight],
        [shape((8, width), F32), both, full, shape((2, *ffn_in_weight.shape))],
        [pltpu.VMEM((width,), BF16)] * 7 + [pltpu.SemaphoreType.DMA((9,))],
        inputs=[vector] + [anywhere] * 9,
        places=[vector] * 3 + [anywhere],
    )
    first_across = [chip_swap(alone)]
    first_beside = core_swap(first)
    passed = core_swap(joined).reshape(2 * width, -1)
    passed_vectors = core_swap(vectors)

    rates = np.power(10000.0, -2.0 * np.arange(HALF) / HEAD_DIM).astype(np.float32)
    windows, marks, waves, proj_bias = line.run(
        partial(table_kernel, block),
        "tables",
        [],
        [segment_ids, jnp.asarray(rates.reshape(HALF, 1)), qkv_bias],
        [
            shape((rows, 2, 16, length)),
            shape((rows, 2, HALF, length), F32),
            shape((3 * local, 1), F32),
        ],
        numbers=[shape((rows * 2 * (length // block),), jnp.int32)],
    )
    proj_weight = jnp.transpose(qkv_weight, (0, 2, 1)).reshape(3 * local, width)

    def project(far, picked, one, two):
        return line.run(
            partial(project_kernel, far, picked),
            "project",
            [],
            [one, two, proj_weight, proj_bias, waves],
            [shape((len(picked), 3 * local, 2 * block))],
        )[0]

    def attend(r):
        *outs, log_norm = line.run(
            partial(attend_kernel, r),
            "attend",
            [windows],
            [near, far[r], marks],
            [shape((local, block))] * 2
            + [shape((2, local, block)), shape((8, length), F32)],
            [
                pltpu.VMEM((heads * KEY_ROWS, length), BF16),
                pltpu.VMEM((heads, length, KEY_ROWS), BF16),
                pltpu.VMEM((local, length), BF16),
                pltpu.VMEM((local, length), BF16),
            ],
            vmem=14,
        )
        logs.append(log_norm)
        return [outs[0], outs[1], chip_swap(outs[2])]

    def feed(*tokens):
        tokens = list(tokens)

        def body(*refs):
            feed_kernel(*(refs if len(tokens) == 2 else (refs[0], None, *refs[1:])))

        act, pre, *outs = line.run(
            body,
            "feed",
            [],
            tokens + [ffn_in_weight, ffn_out_weight, vectors, passed, passed_vectors],
            [shape((block, 2 * units))] * 2 + [full, full],
            vmem=12,
        )
        acts.append(act)
        pres.append(pre)
        return outs

    def pick(values, r):
        def body(values, out):
            out[...] = values[r]

        return line.run(body, "pick", [], [values], [shape(values.shape[1:])])[0]

    near = project(0, tuple(each), first, first_beside)
    cots = line.run(partial(split_kernel, width), "split", [], [cots], [full] * rows)
    far, far_slots = [], []
    logs, attended = [], []
    for r in each:
        (arrived,) = line.keep(first_across[r])
        far_slots += [arrived, core_swap(arrived)]
        if r < last:
            first_across.append(chip_swap(pick(first, r + 1)))
        if r == last:
            (ready,) = line.keep(out_weight)
            out_across = chip_swap(ready)
            out_beside = core_swap(ready)
        far.append(project(1, (r,), *far_slots[-2:]))
        attended.append(attend(r))

    middles, seconds, pairs = [], [], []
    acts, pres, feeds, feed_grads = [], [], [], []
    for r in each:
        if r == 0:
            (out_far,) = line.keep(out_across)
            out_slots = [out_weight, out_beside, out_far, core_swap(out_far)]
        one, two = line.split(attended[r][1], attended[r][2])
        attended[r][1:] = [one, two]
        middle, second, pair = line.run(
            partial(middle_kernel, r),
            "middle",
            [],
            [hid, *attended[r], *out_slots, vectors, cots[r]],
            [shape((block, width), F32), full, shape((2, block, width))],
        )
        middles.append(middle)
        seconds.append(second)
        pairs.append(chip_swap(pair))
        out, grad = feed(second, cots[r])
        feeds.append([out])
        feed_grads.append([grad])
    for r in each:
        out, grad = feed(pairs[r])
        feeds[r].append(out)
        feed_grads[r].append(chip_swap(grad))

    grad_middles, grad_branches, head_grads, norm_sums = [], [], [], []

    def middle_back(r):
        own, *across = feed_grads[r]
        grad_middle, grad_branch, *parts, sums = line.run(
            partial(middle_back_kernel, len(across)),
            "middle_back",
            [],
            [own, *across, middles[r], cots[r], vectors, *out_slots],
            [shape((block, width), F32), full]
            + [shape((local, block))] * 2
            + [shape((2, local, block)), shape((8, width), F32)],
        )
        grad_middles.append(grad_middle)
        grad_branches.append(grad_branch)
        head_grads.append([parts[0], parts[1], chip_swap(parts[2])])
        norm_sums.append(sums)

    own_sums, passed_sums, own_bias, passed_bias = line.run(
        partial(feed_weights_kernel, 2 * rows),
        "feed_weights",
        [],
        [*seconds, *cots, *pairs, *acts, *pres],
        [
            shape((2, units, width)),
            shape((2, units, width)),
            shape((1, units), F32),
            shape((8, units), F32),
        ],
        [pltpu.VMEM((2 * units, width), F32), pltpu.VMEM((width, 2 * units), F32)],
        vmem=22,
    )
    for r in range(last):
        middle_back(r)
    (passed_sums,) = line.keep(passed_sums)
    passed_sums = core_swap(passed_sums)
    passed_bias = core_swap(passed_bias)
    in_bias_sum, *slots = line.run(
        feed_slots_kernel,
        "feed_slots",
        [],
        [own_sums, passed_sums, own_bias, passed_bias],
        [shape((1, units), F32)] + [shape((units // 2, width))] * 4,
    )
    feed_bank = Bank(line, slots, size)
    middle_back(last)
    head_grads[0][1:] = line.split(*head_grads[0][1:])
    blocks_across = [chip_swap(line.keep(feeds[r][1])[0]) for r in range(last)]

    def block_out(r):
        return line.run(
            block_out_kernel,
            "block_out",
            [],
            [feeds[r][0], middles[r], blocks_across[r], vectors],
            [full],
        )[0]

    def attend_back(r, picked, before):
        final = picked[-1] == heads - 1
        some = len(picked)
        made = local if final else some * HEAD_DIM
        grad_proj, *parts = line.run(
            partial(attend_back_kernel, r, picked),
            "attend_back",
            [windows],
            [near, far[r], marks, logs[r], waves, *head_grads[r]]
            + before
            + ([proj_weight] if final else []),
            [shape((3 * made, length))]
            + ([full, full] if final else [])
            + ([full, full] if final and r == last else [])
            + ([shape((2, block, width))] if final and r < last else []),
            [
                pltpu.VMEM((some * KEY_ROWS, length), BF16),
                pltpu.VMEM((some, length, KEY_ROWS), BF16),
                pltpu.VMEM((some * HEAD_DIM, length), BF16),
                pltpu.VMEM((some, length, HEAD_DIM), BF16),
                pltpu.VMEM((some, length, HEAD_DIM), BF16),
                pltpu.VMEM((some * HEAD_DIM, length), BF16),
                pltpu.VMEM((some, length, HEAD_DIM), BF16),
                pltpu.VMEM((some, length, HEAD_DIM), F32),
                pltpu.VMEM((some, length, HEAD_DIM), F32),
                pltpu.VMEM((some * HEAD_DIM, length), F32),
            ],
            vmem=20,
        )
        if not final:
            return [grad_proj]
        projs.append(grad_proj)
        first_grads.append([parts[0], parts[1], *(core_swap(v) for v in parts[2:])])

    projs, first_grads = [], []
    for r in each:
        if r > 0:
            head_grads[r][1:] = line.split(*head_grads[r][1:])
        if r == last:
            feed_bank.advance()
            blocks_out = [block_out(k) for k in range(last)]
            out_parts = line.run(
                partial(out_weight_kernel, rows),
                "out_weight",
                [],
                [*sum(attended, []), *grad_branches],
                [shape((local, width))] * 2 + [shape((2, local, width))],
            )
            out_beside = core_swap(out_parts[2])
            (back,) = line.add([(out_parts[1],), (out_beside, 1)])
            out_sums = [out_parts[0], out_beside, chip_swap(back)]
            blocks_across.append(chip_swap(line.keep(feeds[last][1])[0]))
        attend_back(r, tuple(range(heads)), [])
    grads_in, first_sums = [], []

    def first_back(r):
        own, _, beside, *_ = first_grads[r]
        grad_in, sums = line.run(
            partial(first_back_kernel, r),
            "first_back",
            [],
            [own, beside, first_across_back[r], hid, grad_middles[r], vectors],
            [shape((block, width), F32), shape((8, width), F32)],
        )
        grads_in.append(grad_in)
        first_sums.append(sums)

    *slots, proj_bias_sum = line.run(
        partial(project_weights_kernel, rows),
        "project_weights",
        [],
        [*projs, first, first_beside, *far_slots, *out_sums],
        [shape((local, width))] * 4 + [shape((8, width), F32)],
        [pltpu.VMEM((4 * local, width), F32)],
        vmem=10,
    )
    head_bank = Bank(line, slots, size)
    first_across_back = []
    for r in each:
        far_part = [(first_grads[r][2], 1)] if r < last else [(first_grads[r][3],)]
        (back,) = line.add([(first_grads[r][1],), *far_part])
        first_across_back.append(chip_swap(back))
    blocks_out.append(block_out(last))
    blocks_out = jnp.stack(blocks_out, axis=1)
    while not feed_bank.done:
        feed_bank.advance()
    head_bank.advance()
    for r in each:
        first_back(r)
    input_grad = jnp.stack(grads_in, axis=1)
    (small,) = line.run(
        lambda *refs: small_kernel(refs[:rows], refs[rows : 2 * rows], refs[2 * rows]),
        "small",
        [],
        [*first_sums, *norm_sums],
        [shape((8, width), F32)],
    )
    (small,) = line.add([(small,), (core_swap(small),)])
    (small,) = line.run(
        small_extra_kernel,
        "small_extra",
        [],
        [small, chip_swap(small), in_bias_sum, proj_bias_sum],
        [shape((8, width), F32)],
    )
    while not head_bank.done:
        head_bank.advance()
    bit = 1
    while 2 * bit < size:
        (small,) = line.add([(small,), (swap(small, "dp", size, bit),)])
        bit *= 2
    *lines, grad_proj_bias = line.run(
        finish_small_kernel,
        "finish_small",
        [],
        [small, swap(small, "dp", size, bit)],
        [shape((width,), F32)] * 7 + [shape((3, local), F32)],
        [pltpu.VMEM((8, width), F32)],
    )
    grad_down_weight, grad_in_weight = line.run(
        finish_kernel,
        "finish",
        [],
        feed_bank.slots,
        [shape((units, width), F32), shape((width, units), F32)],
    )
    grad_qkv_weight, grad_out_weight = line.run(
        finish_project_kernel,
        "finish_project",
        [],
        head_bank.slots,
        [shape((3 * local, width), F32), shape((local, width), F32)],
        [pltpu.VMEM((4 * local, width), F32)],
    )
    grad_qkv_weight = jnp.transpose(grad_qkv_weight.reshape(3, local, width), (0, 2, 1))
    return (
        blocks_out,
        input_grad,
        lines[0],
        lines[1],
        grad_qkv_weight,
        grad_proj_bias,
        grad_out_weight,
        lines[5],
        lines[2],
        lines[3],
        grad_in_weight,
        lines[6],
        grad_down_weight,
        lines[4],
    )


def solution(mesh):
    sharded = P("tp", "dp", None)
    return jax.shard_map(
        partial(on_device, mesh.shape["dp"]),
        mesh=mesh,
        in_specs=(
            sharded,
            P("dp", None),
            sharded,
            P(),
            P(),
            P(None, None, "tp"),
            P(None, "tp"),
            P("tp", None),
            P(),
            P(),
            P(),
            P(None, "tp"),
            P("tp"),
            P("tp", None),
            P(),
        ),
        out_specs=(
            sharded,
            sharded,
            P(),
            P(),
            P(None, None, "tp"),
            P(None, "tp"),
            P("tp", None),
            P(),
            P(),
            P(),
            P(None, "tp"),
            P("tp"),
            P("tp", None),
            P(),
        ),
        check_vma=False,
    )
```

```python
from functools import partial

import jax
import jax.numpy as jnp
import numpy as np
from jax import lax
from jax.experimental import pallas as pl
from jax.experimental.pallas import tpu as pltpu
from jax.sharding import PartitionSpec as P

HEAD_DIM = 64
HALF = HEAD_DIM // 2
KEY_ROWS = 128
EPSILON = 1e-05
APART = -1e30
F32 = jnp.float32
BF16 = jnp.bfloat16

NN = (((1,), (0,)), ((), ()))
NT = (((1,), (1,)), ((), ()))
TN = (((0,), (0,)), ((), ()))


def dot(a, b, dims=NN):
    return lax.dot_general(a, b, dims, preferred_element_type=F32)


def shape(dims, dtype=BF16):
    return jax.ShapeDtypeStruct(dims, dtype)


class Line:
    def __init__(self):
        self.tile = None

    def run(
        self, body, name, scalars, arrays, outs, scratch=(), vmem=8, inputs=None, numbers=(), places=None
    ):
        before = [] if self.tile is None else [self.tile]
        count, extra, made = len(scalars) + len(arrays), len(before), len(outs)
        made += len(numbers)

        def whole(*refs):
            tile = refs[count + extra + made]
            tile[...] = jnp.zeros_like(tile)
            body(
                *refs[:count],
                *refs[count + extra : count + extra + made],
                *refs[count + extra + made + 1 :],
            )

        vector = pl.BlockSpec(memory_space=pltpu.VMEM)
        scalar = pl.BlockSpec(memory_space=pltpu.SMEM)
        *results, self.tile = pl.pallas_call(
            whole,
            out_shape=(*numbers, *outs, shape((8, 128), F32)),
            in_specs=[scalar] * len(scalars)
            + (inputs or [vector] * len(arrays))
            + [vector] * extra,
            out_specs=(scalar,) * len(numbers)
            + (tuple(places) if places else (vector,) * len(outs))
            + (vector,),
            scratch_shapes=list(scratch),
            compiler_params=pltpu.CompilerParams(vmem_limit_bytes=vmem * 1024 * 1024),
            cost_estimate=pl.CostEstimate(flops=1, bytes_accessed=1, transcendentals=0),
            name=name,
        )(*scalars, *arrays, *before)
        return results

    def keep(self, *arrays):
        def body(*refs):
            for k in range(len(arrays)):
                refs[len(arrays) + k][...] = refs[k][...]

        return self.run(body, "keep", [], arrays, [shape(v.shape, v.dtype) for v in arrays])

    def split(self, near, pair):
        def body(near, pair, one, two):
            one[...] = pair[0]
            two[0] = near[...]
            two[1] = pair[1]

        made = [shape(near.shape), shape((2, *near.shape))]
        one, two = self.run(body, "split", [], [near, pair], made)
        return [one, core_swap(two)]

    def merge(self, one, two, cuts):
        def body(one, two, *outs):
            total = one[...].astype(F32) + two[...].astype(F32)
            size = total.shape[0] // cuts
            for k, out in enumerate(outs):
                out[...] = total[k * size : (k + 1) * size].astype(out.dtype)

        made = [shape((one.shape[0] // cuts, *one.shape[1:]))] * cuts
        return self.run(body, "merge", [], [one, two], made)

    def join(self, *arrays):
        def body(*refs):
            for k in range(len(arrays)):
                refs[len(arrays)][k] = refs[k][...]

        first = arrays[0]
        made = [shape((len(arrays), *first.shape), first.dtype)]
        return self.run(body, "join", [], arrays, made, vmem=8)[0]

    def add_rows(self, ones, twos):
        count = len(ones)

        def body(*refs):
            for r in range(count):
                total = refs[r][...].astype(F32) + refs[count + r][1].astype(F32)
                refs[2 * count][r] = total.astype(BF16)

        made = [shape((count, *ones[0].shape))]
        return self.run(body, "add_rows", [], [*ones, *twos], made)[0]

    def add_pair(self, one, two):
        def body(a, b, c, d, out):
            out[0] = (a[...].astype(F32) + b[...].astype(F32)).astype(out.dtype)
            out[1] = (c[...].astype(F32) + d[...].astype(F32)).astype(out.dtype)

        made = [shape((2, *one[0].shape), one[0].dtype)]
        return self.run(body, "add_pair", [], [*one, *two], made)[0]

    def add(self, *sums):
        arrays = [term[0] for terms in sums for term in terms]
        parts = [[term[1:] for term in terms] for terms in sums]
        outs = []
        for terms in sums:
            first = terms[0][0]
            outs.append(shape(first.shape[len(terms[0]) - 1 :], first.dtype))

        def body(*refs):
            at = 0
            for k, terms in enumerate(parts):
                total = None
                for index in terms:
                    value = refs[at][index[0]] if index else refs[at][...]
                    value = value.astype(F32)
                    total = value if total is None else total + value
                    at += 1
                out = refs[len(arrays) + k]
                out[...] = total.astype(out.dtype)

        return self.run(body, "add", [], arrays, outs)


def normalize(values):
    average = jnp.mean(values, axis=-1, keepdims=True)
    centered = values - average
    variance = jnp.mean(centered * centered, axis=-1, keepdims=True)
    inverse = lax.rsqrt(variance + EPSILON)
    return centered * inverse, inverse


def normalize_back(gradient, scaled, inverse, gain):
    grad_scaled = gradient * gain
    return inverse * (
        grad_scaled
        - jnp.mean(grad_scaled, axis=-1, keepdims=True)
        - scaled * jnp.mean(grad_scaled * scaled, axis=-1, keepdims=True)
    )


def where_am_i():
    me = lax.axis_index("tp")
    return me, me // 2, lax.axis_index("dp") & 3


def first_norm_kernel(rows, width, hid, *refs):
    lines, (w_in, w_out, vectors, first, alone, joined) = refs[:7], refs[7:13]
    lands, sems = refs[13:20], refs[20]
    copies = [
        pltpu.make_async_copy(line, land, sems.at[k])
        for k, (line, land) in enumerate(zip(lines, lands))
    ]
    sends = [
        pltpu.make_async_copy(w_in, joined.at[0], sems.at[7]),
        pltpu.make_async_copy(w_out, joined.at[1], sems.at[8]),
    ]
    for copy in copies + sends:
        copy.start()
    normed = []
    for r in range(rows):
        values = hid[:, r * width : (r + 1) * width].astype(F32)
        normed.append(normalize(values)[0])
    for copy in copies:
        copy.wait()
    for k, land in enumerate(lands):
        vectors[k : k + 1, :] = land[...].astype(F32).reshape(1, width)
    vectors[7:8, :] = jnp.zeros((1, width), F32)
    for r in range(rows):
        low = (normed[r] * vectors[0:1, :] + vectors[1:2, :]).astype(BF16)
        first[r] = low
        if r == 0:
            alone[...] = low
    for copy in sends:
        copy.wait()


def table_kernel(block, segments, rates, bias, windows, marks, waves, column):
    rows, length = segments.shape
    ids = lax.broadcasted_iota(jnp.int32, (16, length), 0)
    spots = lax.broadcasted_iota(jnp.int32, (1, length), 1)
    for r in range(rows):
        row = segments[r : r + 1, :]
        same = row == ids
        before = jnp.sum((row < ids).astype(F32), axis=1, keepdims=True)
        begins = jnp.sum(jnp.where(same, before, 0.0), axis=0, keepdims=True)
        ends = jnp.sum((row <= ids).astype(F32), axis=1, keepdims=True)
        closes = jnp.sum(jnp.where(same, ends, 0.0), axis=0, keepdims=True)
        marks[r, 0] = same.astype(F32).astype(BF16)
        marks[r, 1] = jnp.where(same | (ids >= 8), 0.0, APART).astype(BF16)
        angles = rates[...] * (spots.astype(F32) - begins)
        waves[r, 0] = jnp.cos(angles)
        waves[r, 1] = jnp.sin(angles)
        blocks = length // block
        for q in range(blocks):
            inside = slice(q * block, (q + 1) * block)
            least = jnp.min(begins[:, inside]).astype(jnp.int32)
            past = jnp.max(closes[:, inside]).astype(jnp.int32)
            start = (least // 128) * 128
            count = (past - start + block - 1) // block
            windows[2 * blocks * r + q] = jnp.minimum(start, length - count * block)
            windows[2 * blocks * r + blocks + q] = count
    local = bias.shape[1]
    tall = jnp.concatenate([bias[...].astype(F32), jnp.zeros((5, local), F32)], axis=0)
    tall = jnp.transpose(tall)
    for c in range(3):
        column[c * local : (c + 1) * local, :] = tall[:, c : c + 1]


def split_kernel(width, whole, *outs):
    for r, out in enumerate(outs):
        out[...] = whole[:, r * width : (r + 1) * width]


def project_kernel(far, picked, one, two, weight, bias, waves, out):
    block = two.shape[-2]
    local = weight.shape[0] // 3
    me, chip, _ = where_am_i()
    half = chip ^ far
    for at, r in enumerate(picked):
        for k, tokens in enumerate((one, two)):
            spot = pl.multiple_of(((me & 1) ^ k) * block, block)
            span = pl.ds(spot, block)
            table = pl.ds(pl.multiple_of(half * (2 * block) + spot, block), block)
            values = tokens[at] if len(tokens.shape) == 3 else tokens[...]
            turned = dot(weight[...], values, NT) + bias[...]
            cs = waves[r, 0, :, table]
            sn = waves[r, 1, :, table]
            for c in range(2):
                for base in range(c * local, (c + 1) * local, HEAD_DIM):
                    a = turned[base : base + HALF]
                    b = turned[base + HALF : base + HEAD_DIM]
                    new_a = a * cs - b * sn
                    new_b = b * cs + a * sn
                    if c == 0:
                        new_a = new_a * HEAD_DIM**-0.5
                        new_b = new_b * HEAD_DIM**-0.5
                    out[at, base : base + HALF, span] = new_a.astype(BF16)
                    out[at, base + HALF : base + HEAD_DIM, span] = new_b.astype(BF16)
            out[at, 2 * local :, span] = turned[2 * local :].astype(BF16)


def turn_over(values):
    return jnp.transpose(values.astype(F32)).astype(BF16)


def sides(r, near, far):
    chip = where_am_i()[1]
    width = near.shape[-1]
    return [
        (source, pl.ds(pl.multiple_of(at, width), width))
        for source, at in ((near.at[r], chip * width), (far.at[0], (1 - chip) * width))
    ]


def lay_out(r, picked, near, far, marked, queries, keys):
    mine = marked[r, 0]
    width = near.shape[-1]
    local = near.shape[1] // 3
    marks = mine.shape[0]
    for source, span in sides(r, near, far):
        for at, h in enumerate(picked):
            queries[at * KEY_ROWS : at * KEY_ROWS + HEAD_DIM, span] = source[
                h * HEAD_DIM : (h + 1) * HEAD_DIM, :
            ]
            column = jnp.concatenate(
                [
                    source[local + h * HEAD_DIM : local + (h + 1) * HEAD_DIM, :],
                    marked[r, 1, :, span],
                    jnp.zeros((KEY_ROWS - HEAD_DIM - marks, width), BF16),
                ],
                axis=0,
            )
            keys[at, span, :] = turn_over(column)
    for at in range(len(picked)):
        base = at * KEY_ROWS + HEAD_DIM
        queries[base : base + marks, :] = mine
        queries[base + marks : (at + 1) * KEY_ROWS, :] = jnp.zeros(
            (KEY_ROWS - HEAD_DIM - marks, queries.shape[1]), BF16
        )


def attend_kernel(r, windows, near, far, marked, *rest):
    outs, (log_norm, queries, keys, values, attended) = rest[:3], rest[3:]
    block = near.shape[-1] // 2
    local = near.shape[1] // 3
    heads = local // HEAD_DIM
    me = where_am_i()[0]
    lay_out(r, range(heads), near, far, marked, queries, keys)
    for source, span in sides(r, near, far):
        values[:, span] = source[2 * local :, :]

    @pl.loop(0, 4)
    def _(quarter):
        span = pl.ds(pl.multiple_of(quarter * block, block), block)
        start = pl.multiple_of(windows[8 * r + quarter], 128)
        count = windows[8 * r + 4 + quarter]

        def work(blocks):
            window = pl.ds(start, blocks * block)

            @pl.loop(0, heads)
            def _(h):
                part = pl.ds(pl.multiple_of(h * HEAD_DIM, HEAD_DIM), HEAD_DIM)
                rows = pl.ds(pl.multiple_of(h * KEY_ROWS, KEY_ROWS), KEY_ROWS)
                scores = dot(keys[h, window, :], queries[rows, span])
                peak = jnp.max(scores, axis=0, keepdims=True)
                weights = jnp.exp(scores - peak)
                total = jnp.sum(weights, axis=0, keepdims=True)
                out = dot(values[part, window], weights.astype(BF16))
                attended[part, span] = (out * (1.0 / total)).astype(BF16)
                log_norm[pl.ds(h, 1), span] = peak + jnp.log(total)

        for blocks in range(1, 5):
            pl.when(count == blocks)(partial(work, blocks))

    for s, out in enumerate((outs[0], outs[1], outs[2].at[0], outs[2].at[1])):
        out[...] = attended[:, pl.ds(pl.multiple_of((me ^ s) * block, block), block)]


def attend_back_kernel(r, picked, windows, near, far, marked, log_norm, waves, *rest):
    grads = (rest[0], rest[2].at[0], rest[1], rest[2].at[1])
    scratch, rest = rest[-8:], rest[3:-8]
    queries, keys, key_rows, value_cols, grad_rows, dk, dv, dq = scratch
    block = near.shape[-1] // 2
    local = near.shape[1] // 3
    heads = local // HEAD_DIM
    me = where_am_i()[0]
    if len(rest) == 1:
        before, weight, grad_proj, partials = None, None, rest[0], ()
    else:
        before = rest[0] if rest[0].shape[0] < rest[1].shape[0] else None
        weight, grad_proj, own, across, *sent = rest[1:] if before is not None else rest
        if len(sent) == 1:
            sent = (sent[0].at[0], sent[0].at[1])
        partials = (own, sent[0], across, sent[1])
    stride = grad_proj.shape[0] // 3
    first = picked[0] if weight is None else 0
    lay_out(r, picked, near, far, marked, queries, keys)
    for source, span in sides(r, near, far):
        for at, h in enumerate(picked):
            part = slice(at * HEAD_DIM, (at + 1) * HEAD_DIM)
            key_rows[part, span] = source[local + h * HEAD_DIM : local + (h + 1) * HEAD_DIM, :]
            value_cols[at, span, :] = turn_over(
                source[2 * local + h * HEAD_DIM : 2 * local + (h + 1) * HEAD_DIM, :]
            )
    for s, grad in enumerate(grads):
        span = pl.ds(pl.multiple_of((me ^ s) * block, block), block)
        for at, h in enumerate(picked):
            rows = grad[h * HEAD_DIM : (h + 1) * HEAD_DIM, :]
            grad_rows[at * HEAD_DIM : (at + 1) * HEAD_DIM, span] = rows
    dk[...] = jnp.zeros_like(dk)
    dv[...] = jnp.zeros_like(dv)

    @pl.loop(0, 4)
    def _(quarter):
        span = pl.ds(pl.multiple_of(quarter * block, block), block)
        start = pl.multiple_of(windows[8 * r + quarter], 128)
        count = windows[8 * r + 4 + quarter]

        def work(blocks):
            window = pl.ds(start, blocks * block)
            for at, h in enumerate(picked):
                part = slice(at * HEAD_DIM, (at + 1) * HEAD_DIM)
                scores = dot(
                    keys[at, window, :], queries[at * KEY_ROWS : (at + 1) * KEY_ROWS, span]
                )
                probs = jnp.exp(scores - log_norm[h : h + 1, span])
                grad_probs = dot(value_cols[at, window, :], grad_rows[part, span])
                inner = jnp.sum(probs * grad_probs, axis=0, keepdims=True)
                grad_scores = (probs * (grad_probs - inner)).astype(BF16)
                dv[part, window] += dot(grad_rows[part, span], probs.astype(BF16), NT)
                asked = slice(at * KEY_ROWS, at * KEY_ROWS + HEAD_DIM)
                dk[part, window] += dot(queries[asked, span], grad_scores, NT)
                dq[part, span] = dot(key_rows[part, window], grad_scores)

        for blocks in range(1, 5):
            pl.when(count == blocks)(partial(work, blocks))

    cs = waves[r, 0]
    sn = waves[r, 1]

    def turn_back(rows, base):
        a = rows[:HALF]
        b = rows[HALF:]
        grad_proj[base : base + HALF, :] = (a * cs + b * sn).astype(BF16)
        grad_proj[base + HALF : base + HEAD_DIM, :] = (b * cs - a * sn).astype(BF16)

    for at, h in enumerate(picked):
        base = (h - first) * HEAD_DIM
        turn_back(dq[at * HEAD_DIM : (at + 1) * HEAD_DIM, :] * HEAD_DIM**-0.5, base)
        part = slice(at * HEAD_DIM, (at + 1) * HEAD_DIM)
        turn_back(dk[part, :], stride + base)
        base += 2 * stride
        grad_proj[base : base + HEAD_DIM, :] = dv[part, :].astype(BF16)
    if before is not None:
        had = before.shape[0] // 3
        for c in range(3):
            grad_proj[c * stride : c * stride + had, :] = before[c * had : (c + 1) * had, :]
    for s, partial_out in enumerate(partials):
        span = pl.ds(pl.multiple_of((me ^ s) * block, block), block)
        partial_out[...] = dot(grad_proj[:, span], weight[...], TN).astype(BF16)


def four(parts):
    return (parts[0], parts[2].at[0], parts[1], parts[2].at[1])


def middle_kernel(row, hid, *rest):
    attended, weights = four(rest[:3]), rest[3:7]
    vectors, cot, middle, second, pair = rest[7:12]
    width = vectors.shape[1]
    branch = vectors[2:3, :]
    for a, w in zip(attended, weights):
        branch = branch + dot(a[...], w[...], TN)
    values = hid[:, row * width : (row + 1) * width].astype(F32) + branch
    middle[...] = values
    scaled, _ = normalize(values)
    low = (scaled * vectors[3:4, :] + vectors[4:5, :]).astype(BF16)
    second[...] = low
    pair[0] = low
    pair[1] = cot[...]


def gelu_parts(h):
    size = jnp.abs(h)
    t = 1.0 / (1.0 + size * (0.3275911 * 0.5**0.5))
    density = jnp.exp(h * h * -0.5)
    poly = t * (
        0.254829592
        + t * (-0.284496736 + t * (1.421413741 + t * (-1.453152027 + t * 1.061405429)))
    )
    tail = 0.5 * poly * density
    below = jnp.where(h < 0, tail, 1.0 - tail)
    return below, density * 0.3989422804014327


def feed_kernel(second, cot, w_in, w_out, vectors, passed, passed_vectors, act, grad_pre, *outs):
    if cot is None:
        second, cot = second.at[0], second.at[1]
    units = w_in.shape[1]
    width = w_in.shape[0]
    step = 256
    tokens = second[...]
    portion = cot[...]
    for side, lines in enumerate((vectors, passed_vectors)):
        for u in range(0, units, step):
            cols = slice(u, u + step)
            spot = slice(side * units + u, side * units + u + step)
            into = passed[:width, cols] if side else w_in[:, cols]
            down = passed[width + u : width + u + step, :] if side else w_out[cols, :]
            pre = dot(tokens, into) + lines[6:7, cols]
            below, density = gelu_parts(pre)
            act[:, spot] = (pre * below).astype(BF16)
            grad_act = dot(portion, down, NT)
            grad_pre[:, spot] = (grad_act * (below + pre * density)).astype(BF16)
    out = dot(act[:, :units], w_out[...]) + dot(act[:, units:], passed[width:, :])
    grad = dot(grad_pre[:, :units], w_in[...], NT) + dot(
        grad_pre[:, units:], passed[:width, :], NT
    )
    half = out.shape[0] // 2
    outs[0][...] = out.astype(BF16)
    low = grad.astype(BF16)
    if len(outs) == 2:
        outs[1][...] = low
    else:
        outs[1][...] = low[:half]
        outs[2][...] = low[half:]


def feed_weights_kernel(count, *refs):
    near = count // 2
    seconds, cots, pairs = refs[:near], refs[near:count], refs[count : count + near]
    seconds = [*seconds, *(pair.at[0] for pair in pairs)]
    cots = [*cots, *(pair.at[1] for pair in pairs)]
    refs = refs[count + near :]
    acts, pres = refs[:count], refs[count : 2 * count]
    own, passed, own_bias, passed_bias, down, up = refs[2 * count :]
    units = own.shape[1]
    for k in range(count):
        pre = pres[k][...]
        part_down = dot(acts[k][...], cots[k][...], TN)
        part_up = dot(seconds[k][...], pre, TN)
        sums = jnp.sum(pre.astype(F32), axis=0, keepdims=True)
        if k == 0:
            down[...] = part_down
            up[...] = part_up
            added = sums
        else:
            down[...] += part_down
            up[...] += part_up
            added += sums
    own_bias[...] = added[:, :units]
    passed_bias[...] = jnp.broadcast_to(added[:, units:], passed_bias.shape)
    own[0] = down[:units, :].astype(BF16)
    own[1] = up[:, :units].astype(BF16)
    passed[0] = down[units:, :].astype(BF16)
    passed[1] = up[:, units:].astype(BF16)


def feed_slots_kernel(own, passed, own_bias, passed_bias, bias, *outs):
    piece = outs[0].shape[0] // 2
    spot = where_am_i()[2]
    bias[...] = own_bias[...] + passed_bias[0:1, :]
    for s, out in enumerate(outs):
        span = pl.ds(pl.multiple_of((spot ^ s) * piece, piece), piece)
        for bank in range(2):
            total = own[bank, span, :].astype(F32) + passed[bank, span, :].astype(F32)
            out[bank * piece : (bank + 1) * piece, :] = total.astype(BF16)


def middle_back_kernel(chips, own, *rest):
    chip, rest = rest[:chips], rest[chips:]
    middle, cot, vectors = rest[:3]
    weights, outs = rest[3:7], rest[7:]
    grad_middle, grad_branch, sums = outs[0], outs[1], outs[5]
    heads = (outs[2], outs[3], outs[4].at[0], outs[4].at[1])
    across = jnp.concatenate([part[...] for part in chip], axis=0) if chips > 1 else chip[0][...]
    grad_second = own[...].astype(F32) + across.astype(F32)
    scaled, inverse = normalize(middle[...])
    grad_out = cot[...].astype(F32)
    total = grad_out + normalize_back(grad_second, scaled, inverse, vectors[3:4, :])
    low = total.astype(BF16)
    grad_middle[...] = total
    grad_branch[...] = low
    for w, out in zip(weights, heads):
        out[...] = dot(w[...], low, NT).astype(BF16)
    sums[0:1, :] = jnp.sum(grad_second * scaled, axis=0, keepdims=True)
    sums[1:2, :] = jnp.sum(grad_second, axis=0, keepdims=True)
    sums[2:3, :] = jnp.sum(grad_out, axis=0, keepdims=True)
    sums[3:4, :] = jnp.sum(low.astype(F32), axis=0, keepdims=True)
    sums[4:, :] = jnp.zeros((4, sums.shape[1]), F32)


def out_weight_kernel(rows, *refs):
    attended, grads, outs = refs[: 3 * rows], refs[3 * rows : 4 * rows], refs[4 * rows :]
    attended = [four(attended[3 * r : 3 * r + 3]) for r in range(rows)]
    own, across, sent = outs
    for s, out in enumerate((own, sent.at[0], across, sent.at[1])):
        total = dot(attended[0][s][...], grads[0][...])
        for r in range(1, rows):
            total = total + dot(attended[r][s][...], grads[r][...])
        out[...] = total.astype(BF16)


def project_weights_kernel(rows, *refs):
    projs, near, far = refs[:rows], refs[rows : rows + 2], refs[rows + 2 : 3 * rows + 2]
    refs = refs[3 * rows + 2 :]
    own, swapped, chip = refs[:3]
    outs, (bias, total) = refs[3:7], refs[7:]
    block = near[0].shape[1]
    me, _, spot = where_am_i()
    size = projs[0].shape[0]
    local = size // 3
    ones = jnp.ones((8, projs[0].shape[1]), BF16)
    bias[...] = jnp.zeros_like(bias)
    for c in range(3):
        part = slice(c * local, (c + 1) * local)
        sums = dot(ones, projs[0][part, :], NT)
        for r in range(1, rows):
            sums += dot(ones, projs[r][part, :], NT)
        bias[:, 256 * c : 256 * c + local] = sums
    for r in range(rows):
        for s in range(4):
            span = pl.ds(pl.multiple_of((me ^ s) * block, block), block)
            tokens = near[s][r] if s < 2 else far[2 * r + s - 2][...]
            product = dot(projs[r][:, span], tokens)
            if r + s == 0:
                total[:size, :] = product
            else:
                total[:size, :] += product
    total[size:, :] = own[...].astype(F32) + swapped[0].astype(F32) + chip[...].astype(F32)
    piece = outs[0].shape[0]
    for s, out in enumerate(outs):
        at = pl.multiple_of((spot ^ s) * piece, piece)
        out[...] = total[pl.ds(at, piece), :].astype(BF16)


def finish_kernel(*refs):
    spot = where_am_i()[2]
    slots, outs = refs[:4], refs[4:]
    for s, slot in enumerate(slots):
        piece = slot.shape[0] // 2
        span = pl.ds(pl.multiple_of((spot ^ s) * piece, piece), piece)
        for k, out in enumerate(outs):
            out[span, :] = slot[k * piece : (k + 1) * piece, :].astype(F32)


def finish_project_kernel(*refs):
    spot = where_am_i()[2]
    slots, (big, small, total) = refs[:4], refs[4:]
    for s, slot in enumerate(slots):
        piece = slot.shape[0]
        at = pl.multiple_of((spot ^ s) * piece, piece)
        total[pl.ds(at, piece), :] = slot[...].astype(F32)
    size = big.shape[0]
    big[...] = total[:size, :]
    small[...] = total[size:, :]


def first_back_kernel(row, own, beside, chip, hid, grad_middle, vectors, grad_in, sums):
    width = vectors.shape[1]
    swapped = beside[0] if len(beside.shape) == 3 else beside[...]
    grad_first = own[...].astype(F32) + swapped.astype(F32) + chip[...].astype(F32)
    scaled, inverse = normalize(hid[:, row * width : (row + 1) * width].astype(F32))
    grad_in[...] = grad_middle[...] + normalize_back(grad_first, scaled, inverse, vectors[0:1, :])
    sums[0:1, :] = jnp.sum(grad_first * scaled, axis=0, keepdims=True)
    sums[1:2, :] = jnp.sum(grad_first, axis=0, keepdims=True)
    sums[2:, :] = jnp.zeros((6, width), F32)


def small_kernel(firsts, middles, out):
    rows = len(firsts)
    out[...] = jnp.zeros_like(out)
    out[0:2, :] = sum(ref[0:2, :] for ref in firsts)
    out[2:6, :] = sum(ref[0:4, :] for ref in middles)


def small_extra_kernel(one, two, in_bias, proj_bias, out):
    out[...] = one[...] + two[...]
    out[6:7, :] = in_bias[...]
    out[7:8, :] = proj_bias[0:1, :]


def finish_small_kernel(one, two, *outs):
    *lines, proj_bias, total = outs
    total[...] = one[...] + two[...]
    width = total.shape[1]
    for k, line in enumerate(lines):
        line[...] = total[k : k + 1, :].reshape(width)
    local = proj_bias.shape[1]
    for c in range(3):
        proj_bias[c : c + 1, :] = total[7:8, 256 * c : 256 * c + local]


def block_out_kernel(own, middle, across, vectors, out):
    total = own[...].astype(F32) + across[...].astype(F32)
    out[...] = (middle[...] + (total + vectors[5:6, :])).astype(BF16)


def swap(values, axis, size, bit):
    return lax.ppermute(values, axis, [(i, i ^ bit) for i in range(size)])


def core_swap(values):
    return swap(values, "tp", 4, 1)


def chip_swap(values):
    return swap(values, "tp", 4, 2)


class Bank:
    def __init__(self, line, slots, size):
        self.line, self.own, self.size = line, slots[0], size
        self.moved = [swap(slots[s], "dp", size, s) for s in range(1, 4)]
        self.bit = 2

    def advance(self):
        (self.own,) = self.line.add([(self.own,), *((v,) for v in self.moved)])
        self.bit *= 2
        if self.bit < self.size:
            self.moved = [swap(self.own, "dp", self.size, self.bit)]
            return
        self.slots = [self.own] + [swap(self.own, "dp", self.size, s) for s in range(1, 4)]

    @property
    def done(self):
        return self.bit >= self.size


def on_device(
    size,
    hidden_in,
    segment_ids,
    cotangent,
    norm1_gain,
    norm1_bias,
    qkv_weight,
    qkv_bias,
    out_weight,
    out_bias,
    norm2_gain,
    norm2_bias,
    ffn_in_weight,
    ffn_in_bias,
    ffn_out_weight,
    ffn_out_bias,
):
    block, rows, width = hidden_in.shape
    length = segment_ids.shape[1]
    local = qkv_weight.shape[2]
    heads = local // HEAD_DIM
    units = ffn_in_weight.shape[1]
    line = Line()
    each, last = range(rows), rows - 1
    full, half, both = shape((block, width)), shape((block // 2, width)), shape((rows, block, width))
    hid = hidden_in.reshape(block, rows * width)
    cots = cotangent.reshape(block, rows * width)
    vector, anywhere = pl.BlockSpec(memory_space=pltpu.VMEM), pl.BlockSpec(memory_space=pltpu.HBM)
    params = [norm1_gain, norm1_bias, out_bias, norm2_gain, norm2_bias, ffn_out_bias, ffn_in_bias]
    vectors, first, alone, joined = line.run(
        partial(first_norm_kernel, rows, width),
        "first_norm",
        [],
        [hid, *params, ffn_in_weight, ffn_out_weight],
        [shape((8, width), F32), both, full, shape((2, *ffn_in_weight.shape))],
        [pltpu.VMEM((width,), BF16)] * 7 + [pltpu.SemaphoreType.DMA((9,))],
        inputs=[vector] + [anywhere] * 9,
        places=[vector] * 3 + [anywhere],
    )
    first_across = [chip_swap(alone)]
    first_beside = core_swap(first)
    passed = core_swap(joined).reshape(2 * width, -1)
    passed_vectors = core_swap(vectors)

    rates = np.power(10000.0, -2.0 * np.arange(HALF) / HEAD_DIM).astype(np.float32)
    windows, marks, waves, proj_bias = line.run(
        partial(table_kernel, block),
        "tables",
        [],
        [segment_ids, jnp.asarray(rates.reshape(HALF, 1)), qkv_bias],
        [
            shape((rows, 2, 16, length)),
            shape((rows, 2, HALF, length), F32),
            shape((3 * local, 1), F32),
        ],
        numbers=[shape((rows * 2 * (length // block),), jnp.int32)],
    )
    proj_weight = jnp.transpose(qkv_weight, (0, 2, 1)).reshape(3 * local, width)

    def project(far, picked, one, two):
        return line.run(
            partial(project_kernel, far, picked),
            "project",
            [],
            [one, two, proj_weight, proj_bias, waves],
            [shape((len(picked), 3 * local, 2 * block))],
        )[0]

    def attend(r):
        *outs, log_norm = line.run(
            partial(attend_kernel, r),
            "attend",
            [windows],
            [near, far[r], marks],
            [shape((local, block))] * 2
            + [shape((2, local, block)), shape((8, length), F32)],
            [
                pltpu.VMEM((heads * KEY_ROWS, length), BF16),
                pltpu.VMEM((heads, length, KEY_ROWS), BF16),
                pltpu.VMEM((local, length), BF16),
                pltpu.VMEM((local, length), BF16),
            ],
            vmem=14,
        )
        logs.append(log_norm)
        return [outs[0], outs[1], chip_swap(outs[2])]

    def feed(*tokens):
        tokens = list(tokens)

        def body(*refs):
            feed_kernel(*(refs if len(tokens) == 2 else (refs[0], None, *refs[1:])))

        act, pre, *outs = line.run(
            body,
            "feed",
            [],
            tokens + [ffn_in_weight, ffn_out_weight, vectors, passed, passed_vectors],
            [shape((block, 2 * units))] * 2 + [full, full],
            vmem=12,
        )
        acts.append(act)
        pres.append(pre)
        return outs

    def pick(values, r):
        def body(values, out):
            out[...] = values[r]

        return line.run(body, "pick", [], [values], [shape(values.shape[1:])])[0]

    near = project(0, tuple(each), first, first_beside)
    cots = line.run(partial(split_kernel, width), "split", [], [cots], [full] * rows)
    far, far_slots = [], []
    logs, attended = [], []
    for r in each:
        (arrived,) = line.keep(first_across[r])
        far_slots += [arrived, core_swap(arrived)]
        if r < last:
            first_across.append(chip_swap(pick(first, r + 1)))
        if r == last:
            (ready,) = line.keep(out_weight)
            out_across = chip_swap(ready)
            out_beside = core_swap(ready)
        far.append(project(1, (r,), *far_slots[-2:]))
        attended.append(attend(r))

    middles, seconds, pairs = [], [], []
    acts, pres, feeds, feed_grads = [], [], [], []
    for r in each:
        if r == 0:
            (out_far,) = line.keep(out_across)
            out_slots = [out_weight, out_beside, out_far, core_swap(out_far)]
        one, two = line.split(attended[r][1], attended[r][2])
        attended[r][1:] = [one, two]
        middle, second, pair = line.run(
            partial(middle_kernel, r),
            "middle",
            [],
            [hid, *attended[r], *out_slots, vectors, cots[r]],
            [shape((block, width), F32), full, shape((2, block, width))],
        )
        middles.append(middle)
        seconds.append(second)
        pairs.append(chip_swap(pair))
        out, grad = feed(second, cots[r])
        feeds.append([out])
        feed_grads.append([grad])
    for r in each:
        out, grad = feed(pairs[r])
        feeds[r].append(out)
        feed_grads[r].append(chip_swap(grad))

    grad_middles, grad_branches, head_grads, norm_sums = [], [], [], []

    def middle_back(r):
        own, *across = feed_grads[r]
        grad_middle, grad_branch, *parts, sums = line.run(
            partial(middle_back_kernel, len(across)),
            "middle_back",
            [],
            [own, *across, middles[r], cots[r], vectors, *out_slots],
            [shape((block, width), F32), full]
            + [shape((local, block))] * 2
            + [shape((2, local, block)), shape((8, width), F32)],
        )
        grad_middles.append(grad_middle)
        grad_branches.append(grad_branch)
        head_grads.append([parts[0], parts[1], chip_swap(parts[2])])
        norm_sums.append(sums)

    own_sums, passed_sums, own_bias, passed_bias = line.run(
        partial(feed_weights_kernel, 2 * rows),
        "feed_weights",
        [],
        [*seconds, *cots, *pairs, *acts, *pres],
        [
            shape((2, units, width)),
            shape((2, units, width)),
            shape((1, units), F32),
            shape((8, units), F32),
        ],
        [pltpu.VMEM((2 * units, width), F32), pltpu.VMEM((width, 2 * units), F32)],
        vmem=22,
    )
    for r in range(last):
        middle_back(r)
    (passed_sums,) = line.keep(passed_sums)
    passed_sums = core_swap(passed_sums)
    passed_bias = core_swap(passed_bias)
    in_bias_sum, *slots = line.run(
        feed_slots_kernel,
        "feed_slots",
        [],
        [own_sums, passed_sums, own_bias, passed_bias],
        [shape((1, units), F32)] + [shape((units // 2, width))] * 4,
    )
    feed_bank = Bank(line, slots, size)
    middle_back(last)
    head_grads[0][1:] = line.split(*head_grads[0][1:])
    blocks_across = [chip_swap(line.keep(feeds[r][1])[0]) for r in range(last)]

    def block_out(r):
        return line.run(
            block_out_kernel,
            "block_out",
            [],
            [feeds[r][0], middles[r], blocks_across[r], vectors],
            [full],
        )[0]

    def attend_back(r, picked, before):
        final = picked[-1] == heads - 1
        some = len(picked)
        made = local if final else some * HEAD_DIM
        grad_proj, *parts = line.run(
            partial(attend_back_kernel, r, picked),
            "attend_back",
            [windows],
            [near, far[r], marks, logs[r], waves, *head_grads[r]]
            + before
            + ([proj_weight] if final else []),
            [shape((3 * made, length))]
            + ([full, full] if final else [])
            + ([full, full] if final and r == last else [])
            + ([shape((2, block, width))] if final and r < last else []),
            [
                pltpu.VMEM((some * KEY_ROWS, length), BF16),
                pltpu.VMEM((some, length, KEY_ROWS), BF16),
                pltpu.VMEM((some * HEAD_DIM, length), BF16),
                pltpu.VMEM((some, length, HEAD_DIM), BF16),
                pltpu.VMEM((some * HEAD_DIM, length), BF16),
                pltpu.VMEM((some * HEAD_DIM, length), F32),
                pltpu.VMEM((some * HEAD_DIM, length), F32),
                pltpu.VMEM((some * HEAD_DIM, length), F32),
            ],
            vmem=20,
        )
        if not final:
            return [grad_proj]
        projs.append(grad_proj)
        first_grads.append([parts[0], parts[1], *(core_swap(v) for v in parts[2:])])

    projs, first_grads = [], []
    for r in each:
        if r > 0:
            head_grads[r][1:] = line.split(*head_grads[r][1:])
        if r == last:
            feed_bank.advance()
            blocks_out = [block_out(k) for k in range(last)]
            out_parts = line.run(
                partial(out_weight_kernel, rows),
                "out_weight",
                [],
                [*sum(attended, []), *grad_branches],
                [shape((local, width))] * 2 + [shape((2, local, width))],
            )
            out_beside = core_swap(out_parts[2])
            (back,) = line.add([(out_parts[1],), (out_beside, 1)])
            out_sums = [out_parts[0], out_beside, chip_swap(back)]
            blocks_across.append(chip_swap(line.keep(feeds[last][1])[0]))
        attend_back(r, tuple(range(heads)), [])
    grads_in, first_sums = [], []

    def first_back(r):
        own, _, beside, *_ = first_grads[r]
        grad_in, sums = line.run(
            partial(first_back_kernel, r),
            "first_back",
            [],
            [own, beside, first_across_back[r], hid, grad_middles[r], vectors],
            [shape((block, width), F32), shape((8, width), F32)],
        )
        grads_in.append(grad_in)
        first_sums.append(sums)

    *slots, proj_bias_sum = line.run(
        partial(project_weights_kernel, rows),
        "project_weights",
        [],
        [*projs, first, first_beside, *far_slots, *out_sums],
        [shape((local, width))] * 4 + [shape((8, width), F32)],
        [pltpu.VMEM((4 * local, width), F32)],
        vmem=10,
    )
    head_bank = Bank(line, slots, size)
    first_across_back = []
    for r in each:
        far_part = [(first_grads[r][2], 1)] if r < last else [(first_grads[r][3],)]
        (back,) = line.add([(first_grads[r][1],), *far_part])
        first_across_back.append(chip_swap(back))
    blocks_out.append(block_out(last))
    blocks_out = jnp.stack(blocks_out, axis=1)
    while not feed_bank.done:
        feed_bank.advance()
    head_bank.advance()
    for r in each:
        first_back(r)
    input_grad = jnp.stack(grads_in, axis=1)
    (small,) = line.run(
        lambda *refs: small_kernel(refs[:rows], refs[rows : 2 * rows], refs[2 * rows]),
        "small",
        [],
        [*first_sums, *norm_sums],
        [shape((8, width), F32)],
    )
    (small,) = line.add([(small,), (core_swap(small),)])
    (small,) = line.run(
        small_extra_kernel,
        "small_extra",
        [],
        [small, chip_swap(small), in_bias_sum, proj_bias_sum],
        [shape((8, width), F32)],
    )
    while not head_bank.done:
        head_bank.advance()
    bit = 1
    while 2 * bit < size:
        (small,) = line.add([(small,), (swap(small, "dp", size, bit),)])
        bit *= 2
    *lines, grad_proj_bias = line.run(
        finish_small_kernel,
        "finish_small",
        [],
        [small, swap(small, "dp", size, bit)],
        [shape((width,), F32)] * 7 + [shape((3, local), F32)],
        [pltpu.VMEM((8, width), F32)],
    )
    grad_down_weight, grad_in_weight = line.run(
        finish_kernel,
        "finish",
        [],
        feed_bank.slots,
        [shape((units, width), F32), shape((width, units), F32)],
    )
    grad_qkv_weight, grad_out_weight = line.run(
        finish_project_kernel,
        "finish_project",
        [],
        head_bank.slots,
        [shape((3 * local, width), F32), shape((local, width), F32)],
        [pltpu.VMEM((4 * local, width), F32)],
    )
    grad_qkv_weight = jnp.transpose(grad_qkv_weight.reshape(3, local, width), (0, 2, 1))
    return (
        blocks_out,
        input_grad,
        lines[0],
        lines[1],
        grad_qkv_weight,
        grad_proj_bias,
        grad_out_weight,
        lines[5],
        lines[2],
        lines[3],
        grad_in_weight,
        lines[6],
        grad_down_weight,
        lines[4],
    )


def solution(mesh):
    sharded = P("tp", "dp", None)
    return jax.shard_map(
        partial(on_device, mesh.shape["dp"]),
        mesh=mesh,
        in_specs=(
            sharded,
            P("dp", None),
            sharded,
            P(),
            P(),
            P(None, None, "tp"),
            P(None, "tp"),
            P("tp", None),
            P(),
            P(),
            P(),
            P(None, "tp"),
            P("tp"),
            P("tp", None),
            P(),
        ),
        out_specs=(
            sharded,
            sharded,
            P(),
            P(),
            P(None, None, "tp"),
            P(None, "tp"),
            P("tp", None),
            P(),
            P(),
            P(),
            P(None, "tp"),
            P("tp"),
            P("tp", None),
            P(),
        ),
        check_vma=False,
    )
```

```python
from functools import partial

import jax
import jax.numpy as jnp
import numpy as np
from jax import lax
from jax.experimental import pallas as pl
from jax.experimental.pallas import tpu as pltpu
from jax.sharding import PartitionSpec as P

HEAD_DIM = 64
HALF = HEAD_DIM // 2
KEY_ROWS = 128
EPSILON = 1e-05
APART = -1e30
F32 = jnp.float32
BF16 = jnp.bfloat16

NN = (((1,), (0,)), ((), ()))
NT = (((1,), (1,)), ((), ()))
TN = (((0,), (0,)), ((), ()))


def dot(a, b, dims=NN):
    return lax.dot_general(a, b, dims, preferred_element_type=F32)


def shape(dims, dtype=BF16):
    return jax.ShapeDtypeStruct(dims, dtype)


class Line:
    def __init__(self):
        self.tile = None

    def run(
        self, body, name, scalars, arrays, outs, scratch=(), vmem=8, inputs=None, numbers=(), places=None
    ):
        before = [] if self.tile is None else [self.tile]
        count, extra, made = len(scalars) + len(arrays), len(before), len(outs)
        made += len(numbers)

        def whole(*refs):
            tile = refs[count + extra + made]
            tile[...] = jnp.zeros_like(tile)
            body(
                *refs[:count],
                *refs[count + extra : count + extra + made],
                *refs[count + extra + made + 1 :],
            )

        vector = pl.BlockSpec(memory_space=pltpu.VMEM)
        scalar = pl.BlockSpec(memory_space=pltpu.SMEM)
        *results, self.tile = pl.pallas_call(
            whole,
            out_shape=(*numbers, *outs, shape((8, 128), F32)),
            in_specs=[scalar] * len(scalars)
            + (inputs or [vector] * len(arrays))
            + [vector] * extra,
            out_specs=(scalar,) * len(numbers)
            + (tuple(places) if places else (vector,) * len(outs))
            + (vector,),
            scratch_shapes=list(scratch),
            compiler_params=pltpu.CompilerParams(vmem_limit_bytes=vmem * 1024 * 1024),
            cost_estimate=pl.CostEstimate(flops=1, bytes_accessed=1, transcendentals=0),
            name=name,
        )(*scalars, *arrays, *before)
        return results

    def keep(self, *arrays):
        def body(*refs):
            for k in range(len(arrays)):
                refs[len(arrays) + k][...] = refs[k][...]

        return self.run(body, "keep", [], arrays, [shape(v.shape, v.dtype) for v in arrays])

    def split(self, near, pair):
        def body(near, pair, one, two):
            one[...] = pair[0]
            two[0] = near[...]
            two[1] = pair[1]

        made = [shape(near.shape), shape((2, *near.shape))]
        one, two = self.run(body, "split", [], [near, pair], made)
        return [one, core_swap(two)]

    def merge(self, one, two, cuts):
        def body(one, two, *outs):
            total = one[...].astype(F32) + two[...].astype(F32)
            size = total.shape[0] // cuts
            for k, out in enumerate(outs):
                out[...] = total[k * size : (k + 1) * size].astype(out.dtype)

        made = [shape((one.shape[0] // cuts, *one.shape[1:]))] * cuts
        return self.run(body, "merge", [], [one, two], made)

    def join(self, *arrays):
        def body(*refs):
            for k in range(len(arrays)):
                refs[len(arrays)][k] = refs[k][...]

        first = arrays[0]
        made = [shape((len(arrays), *first.shape), first.dtype)]
        return self.run(body, "join", [], arrays, made, vmem=8)[0]

    def add_rows(self, ones, twos):
        count = len(ones)

        def body(*refs):
            for r in range(count):
                total = refs[r][...].astype(F32) + refs[count + r][1].astype(F32)
                refs[2 * count][r] = total.astype(BF16)

        made = [shape((count, *ones[0].shape))]
        return self.run(body, "add_rows", [], [*ones, *twos], made)[0]

    def add_pair(self, one, two):
        def body(a, b, c, d, out):
            out[0] = (a[...].astype(F32) + b[...].astype(F32)).astype(out.dtype)
            out[1] = (c[...].astype(F32) + d[...].astype(F32)).astype(out.dtype)

        made = [shape((2, *one[0].shape), one[0].dtype)]
        return self.run(body, "add_pair", [], [*one, *two], made)[0]

    def add(self, *sums):
        arrays = [term[0] for terms in sums for term in terms]
        parts = [[term[1:] for term in terms] for terms in sums]
        outs = []
        for terms in sums:
            first = terms[0][0]
            outs.append(shape(first.shape[len(terms[0]) - 1 :], first.dtype))

        def body(*refs):
            at = 0
            for k, terms in enumerate(parts):
                total = None
                for index in terms:
                    value = refs[at][index[0]] if index else refs[at][...]
                    value = value.astype(F32)
                    total = value if total is None else total + value
                    at += 1
                out = refs[len(arrays) + k]
                out[...] = total.astype(out.dtype)

        return self.run(body, "add", [], arrays, outs)


def normalize(values):
    average = jnp.mean(values, axis=-1, keepdims=True)
    centered = values - average
    variance = jnp.mean(centered * centered, axis=-1, keepdims=True)
    inverse = lax.rsqrt(variance + EPSILON)
    return centered * inverse, inverse


def normalize_back(gradient, scaled, inverse, gain):
    grad_scaled = gradient * gain
    return inverse * (
        grad_scaled
        - jnp.mean(grad_scaled, axis=-1, keepdims=True)
        - scaled * jnp.mean(grad_scaled * scaled, axis=-1, keepdims=True)
    )


def where_am_i():
    me = lax.axis_index("tp")
    return me, me // 2, lax.axis_index("dp") & 3


def first_norm_kernel(rows, width, hid, *refs):
    lines, (vectors, first, alone) = refs[:7], refs[7:10]
    lands, sems = refs[10:17], refs[17]
    copies = [
        pltpu.make_async_copy(line, land, sems.at[k])
        for k, (line, land) in enumerate(zip(lines, lands))
    ]
    for copy in copies:
        copy.start()
    normed = []
    for r in range(rows):
        values = hid[:, r * width : (r + 1) * width].astype(F32)
        normed.append(normalize(values)[0])
    for copy in copies:
        copy.wait()
    for k, land in enumerate(lands):
        vectors[k : k + 1, :] = land[...].astype(F32).reshape(1, width)
    vectors[7:8, :] = jnp.zeros((1, width), F32)
    for r in range(rows):
        low = (normed[r] * vectors[0:1, :] + vectors[1:2, :]).astype(BF16)
        first[r] = low
        if r == 0:
            alone[...] = low


def table_kernel(block, segments, rates, bias, windows, marks, waves, column):
    rows, length = segments.shape
    ids = lax.broadcasted_iota(jnp.int32, (16, length), 0)
    spots = lax.broadcasted_iota(jnp.int32, (1, length), 1)
    for r in range(rows):
        row = segments[r : r + 1, :]
        same = row == ids
        before = jnp.sum((row < ids).astype(F32), axis=1, keepdims=True)
        begins = jnp.sum(jnp.where(same, before, 0.0), axis=0, keepdims=True)
        ends = jnp.sum((row <= ids).astype(F32), axis=1, keepdims=True)
        closes = jnp.sum(jnp.where(same, ends, 0.0), axis=0, keepdims=True)
        marks[r, 0] = same.astype(F32).astype(BF16)
        marks[r, 1] = jnp.where(same | (ids >= 8), 0.0, APART).astype(BF16)
        angles = rates[...] * (spots.astype(F32) - begins)
        waves[r, 0] = jnp.cos(angles)
        waves[r, 1] = jnp.sin(angles)
        blocks = length // block
        for q in range(blocks):
            inside = slice(q * block, (q + 1) * block)
            least = jnp.min(begins[:, inside]).astype(jnp.int32)
            past = jnp.max(closes[:, inside]).astype(jnp.int32)
            start = (least // 128) * 128
            count = (past - start + block - 1) // block
            windows[2 * blocks * r + q] = jnp.minimum(start, length - count * block)
            windows[2 * blocks * r + blocks + q] = count
    local = bias.shape[1]
    tall = jnp.concatenate([bias[...].astype(F32), jnp.zeros((5, local), F32)], axis=0)
    tall = jnp.transpose(tall)
    for c in range(3):
        column[c * local : (c + 1) * local, :] = tall[:, c : c + 1]


def split_kernel(width, whole, *outs):
    for r, out in enumerate(outs):
        out[...] = whole[:, r * width : (r + 1) * width]


def project_kernel(far, picked, one, two, weight, bias, waves, out):
    block = two.shape[-2]
    local = weight.shape[0] // 3
    me, chip, _ = where_am_i()
    half = chip ^ far
    for at, r in enumerate(picked):
        for k, tokens in enumerate((one, two)):
            spot = pl.multiple_of(((me & 1) ^ k) * block, block)
            span = pl.ds(spot, block)
            table = pl.ds(pl.multiple_of(half * (2 * block) + spot, block), block)
            values = tokens[at] if len(tokens.shape) == 3 else tokens[...]
            turned = dot(weight[...], values, NT) + bias[...]
            cs = waves[r, 0, :, table]
            sn = waves[r, 1, :, table]
            for c in range(2):
                for base in range(c * local, (c + 1) * local, HEAD_DIM):
                    a = turned[base : base + HALF]
                    b = turned[base + HALF : base + HEAD_DIM]
                    new_a = a * cs - b * sn
                    new_b = b * cs + a * sn
                    if c == 0:
                        new_a = new_a * HEAD_DIM**-0.5
                        new_b = new_b * HEAD_DIM**-0.5
                    out[at, base : base + HALF, span] = new_a.astype(BF16)
                    out[at, base + HALF : base + HEAD_DIM, span] = new_b.astype(BF16)
            out[at, 2 * local :, span] = turned[2 * local :].astype(BF16)


def turn_over(values):
    return jnp.transpose(values.astype(F32)).astype(BF16)


def sides(r, near, far):
    chip = where_am_i()[1]
    width = near.shape[-1]
    return [
        (source, pl.ds(pl.multiple_of(at, width), width))
        for source, at in ((near.at[r], chip * width), (far.at[0], (1 - chip) * width))
    ]


def lay_out(r, picked, near, far, marked, queries, keys):
    mine = marked[r, 0]
    width = near.shape[-1]
    local = near.shape[1] // 3
    marks = mine.shape[0]
    for source, span in sides(r, near, far):
        for at, h in enumerate(picked):
            queries[at * KEY_ROWS : at * KEY_ROWS + HEAD_DIM, span] = source[
                h * HEAD_DIM : (h + 1) * HEAD_DIM, :
            ]
            column = jnp.concatenate(
                [
                    source[local + h * HEAD_DIM : local + (h + 1) * HEAD_DIM, :],
                    marked[r, 1, :, span],
                    jnp.zeros((KEY_ROWS - HEAD_DIM - marks, width), BF16),
                ],
                axis=0,
            )
            keys[at, span, :] = turn_over(column)
    for at in range(len(picked)):
        base = at * KEY_ROWS + HEAD_DIM
        queries[base : base + marks, :] = mine
        queries[base + marks : (at + 1) * KEY_ROWS, :] = jnp.zeros(
            (KEY_ROWS - HEAD_DIM - marks, queries.shape[1]), BF16
        )


def attend_kernel(r, windows, near, far, marked, *rest):
    outs, (log_norm, queries, keys, values, attended) = rest[:3], rest[3:]
    block = near.shape[-1] // 2
    local = near.shape[1] // 3
    heads = local // HEAD_DIM
    me = where_am_i()[0]
    lay_out(r, range(heads), near, far, marked, queries, keys)
    for source, span in sides(r, near, far):
        values[:, span] = source[2 * local :, :]

    @pl.loop(0, 4)
    def _(quarter):
        span = pl.ds(pl.multiple_of(quarter * block, block), block)
        start = pl.multiple_of(windows[8 * r + quarter], 128)
        count = windows[8 * r + 4 + quarter]

        def work(blocks):
            window = pl.ds(start, blocks * block)

            @pl.loop(0, heads)
            def _(h):
                part = pl.ds(pl.multiple_of(h * HEAD_DIM, HEAD_DIM), HEAD_DIM)
                rows = pl.ds(pl.multiple_of(h * KEY_ROWS, KEY_ROWS), KEY_ROWS)
                scores = dot(keys[h, window, :], queries[rows, span])
                peak = jnp.max(scores, axis=0, keepdims=True)
                weights = jnp.exp(scores - peak)
                total = jnp.sum(weights, axis=0, keepdims=True)
                out = dot(values[part, window], weights.astype(BF16))
                attended[part, span] = (out * (1.0 / total)).astype(BF16)
                log_norm[pl.ds(h, 1), span] = peak + jnp.log(total)

        for blocks in range(1, 5):
            pl.when(count == blocks)(partial(work, blocks))

    for s, out in enumerate((outs[0], outs[1], outs[2].at[0], outs[2].at[1])):
        out[...] = attended[:, pl.ds(pl.multiple_of((me ^ s) * block, block), block)]


def attend_back_kernel(r, picked, windows, near, far, marked, log_norm, waves, *rest):
    grads = (rest[0], rest[2].at[0], rest[1], rest[2].at[1])
    scratch, rest = rest[-8:], rest[3:-8]
    queries, keys, key_rows, value_cols, grad_rows, dk, dv, dq = scratch
    block = near.shape[-1] // 2
    local = near.shape[1] // 3
    heads = local // HEAD_DIM
    me = where_am_i()[0]
    if len(rest) == 1:
        before, weight, grad_proj, partials = None, None, rest[0], ()
    else:
        before = rest[0] if rest[0].shape[0] < rest[1].shape[0] else None
        weight, grad_proj, own, across, *sent = rest[1:] if before is not None else rest
        if len(sent) == 1:
            sent = (sent[0].at[0], sent[0].at[1])
        partials = (own, sent[0], across, sent[1])
    stride = grad_proj.shape[0] // 3
    first = picked[0] if weight is None else 0
    lay_out(r, picked, near, far, marked, queries, keys)
    for source, span in sides(r, near, far):
        for at, h in enumerate(picked):
            part = slice(at * HEAD_DIM, (at + 1) * HEAD_DIM)
            key_rows[part, span] = source[local + h * HEAD_DIM : local + (h + 1) * HEAD_DIM, :]
            value_cols[at, span, :] = turn_over(
                source[2 * local + h * HEAD_DIM : 2 * local + (h + 1) * HEAD_DIM, :]
            )
    for s, grad in enumerate(grads):
        span = pl.ds(pl.multiple_of((me ^ s) * block, block), block)
        for at, h in enumerate(picked):
            rows = grad[h * HEAD_DIM : (h + 1) * HEAD_DIM, :]
            grad_rows[at * HEAD_DIM : (at + 1) * HEAD_DIM, span] = rows
    dk[...] = jnp.zeros_like(dk)
    dv[...] = jnp.zeros_like(dv)

    @pl.loop(0, 4)
    def _(quarter):
        span = pl.ds(pl.multiple_of(quarter * block, block), block)
        start = pl.multiple_of(windows[8 * r + quarter], 128)
        count = windows[8 * r + 4 + quarter]

        def work(blocks):
            window = pl.ds(start, blocks * block)
            for at, h in enumerate(picked):
                part = slice(at * HEAD_DIM, (at + 1) * HEAD_DIM)
                scores = dot(
                    keys[at, window, :], queries[at * KEY_ROWS : (at + 1) * KEY_ROWS, span]
                )
                probs = jnp.exp(scores - log_norm[h : h + 1, span])
                grad_probs = dot(value_cols[at, window, :], grad_rows[part, span])
                inner = jnp.sum(probs * grad_probs, axis=0, keepdims=True)
                grad_scores = (probs * (grad_probs - inner)).astype(BF16)
                dv[part, window] += dot(grad_rows[part, span], probs.astype(BF16), NT)
                asked = slice(at * KEY_ROWS, at * KEY_ROWS + HEAD_DIM)
                dk[part, window] += dot(queries[asked, span], grad_scores, NT)
                dq[part, span] = dot(key_rows[part, window], grad_scores)

        for blocks in range(1, 5):
            pl.when(count == blocks)(partial(work, blocks))

    cs = waves[r, 0]
    sn = waves[r, 1]

    def turn_back(rows, base):
        a = rows[:HALF]
        b = rows[HALF:]
        grad_proj[base : base + HALF, :] = (a * cs + b * sn).astype(BF16)
        grad_proj[base + HALF : base + HEAD_DIM, :] = (b * cs - a * sn).astype(BF16)

    for at, h in enumerate(picked):
        base = (h - first) * HEAD_DIM
        turn_back(dq[at * HEAD_DIM : (at + 1) * HEAD_DIM, :] * HEAD_DIM**-0.5, base)
        part = slice(at * HEAD_DIM, (at + 1) * HEAD_DIM)
        turn_back(dk[part, :], stride + base)
        base += 2 * stride
        grad_proj[base : base + HEAD_DIM, :] = dv[part, :].astype(BF16)
    if before is not None:
        had = before.shape[0] // 3
        for c in range(3):
            grad_proj[c * stride : c * stride + had, :] = before[c * had : (c + 1) * had, :]
    for s, partial_out in enumerate(partials):
        span = pl.ds(pl.multiple_of((me ^ s) * block, block), block)
        partial_out[...] = dot(grad_proj[:, span], weight[...], TN).astype(BF16)


def four(parts):
    return (parts[0], parts[2].at[0], parts[1], parts[2].at[1])


def middle_kernel(row, hid, *rest):
    attended, weights = four(rest[:3]), rest[3:7]
    vectors, cot, middle, second, pair = rest[7:12]
    width = vectors.shape[1]
    branch = vectors[2:3, :]
    for a, w in zip(attended, weights):
        branch = branch + dot(a[...], w[...], TN)
    values = hid[:, row * width : (row + 1) * width].astype(F32) + branch
    middle[...] = values
    scaled, _ = normalize(values)
    low = (scaled * vectors[3:4, :] + vectors[4:5, :]).astype(BF16)
    second[...] = low
    pair[0] = low
    pair[1] = cot[...]


def gelu_parts(h):
    size = jnp.abs(h)
    t = 1.0 / (1.0 + size * (0.3275911 * 0.5**0.5))
    density = jnp.exp(h * h * -0.5)
    poly = t * (
        0.254829592
        + t * (-0.284496736 + t * (1.421413741 + t * (-1.453152027 + t * 1.061405429)))
    )
    tail = 0.5 * poly * density
    below = jnp.where(h < 0, tail, 1.0 - tail)
    return below, density * 0.3989422804014327


def feed_kernel(second, cot, w_in, w_out, vectors, passed_in, passed_out, passed_vectors, act, grad_pre, *outs):
    if cot is None:
        second, cot = second.at[0], second.at[1]
    units = w_in.shape[1]
    width = w_in.shape[0]
    step = 256
    tokens = second[...]
    portion = cot[...]
    for side, lines in enumerate((vectors, passed_vectors)):
        for u in range(0, units, step):
            cols = slice(u, u + step)
            spot = slice(side * units + u, side * units + u + step)
            into = passed_in[:, cols] if side else w_in[:, cols]
            down = passed_out[u : u + step, :] if side else w_out[cols, :]
            pre = dot(tokens, into) + lines[6:7, cols]
            below, density = gelu_parts(pre)
            act[:, spot] = (pre * below).astype(BF16)
            grad_act = dot(portion, down, NT)
            grad_pre[:, spot] = (grad_act * (below + pre * density)).astype(BF16)
    out = dot(act[:, :units], w_out[...]) + dot(act[:, units:], passed_out[...])
    grad = dot(grad_pre[:, :units], w_in[...], NT) + dot(
        grad_pre[:, units:], passed_in[...], NT
    )
    half = out.shape[0] // 2
    outs[0][...] = out.astype(BF16)
    low = grad.astype(BF16)
    if len(outs) == 2:
        outs[1][...] = low
    else:
        outs[1][...] = low[:half]
        outs[2][...] = low[half:]


def feed_weights_kernel(count, *refs):
    near = count // 2
    seconds, cots, pairs = refs[:near], refs[near:count], refs[count : count + near]
    seconds = [*seconds, *(pair.at[0] for pair in pairs)]
    cots = [*cots, *(pair.at[1] for pair in pairs)]
    refs = refs[count + near :]
    acts, pres = refs[:count], refs[count : 2 * count]
    own, passed, own_bias, passed_bias, down, up = refs[2 * count :]
    units = own.shape[1]
    for k in range(count):
        pre = pres[k][...]
        part_down = dot(acts[k][...], cots[k][...], TN)
        part_up = dot(seconds[k][...], pre, TN)
        sums = jnp.sum(pre.astype(F32), axis=0, keepdims=True)
        if k == 0:
            down[...] = part_down
            up[...] = part_up
            added = sums
        else:
            down[...] += part_down
            up[...] += part_up
            added += sums
    own_bias[...] = added[:, :units]
    passed_bias[...] = jnp.broadcast_to(added[:, units:], passed_bias.shape)
    own[0] = down[:units, :].astype(BF16)
    own[1] = up[:, :units].astype(BF16)
    passed[0] = down[units:, :].astype(BF16)
    passed[1] = up[:, units:].astype(BF16)


def feed_slots_kernel(own, passed, own_bias, passed_bias, bias, *outs):
    piece = outs[0].shape[0] // 2
    spot = where_am_i()[2]
    bias[...] = own_bias[...] + passed_bias[0:1, :]
    for s, out in enumerate(outs):
        span = pl.ds(pl.multiple_of((spot ^ s) * piece, piece), piece)
        for bank in range(2):
            total = own[bank, span, :].astype(F32) + passed[bank, span, :].astype(F32)
            out[bank * piece : (bank + 1) * piece, :] = total.astype(BF16)


def middle_back_kernel(chips, own, *rest):
    chip, rest = rest[:chips], rest[chips:]
    middle, cot, vectors = rest[:3]
    weights, outs = rest[3:7], rest[7:]
    grad_middle, grad_branch, sums = outs[0], outs[1], outs[5]
    heads = (outs[2], outs[3], outs[4].at[0], outs[4].at[1])
    across = jnp.concatenate([part[...] for part in chip], axis=0) if chips > 1 else chip[0][...]
    grad_second = own[...].astype(F32) + across.astype(F32)
    scaled, inverse = normalize(middle[...])
    grad_out = cot[...].astype(F32)
    total = grad_out + normalize_back(grad_second, scaled, inverse, vectors[3:4, :])
    low = total.astype(BF16)
    grad_middle[...] = total
    grad_branch[...] = low
    for w, out in zip(weights, heads):
        out[...] = dot(w[...], low, NT).astype(BF16)
    sums[0:1, :] = jnp.sum(grad_second * scaled, axis=0, keepdims=True)
    sums[1:2, :] = jnp.sum(grad_second, axis=0, keepdims=True)
    sums[2:3, :] = jnp.sum(grad_out, axis=0, keepdims=True)
    sums[3:4, :] = jnp.sum(low.astype(F32), axis=0, keepdims=True)
    sums[4:, :] = jnp.zeros((4, sums.shape[1]), F32)


def out_weight_kernel(rows, *refs):
    attended, grads, outs = refs[: 3 * rows], refs[3 * rows : 4 * rows], refs[4 * rows :]
    attended = [four(attended[3 * r : 3 * r + 3]) for r in range(rows)]
    own, across, sent = outs
    for s, out in enumerate((own, sent.at[0], across, sent.at[1])):
        total = dot(attended[0][s][...], grads[0][...])
        for r in range(1, rows):
            total = total + dot(attended[r][s][...], grads[r][...])
        out[...] = total.astype(BF16)


def project_weights_kernel(rows, *refs):
    projs, near, far = refs[:rows], refs[rows : rows + 2], refs[rows + 2 : 3 * rows + 2]
    refs = refs[3 * rows + 2 :]
    own, swapped, chip = refs[:3]
    outs, (bias, total) = refs[3:7], refs[7:]
    block = near[0].shape[1]
    me, _, spot = where_am_i()
    size = projs[0].shape[0]
    local = size // 3
    ones = jnp.ones((8, projs[0].shape[1]), BF16)
    bias[...] = jnp.zeros_like(bias)
    for c in range(3):
        part = slice(c * local, (c + 1) * local)
        sums = dot(ones, projs[0][part, :], NT)
        for r in range(1, rows):
            sums += dot(ones, projs[r][part, :], NT)
        bias[:, 256 * c : 256 * c + local] = sums
    for r in range(rows):
        for s in range(4):
            span = pl.ds(pl.multiple_of((me ^ s) * block, block), block)
            tokens = near[s][r] if s < 2 else far[2 * r + s - 2][...]
            product = dot(projs[r][:, span], tokens)
            if r + s == 0:
                total[:size, :] = product
            else:
                total[:size, :] += product
    total[size:, :] = own[...].astype(F32) + swapped[0].astype(F32) + chip[...].astype(F32)
    piece = outs[0].shape[0]
    for s, out in enumerate(outs):
        at = pl.multiple_of((spot ^ s) * piece, piece)
        out[...] = total[pl.ds(at, piece), :].astype(BF16)


def finish_kernel(*refs):
    spot = where_am_i()[2]
    slots, outs = refs[:4], refs[4:]
    for s, slot in enumerate(slots):
        piece = slot.shape[0] // 2
        span = pl.ds(pl.multiple_of((spot ^ s) * piece, piece), piece)
        for k, out in enumerate(outs):
            out[span, :] = slot[k * piece : (k + 1) * piece, :].astype(F32)


def finish_project_kernel(*refs):
    spot = where_am_i()[2]
    slots, (big, small, total) = refs[:4], refs[4:]
    for s, slot in enumerate(slots):
        piece = slot.shape[0]
        at = pl.multiple_of((spot ^ s) * piece, piece)
        total[pl.ds(at, piece), :] = slot[...].astype(F32)
    size = big.shape[0]
    big[...] = total[:size, :]
    small[...] = total[size:, :]


def first_back_kernel(row, kept, chip, hid, grad_middle, vectors, grad_in, sums):
    width = vectors.shape[1]
    grad_first = sum(part[...].astype(F32) for part in kept) + chip[...].astype(F32)
    scaled, inverse = normalize(hid[:, row * width : (row + 1) * width].astype(F32))
    grad_in[...] = grad_middle[...] + normalize_back(grad_first, scaled, inverse, vectors[0:1, :])
    sums[0:1, :] = jnp.sum(grad_first * scaled, axis=0, keepdims=True)
    sums[1:2, :] = jnp.sum(grad_first, axis=0, keepdims=True)
    sums[2:, :] = jnp.zeros((6, width), F32)


def small_kernel(firsts, middles, out):
    rows = len(firsts)
    out[...] = jnp.zeros_like(out)
    out[0:2, :] = sum(ref[0:2, :] for ref in firsts)
    out[2:6, :] = sum(ref[0:4, :] for ref in middles)


def small_extra_kernel(one, two, in_bias, proj_bias, out):
    out[...] = one[...] + two[...]
    out[6:7, :] = in_bias[...]
    out[7:8, :] = proj_bias[0:1, :]


def finish_small_kernel(one, two, *outs):
    *lines, proj_bias, total = outs
    total[...] = one[...] + two[...]
    width = total.shape[1]
    for k, line in enumerate(lines):
        line[...] = total[k : k + 1, :].reshape(width)
    local = proj_bias.shape[1]
    for c in range(3):
        proj_bias[c : c + 1, :] = total[7:8, 256 * c : 256 * c + local]


def block_out_kernel(own, middle, across, vectors, out):
    total = own[...].astype(F32) + across[...].astype(F32)
    out[...] = (middle[...] + (total + vectors[5:6, :])).astype(BF16)


def swap(values, axis, size, bit):
    return lax.ppermute(values, axis, [(i, i ^ bit) for i in range(size)])


def core_swap(values):
    return swap(values, "tp", 4, 1)


def chip_swap(values):
    return swap(values, "tp", 4, 2)


class Bank:
    def __init__(self, line, slots, size):
        self.line, self.own, self.size = line, slots[0], size
        self.moved = [swap(slots[s], "dp", size, s) for s in range(1, 4)]
        self.bit = 2

    def advance(self):
        (self.own,) = self.line.add([(self.own,), *((v,) for v in self.moved)])
        self.bit *= 2
        if self.bit < self.size:
            self.moved = [swap(self.own, "dp", self.size, self.bit)]
            return
        self.slots = [self.own] + [swap(self.own, "dp", self.size, s) for s in range(1, 4)]

    @property
    def done(self):
        return self.bit >= self.size


def on_device(
    size,
    hidden_in,
    segment_ids,
    cotangent,
    norm1_gain,
    norm1_bias,
    qkv_weight,
    qkv_bias,
    out_weight,
    out_bias,
    norm2_gain,
    norm2_bias,
    ffn_in_weight,
    ffn_in_bias,
    ffn_out_weight,
    ffn_out_bias,
):
    block, rows, width = hidden_in.shape
    length = segment_ids.shape[1]
    local = qkv_weight.shape[2]
    heads = local // HEAD_DIM
    units = ffn_in_weight.shape[1]
    line = Line()
    each, last = range(rows), rows - 1
    full, half, both = shape((block, width)), shape((block // 2, width)), shape((rows, block, width))
    hid = hidden_in.reshape(block, rows * width)
    cots = cotangent.reshape(block, rows * width)
    vector, anywhere = pl.BlockSpec(memory_space=pltpu.VMEM), pl.BlockSpec(memory_space=pltpu.HBM)
    params = [norm1_gain, norm1_bias, out_bias, norm2_gain, norm2_bias, ffn_out_bias, ffn_in_bias]
    vectors, first, alone = line.run(
        partial(first_norm_kernel, rows, width),
        "first_norm",
        [],
        [hid, *params],
        [shape((8, width), F32), both, full],
        [pltpu.VMEM((width,), BF16)] * 7 + [pltpu.SemaphoreType.DMA((7,))],
        inputs=[vector] + [anywhere] * 7,
    )
    first_across = [chip_swap(alone)]
    first_beside = core_swap(first)
    passed_in, passed_out = core_swap(ffn_in_weight), core_swap(ffn_out_weight)
    passed_vectors = core_swap(vectors)

    rates = np.power(10000.0, -2.0 * np.arange(HALF) / HEAD_DIM).astype(np.float32)
    windows, marks, waves, proj_bias = line.run(
        partial(table_kernel, block),
        "tables",
        [],
        [segment_ids, jnp.asarray(rates.reshape(HALF, 1)), qkv_bias],
        [
            shape((rows, 2, 16, length)),
            shape((rows, 2, HALF, length), F32),
            shape((3 * local, 1), F32),
        ],
        numbers=[shape((rows * 2 * (length // block),), jnp.int32)],
    )
    proj_weight = jnp.transpose(qkv_weight, (0, 2, 1)).reshape(3 * local, width)

    def project(far, picked, one, two):
        return line.run(
            partial(project_kernel, far, picked),
            "project",
            [],
            [one, two, proj_weight, proj_bias, waves],
            [shape((len(picked), 3 * local, 2 * block))],
        )[0]

    def attend(r):
        *outs, log_norm = line.run(
            partial(attend_kernel, r),
            "attend",
            [windows],
            [near, far[r], marks],
            [shape((local, block))] * 2
            + [shape((2, local, block)), shape((8, length), F32)],
            [
                pltpu.VMEM((heads * KEY_ROWS, length), BF16),
                pltpu.VMEM((heads, length, KEY_ROWS), BF16),
                pltpu.VMEM((local, length), BF16),
                pltpu.VMEM((local, length), BF16),
            ],
            vmem=14,
        )
        logs.append(log_norm)
        return [outs[0], outs[1], chip_swap(outs[2])]

    def feed(*tokens):
        tokens = list(tokens)

        def body(*refs):
            feed_kernel(*(refs if len(tokens) == 2 else (refs[0], None, *refs[1:])))

        act, pre, *outs = line.run(
            body,
            "feed",
            [],
            tokens + [ffn_in_weight, ffn_out_weight, vectors, passed_in, passed_out, passed_vectors],
            [shape((block, 2 * units))] * 2 + [full, full],
            vmem=12,
        )
        acts.append(act)
        pres.append(pre)
        return outs

    def pick(values, r):
        def body(values, out):
            out[...] = values[r]

        return line.run(body, "pick", [], [values], [shape(values.shape[1:])])[0]

    near = project(0, tuple(each), first, first_beside)
    cots = line.run(partial(split_kernel, width), "split", [], [cots], [full] * rows)
    far, far_slots = [], []
    logs, attended = [], []
    for r in each:
        (arrived,) = line.keep(first_across[r])
        far_slots += [arrived, core_swap(arrived)]
        if r < last:
            first_across.append(chip_swap(pick(first, r + 1)))
        if r == last:
            (ready,) = line.keep(out_weight)
            out_across = chip_swap(ready)
            out_beside = core_swap(ready)
        far.append(project(1, (r,), *far_slots[-2:]))
        attended.append(attend(r))

    middles, seconds, pairs = [], [], []
    acts, pres, feeds, feed_grads = [], [], [], []
    for r in each:
        if r == 0:
            (out_far,) = line.keep(out_across)
            out_slots = [out_weight, out_beside, out_far, core_swap(out_far)]
        one, two = line.split(attended[r][1], attended[r][2])
        attended[r][1:] = [one, two]
        middle, second, pair = line.run(
            partial(middle_kernel, r),
            "middle",
            [],
            [hid, *attended[r], *out_slots, vectors, cots[r]],
            [shape((block, width), F32), full, shape((2, block, width))],
        )
        middles.append(middle)
        seconds.append(second)
        pairs.append(chip_swap(pair))
        out, grad = feed(second, cots[r])
        feeds.append([out])
        feed_grads.append([grad])
    for r in each:
        out, grad = feed(pairs[r])
        feeds[r].append(out)
        feed_grads[r].append(chip_swap(grad))

    grad_middles, grad_branches, head_grads, norm_sums = [], [], [], []

    def middle_back(r):
        own, *across = feed_grads[r]
        grad_middle, grad_branch, *parts, sums = line.run(
            partial(middle_back_kernel, len(across)),
            "middle_back",
            [],
            [own, *across, middles[r], cots[r], vectors, *out_slots],
            [shape((block, width), F32), full]
            + [shape((local, block))] * 2
            + [shape((2, local, block)), shape((8, width), F32)],
        )
        grad_middles.append(grad_middle)
        grad_branches.append(grad_branch)
        head_grads.append([parts[0], parts[1], chip_swap(parts[2])])
        norm_sums.append(sums)

    own_sums, passed_sums, own_bias, passed_bias = line.run(
        partial(feed_weights_kernel, 2 * rows),
        "feed_weights",
        [],
        [*seconds, *cots, *pairs, *acts, *pres],
        [
            shape((2, units, width)),
            shape((2, units, width)),
            shape((1, units), F32),
            shape((8, units), F32),
        ],
        [pltpu.VMEM((2 * units, width), F32), pltpu.VMEM((width, 2 * units), F32)],
        vmem=22,
    )
    for r in range(last):
        middle_back(r)
    (passed_sums,) = line.keep(passed_sums)
    passed_sums = core_swap(passed_sums)
    passed_bias = core_swap(passed_bias)
    in_bias_sum, *slots = line.run(
        feed_slots_kernel,
        "feed_slots",
        [],
        [own_sums, passed_sums, own_bias, passed_bias],
        [shape((1, units), F32)] + [shape((units // 2, width))] * 4,
    )
    feed_bank = Bank(line, slots, size)
    middle_back(last)
    head_grads[0][1:] = line.split(*head_grads[0][1:])
    blocks_across = [chip_swap(line.keep(feeds[r][1])[0]) for r in range(last)]

    def block_out(r):
        return line.run(
            block_out_kernel,
            "block_out",
            [],
            [feeds[r][0], middles[r], blocks_across[r], vectors],
            [full],
        )[0]

    def attend_back(r, picked, before):
        final = picked[-1] == heads - 1
        some = len(picked)
        made = local if final else some * HEAD_DIM
        grad_proj, *parts = line.run(
            partial(attend_back_kernel, r, picked),
            "attend_back",
            [windows],
            [near, far[r], marks, logs[r], waves, *head_grads[r]]
            + before
            + ([proj_weight] if final else []),
            [shape((3 * made, length))]
            + ([full, full] if final else [])
            + ([full, full] if final and r == last else [])
            + ([shape((2, block, width))] if final and r < last else []),
            [
                pltpu.VMEM((some * KEY_ROWS, length), BF16),
                pltpu.VMEM((some, length, KEY_ROWS), BF16),
                pltpu.VMEM((some * HEAD_DIM, length), BF16),
                pltpu.VMEM((some, length, HEAD_DIM), BF16),
                pltpu.VMEM((some * HEAD_DIM, length), BF16),
                pltpu.VMEM((some * HEAD_DIM, length), F32),
                pltpu.VMEM((some * HEAD_DIM, length), F32),
                pltpu.VMEM((some * HEAD_DIM, length), F32),
            ],
            vmem=20,
        )
        if not final:
            return [grad_proj]
        projs.append(grad_proj)
        first_grads.append([parts[0], parts[1], *(core_swap(v) for v in parts[2:])])

    projs, first_grads, kepts, backs = [], [], [], []
    for r in each:
        if r > 0:
            head_grads[r][1:] = line.split(*head_grads[r][1:])
        if r == last:
            feed_bank.advance()
            blocks_out = [block_out(k) for k in range(last)]
            out_parts = line.run(
                partial(out_weight_kernel, rows),
                "out_weight",
                [],
                [*sum(attended, []), *grad_branches],
                [shape((local, width))] * 2 + [shape((2, local, width))],
            )
            out_beside = core_swap(out_parts[2])
            (back,) = line.add([(out_parts[1],), (out_beside, 1)])
            out_sums = [out_parts[0], out_beside, chip_swap(back)]
            blocks_across.append(chip_swap(line.keep(feeds[last][1])[0]))
            for k in range(last):
                kept, back = line.add(
                    [(first_grads[k][0],), (first_grads[k][2], 0)],
                    [(first_grads[k][1],), (first_grads[k][2], 1)],
                )
                kepts.append([kept])
                backs.append(back)
        attend_back(r, tuple(range(heads)), [])
    grads_in, first_sums = [], []

    def first_back(r):
        grad_in, sums = line.run(
            lambda *refs: first_back_kernel(r, refs[: len(kepts[r])], *refs[len(kepts[r]) :]),
            "first_back",
            [],
            [*kepts[r], first_across_back[r], hid, grad_middles[r], vectors],
            [shape((block, width), F32), shape((8, width), F32)],
        )
        grads_in.append(grad_in)
        first_sums.append(sums)

    *slots, proj_bias_sum = line.run(
        partial(project_weights_kernel, rows),
        "project_weights",
        [],
        [*projs, first, first_beside, *far_slots, *out_sums],
        [shape((local, width))] * 4 + [shape((8, width), F32)],
        [pltpu.VMEM((4 * local, width), F32)],
        vmem=10,
    )
    head_bank = Bank(line, slots, size)
    blocks_out.append(block_out(last))
    blocks_out = jnp.stack(blocks_out, axis=1)
    first_across_back = [chip_swap(v) for v in line.keep(*backs)]
    own, across, beside, sent = first_grads[last]
    kepts.append([own, beside])
    (back,) = line.add([(across,), (sent,)])
    first_across_back.append(chip_swap(back))
    while not feed_bank.done:
        feed_bank.advance()
    head_bank.advance()
    for r in each:
        first_back(r)
    input_grad = jnp.stack(grads_in, axis=1)
    (small,) = line.run(
        lambda *refs: small_kernel(refs[:rows], refs[rows : 2 * rows], refs[2 * rows]),
        "small",
        [],
        [*first_sums, *norm_sums],
        [shape((8, width), F32)],
    )
    (small,) = line.add([(small,), (core_swap(small),)])
    (small,) = line.run(
        small_extra_kernel,
        "small_extra",
        [],
        [small, chip_swap(small), in_bias_sum, proj_bias_sum],
        [shape((8, width), F32)],
    )
    while not head_bank.done:
        head_bank.advance()
    bit = 1
    while 2 * bit < size:
        (small,) = line.add([(small,), (swap(small, "dp", size, bit),)])
        bit *= 2
    *lines, grad_proj_bias = line.run(
        finish_small_kernel,
        "finish_small",
        [],
        [small, swap(small, "dp", size, bit)],
        [shape((width,), F32)] * 7 + [shape((3, local), F32)],
        [pltpu.VMEM((8, width), F32)],
    )
    grad_down_weight, grad_in_weight = line.run(
        finish_kernel,
        "finish",
        [],
        feed_bank.slots,
        [shape((units, width), F32), shape((width, units), F32)],
    )
    grad_qkv_weight, grad_out_weight = line.run(
        finish_project_kernel,
        "finish_project",
        [],
        head_bank.slots,
        [shape((3 * local, width), F32), shape((local, width), F32)],
        [pltpu.VMEM((4 * local, width), F32)],
    )
    grad_qkv_weight = jnp.transpose(grad_qkv_weight.reshape(3, local, width), (0, 2, 1))
    return (
        blocks_out,
        input_grad,
        lines[0],
        lines[1],
        grad_qkv_weight,
        grad_proj_bias,
        grad_out_weight,
        lines[5],
        lines[2],
        lines[3],
        grad_in_weight,
        lines[6],
        grad_down_weight,
        lines[4],
    )


def solution(mesh):
    sharded = P("tp", "dp", None)
    return jax.shard_map(
        partial(on_device, mesh.shape["dp"]),
        mesh=mesh,
        in_specs=(
            sharded,
            P("dp", None),
            sharded,
            P(),
            P(),
            P(None, None, "tp"),
            P(None, "tp"),
            P("tp", None),
            P(),
            P(),
            P(),
            P(None, "tp"),
            P("tp"),
            P("tp", None),
            P(),
        ),
        out_specs=(
            sharded,
            sharded,
            P(),
            P(),
            P(None, None, "tp"),
            P(None, "tp"),
            P("tp", None),
            P(),
            P(),
            P(),
            P(None, "tp"),
            P("tp"),
            P("tp", None),
            P(),
        ),
        check_vma=False,
    )
```

```python
from functools import partial

import jax
import jax.numpy as jnp
import numpy as np
from jax import lax
from jax.experimental import pallas as pl
from jax.experimental.pallas import tpu as pltpu
from jax.sharding import PartitionSpec as P

HEAD_DIM = 64
HALF = HEAD_DIM // 2
KEY_ROWS = 128
EPSILON = 1e-05
APART = -1e30
F32 = jnp.float32
BF16 = jnp.bfloat16

NN = (((1,), (0,)), ((), ()))
NT = (((1,), (1,)), ((), ()))
TN = (((0,), (0,)), ((), ()))


def dot(a, b, dims=NN):
    return lax.dot_general(a, b, dims, preferred_element_type=F32)


def shape(dims, dtype=BF16):
    return jax.ShapeDtypeStruct(dims, dtype)


class Line:
    def __init__(self):
        self.tile = None

    def run(
        self, body, name, scalars, arrays, outs, scratch=(), vmem=8, inputs=None, numbers=(), places=None
    ):
        before = [] if self.tile is None else [self.tile]
        count, extra, made = len(scalars) + len(arrays), len(before), len(outs)
        made += len(numbers)

        def whole(*refs):
            tile = refs[count + extra + made]
            tile[...] = jnp.zeros_like(tile)
            body(
                *refs[:count],
                *refs[count + extra : count + extra + made],
                *refs[count + extra + made + 1 :],
            )

        vector = pl.BlockSpec(memory_space=pltpu.VMEM)
        scalar = pl.BlockSpec(memory_space=pltpu.SMEM)
        *results, self.tile = pl.pallas_call(
            whole,
            out_shape=(*numbers, *outs, shape((8, 128), F32)),
            in_specs=[scalar] * len(scalars)
            + (inputs or [vector] * len(arrays))
            + [vector] * extra,
            out_specs=(scalar,) * len(numbers)
            + (tuple(places) if places else (vector,) * len(outs))
            + (vector,),
            scratch_shapes=list(scratch),
            compiler_params=pltpu.CompilerParams(vmem_limit_bytes=vmem * 1024 * 1024),
            cost_estimate=pl.CostEstimate(flops=1, bytes_accessed=1, transcendentals=0),
            name=name,
        )(*scalars, *arrays, *before)
        return results

    def keep(self, *arrays):
        def body(*refs):
            for k in range(len(arrays)):
                refs[len(arrays) + k][...] = refs[k][...]

        return self.run(body, "keep", [], arrays, [shape(v.shape, v.dtype) for v in arrays])

    def split(self, near, pair):
        def body(near, pair, one, two):
            one[...] = pair[0]
            two[0] = near[...]
            two[1] = pair[1]

        made = [shape(near.shape), shape((2, *near.shape))]
        one, two = self.run(body, "split", [], [near, pair], made)
        return [one, core_swap(two)]

    def merge(self, one, two, cuts):
        def body(one, two, *outs):
            total = one[...].astype(F32) + two[...].astype(F32)
            size = total.shape[0] // cuts
            for k, out in enumerate(outs):
                out[...] = total[k * size : (k + 1) * size].astype(out.dtype)

        made = [shape((one.shape[0] // cuts, *one.shape[1:]))] * cuts
        return self.run(body, "merge", [], [one, two], made)

    def join(self, *arrays):
        def body(*refs):
            for k in range(len(arrays)):
                refs[len(arrays)][k] = refs[k][...]

        first = arrays[0]
        made = [shape((len(arrays), *first.shape), first.dtype)]
        return self.run(body, "join", [], arrays, made, vmem=8)[0]

    def add_rows(self, ones, twos):
        count = len(ones)

        def body(*refs):
            for r in range(count):
                total = refs[r][...].astype(F32) + refs[count + r][1].astype(F32)
                refs[2 * count][r] = total.astype(BF16)

        made = [shape((count, *ones[0].shape))]
        return self.run(body, "add_rows", [], [*ones, *twos], made)[0]

    def add_pair(self, one, two):
        def body(a, b, c, d, out):
            out[0] = (a[...].astype(F32) + b[...].astype(F32)).astype(out.dtype)
            out[1] = (c[...].astype(F32) + d[...].astype(F32)).astype(out.dtype)

        made = [shape((2, *one[0].shape), one[0].dtype)]
        return self.run(body, "add_pair", [], [*one, *two], made)[0]

    def add(self, *sums):
        arrays = [term[0] for terms in sums for term in terms]
        parts = [[term[1:] for term in terms] for terms in sums]
        outs = []
        for terms in sums:
            first = terms[0][0]
            outs.append(shape(first.shape[len(terms[0]) - 1 :], first.dtype))

        def body(*refs):
            at = 0
            for k, terms in enumerate(parts):
                total = None
                for index in terms:
                    value = refs[at][index[0]] if index else refs[at][...]
                    value = value.astype(F32)
                    total = value if total is None else total + value
                    at += 1
                out = refs[len(arrays) + k]
                out[...] = total.astype(out.dtype)

        return self.run(body, "add", [], arrays, outs)


def normalize(values):
    average = jnp.mean(values, axis=-1, keepdims=True)
    centered = values - average
    variance = jnp.mean(centered * centered, axis=-1, keepdims=True)
    inverse = lax.rsqrt(variance + EPSILON)
    return centered * inverse, inverse


def normalize_back(gradient, scaled, inverse, gain):
    grad_scaled = gradient * gain
    return inverse * (
        grad_scaled
        - jnp.mean(grad_scaled, axis=-1, keepdims=True)
        - scaled * jnp.mean(grad_scaled * scaled, axis=-1, keepdims=True)
    )


def where_am_i():
    me = lax.axis_index("tp")
    return me, me // 2, lax.axis_index("dp") & 3


def first_norm_kernel(rows, width, hid, *refs):
    lines, (vectors, first, alone) = refs[:7], refs[7:10]
    parts, lands, sems = refs[10 : 10 + 2 * rows], refs[10 + 2 * rows : 17 + 2 * rows], refs[-1]
    copies = [
        pltpu.make_async_copy(line, land, sems.at[k])
        for k, (line, land) in enumerate(zip(lines, lands))
    ]
    for copy in copies:
        copy.start()
    normed = []
    for r in range(rows):
        values = hid[:, r * width : (r + 1) * width].astype(F32)
        normed.append(normalize(values)[0])
    for copy in copies:
        copy.wait()
    for k, land in enumerate(lands):
        vectors[k : k + 1, :] = land[...].astype(F32).reshape(1, width)
    vectors[7:8, :] = jnp.zeros((1, width), F32)
    for r in range(rows):
        low = (normed[r] * vectors[0:1, :] + vectors[1:2, :]).astype(BF16)
        first[r] = low
        half = low.shape[0] // 2
        parts[2 * r][...] = low[:half]
        parts[2 * r + 1][...] = low[half:]
        if r == 0:
            alone[...] = low


def table_kernel(block, segments, rates, bias, windows, marks, waves, column):
    rows, length = segments.shape
    ids = lax.broadcasted_iota(jnp.int32, (16, length), 0)
    spots = lax.broadcasted_iota(jnp.int32, (1, length), 1)
    for r in range(rows):
        row = segments[r : r + 1, :]
        same = row == ids
        before = jnp.sum((row < ids).astype(F32), axis=1, keepdims=True)
        begins = jnp.sum(jnp.where(same, before, 0.0), axis=0, keepdims=True)
        ends = jnp.sum((row <= ids).astype(F32), axis=1, keepdims=True)
        closes = jnp.sum(jnp.where(same, ends, 0.0), axis=0, keepdims=True)
        marks[r, 0] = same.astype(F32).astype(BF16)
        marks[r, 1] = jnp.where(same | (ids >= 8), 0.0, APART).astype(BF16)
        angles = rates[...] * (spots.astype(F32) - begins)
        waves[r, 0] = jnp.cos(angles)
        waves[r, 1] = jnp.sin(angles)
        blocks = length // block
        for q in range(blocks):
            inside = slice(q * block, (q + 1) * block)
            least = jnp.min(begins[:, inside]).astype(jnp.int32)
            past = jnp.max(closes[:, inside]).astype(jnp.int32)
            start = (least // 128) * 128
            count = (past - start + block - 1) // block
            windows[2 * blocks * r + q] = jnp.minimum(start, length - count * block)
            windows[2 * blocks * r + blocks + q] = count
    local = bias.shape[1]
    tall = jnp.concatenate([bias[...].astype(F32), jnp.zeros((5, local), F32)], axis=0)
    tall = jnp.transpose(tall)
    for c in range(3):
        column[c * local : (c + 1) * local, :] = tall[:, c : c + 1]


def split_kernel(width, whole, *outs):
    for r, out in enumerate(outs):
        out[...] = whole[:, r * width : (r + 1) * width]


def project_kernel(far, picked, one, *refs):
    two, (weight, bias, waves, out) = refs[:-4], refs[-4:]
    block = one.shape[-2]
    local = weight.shape[0] // 3
    me, chip, _ = where_am_i()
    half = chip ^ far
    for at, r in enumerate(picked):
        for k, tokens in enumerate((one, two)):
            spot = pl.multiple_of(((me & 1) ^ k) * block, block)
            span = pl.ds(spot, block)
            table = pl.ds(pl.multiple_of(half * (2 * block) + spot, block), block)
            if k == 0:
                values = tokens[at] if len(tokens.shape) == 3 else tokens[...]
            elif len(tokens) == 1:
                values = tokens[0][...]
            else:
                values = jnp.concatenate([tokens[2 * at][...], tokens[2 * at + 1][...]], axis=0)
            turned = dot(weight[...], values, NT) + bias[...]
            cs = waves[r, 0, :, table]
            sn = waves[r, 1, :, table]
            for c in range(2):
                for base in range(c * local, (c + 1) * local, HEAD_DIM):
                    a = turned[base : base + HALF]
                    b = turned[base + HALF : base + HEAD_DIM]
                    new_a = a * cs - b * sn
                    new_b = b * cs + a * sn
                    if c == 0:
                        new_a = new_a * HEAD_DIM**-0.5
                        new_b = new_b * HEAD_DIM**-0.5
                    out[at, base : base + HALF, span] = new_a.astype(BF16)
                    out[at, base + HALF : base + HEAD_DIM, span] = new_b.astype(BF16)
            out[at, 2 * local :, span] = turned[2 * local :].astype(BF16)


def turn_over(values):
    return jnp.transpose(values.astype(F32)).astype(BF16)


def sides(r, near, far):
    chip = where_am_i()[1]
    width = near.shape[-1]
    return [
        (source, pl.ds(pl.multiple_of(at, width), width))
        for source, at in ((near.at[r], chip * width), (far.at[0], (1 - chip) * width))
    ]


def lay_out(r, picked, near, far, marked, queries, keys):
    mine = marked[r, 0]
    width = near.shape[-1]
    local = near.shape[1] // 3
    marks = mine.shape[0]
    for source, span in sides(r, near, far):
        for at, h in enumerate(picked):
            queries[at * KEY_ROWS : at * KEY_ROWS + HEAD_DIM, span] = source[
                h * HEAD_DIM : (h + 1) * HEAD_DIM, :
            ]
            column = jnp.concatenate(
                [
                    source[local + h * HEAD_DIM : local + (h + 1) * HEAD_DIM, :],
                    marked[r, 1, :, span],
                    jnp.zeros((KEY_ROWS - HEAD_DIM - marks, width), BF16),
                ],
                axis=0,
            )
            keys[at, span, :] = turn_over(column)
    for at in range(len(picked)):
        base = at * KEY_ROWS + HEAD_DIM
        queries[base : base + marks, :] = mine
        queries[base + marks : (at + 1) * KEY_ROWS, :] = jnp.zeros(
            (KEY_ROWS - HEAD_DIM - marks, queries.shape[1]), BF16
        )


def attend_kernel(r, windows, near, far, marked, *rest):
    outs, (log_norm, queries, keys, values, attended) = rest[:3], rest[3:]
    block = near.shape[-1] // 2
    local = near.shape[1] // 3
    heads = local // HEAD_DIM
    me = where_am_i()[0]
    lay_out(r, range(heads), near, far, marked, queries, keys)
    for source, span in sides(r, near, far):
        values[:, span] = source[2 * local :, :]

    @pl.loop(0, 4)
    def _(quarter):
        span = pl.ds(pl.multiple_of(quarter * block, block), block)
        start = pl.multiple_of(windows[8 * r + quarter], 128)
        count = windows[8 * r + 4 + quarter]

        def work(blocks):
            window = pl.ds(start, blocks * block)

            @pl.loop(0, heads)
            def _(h):
                part = pl.ds(pl.multiple_of(h * HEAD_DIM, HEAD_DIM), HEAD_DIM)
                rows = pl.ds(pl.multiple_of(h * KEY_ROWS, KEY_ROWS), KEY_ROWS)
                scores = dot(keys[h, window, :], queries[rows, span])
                peak = jnp.max(scores, axis=0, keepdims=True)
                weights = jnp.exp(scores - peak)
                total = jnp.sum(weights, axis=0, keepdims=True)
                out = dot(values[part, window], weights.astype(BF16))
                attended[part, span] = (out * (1.0 / total)).astype(BF16)
                log_norm[pl.ds(h, 1), span] = peak + jnp.log(total)

        for blocks in range(1, 5):
            pl.when(count == blocks)(partial(work, blocks))

    for s, out in enumerate((outs[0], outs[1], outs[2].at[0], outs[2].at[1])):
        out[...] = attended[:, pl.ds(pl.multiple_of((me ^ s) * block, block), block)]


def attend_back_kernel(r, picked, windows, near, far, marked, log_norm, waves, *rest):
    grads = (rest[0], rest[2].at[0], rest[1], rest[2].at[1])
    scratch, rest = rest[-8:], rest[3:-8]
    queries, keys, key_rows, value_cols, grad_rows, dk, dv, dq = scratch
    block = near.shape[-1] // 2
    local = near.shape[1] // 3
    heads = local // HEAD_DIM
    me = where_am_i()[0]
    if len(rest) == 1:
        before, weight, grad_proj, partials = None, None, rest[0], ()
    else:
        before = rest[0] if rest[0].shape[0] < rest[1].shape[0] else None
        weight, grad_proj, own, across, *sent = rest[1:] if before is not None else rest
        if len(sent) == 1:
            sent = (sent[0].at[0], sent[0].at[1])
        partials = (own, sent[0], across, sent[1])
    stride = grad_proj.shape[0] // 3
    first = picked[0] if weight is None else 0
    lay_out(r, picked, near, far, marked, queries, keys)
    for source, span in sides(r, near, far):
        for at, h in enumerate(picked):
            part = slice(at * HEAD_DIM, (at + 1) * HEAD_DIM)
            key_rows[part, span] = source[local + h * HEAD_DIM : local + (h + 1) * HEAD_DIM, :]
            value_cols[at, span, :] = turn_over(
                source[2 * local + h * HEAD_DIM : 2 * local + (h + 1) * HEAD_DIM, :]
            )
    for s, grad in enumerate(grads):
        span = pl.ds(pl.multiple_of((me ^ s) * block, block), block)
        for at, h in enumerate(picked):
            rows = grad[h * HEAD_DIM : (h + 1) * HEAD_DIM, :]
            grad_rows[at * HEAD_DIM : (at + 1) * HEAD_DIM, span] = rows
    dk[...] = jnp.zeros_like(dk)
    dv[...] = jnp.zeros_like(dv)

    @pl.loop(0, 4)
    def _(quarter):
        span = pl.ds(pl.multiple_of(quarter * block, block), block)
        start = pl.multiple_of(windows[8 * r + quarter], 128)
        count = windows[8 * r + 4 + quarter]

        def work(blocks):
            window = pl.ds(start, blocks * block)
            for at, h in enumerate(picked):
                part = slice(at * HEAD_DIM, (at + 1) * HEAD_DIM)
                scores = dot(
                    keys[at, window, :], queries[at * KEY_ROWS : (at + 1) * KEY_ROWS, span]
                )
                probs = jnp.exp(scores - log_norm[h : h + 1, span])
                grad_probs = dot(value_cols[at, window, :], grad_rows[part, span])
                inner = jnp.sum(probs * grad_probs, axis=0, keepdims=True)
                grad_scores = (probs * (grad_probs - inner)).astype(BF16)
                dv[part, window] += dot(grad_rows[part, span], probs.astype(BF16), NT)
                asked = slice(at * KEY_ROWS, at * KEY_ROWS + HEAD_DIM)
                dk[part, window] += dot(queries[asked, span], grad_scores, NT)
                dq[part, span] = dot(key_rows[part, window], grad_scores)

        for blocks in range(1, 5):
            pl.when(count == blocks)(partial(work, blocks))

    cs = waves[r, 0]
    sn = waves[r, 1]

    def turn_back(rows, base):
        a = rows[:HALF]
        b = rows[HALF:]
        grad_proj[base : base + HALF, :] = (a * cs + b * sn).astype(BF16)
        grad_proj[base + HALF : base + HEAD_DIM, :] = (b * cs - a * sn).astype(BF16)

    for at, h in enumerate(picked):
        base = (h - first) * HEAD_DIM
        turn_back(dq[at * HEAD_DIM : (at + 1) * HEAD_DIM, :] * HEAD_DIM**-0.5, base)
        part = slice(at * HEAD_DIM, (at + 1) * HEAD_DIM)
        turn_back(dk[part, :], stride + base)
        base += 2 * stride
        grad_proj[base : base + HEAD_DIM, :] = dv[part, :].astype(BF16)
    if before is not None:
        had = before.shape[0] // 3
        for c in range(3):
            grad_proj[c * stride : c * stride + had, :] = before[c * had : (c + 1) * had, :]
    for s, partial_out in enumerate(partials):
        span = pl.ds(pl.multiple_of((me ^ s) * block, block), block)
        partial_out[...] = dot(grad_proj[:, span], weight[...], TN).astype(BF16)


def four(parts):
    return (parts[0], parts[2].at[0], parts[1], parts[2].at[1])


def middle_kernel(row, hid, *rest):
    attended, weights = four(rest[:3]), rest[3:7]
    vectors, cot, middle, second, pair = rest[7:12]
    width = vectors.shape[1]
    branch = vectors[2:3, :]
    for a, w in zip(attended, weights):
        branch = branch + dot(a[...], w[...], TN)
    values = hid[:, row * width : (row + 1) * width].astype(F32) + branch
    middle[...] = values
    scaled, _ = normalize(values)
    low = (scaled * vectors[3:4, :] + vectors[4:5, :]).astype(BF16)
    second[...] = low
    pair[0] = low
    pair[1] = cot[...]


def gelu_parts(h):
    size = jnp.abs(h)
    t = 1.0 / (1.0 + size * (0.3275911 * 0.5**0.5))
    density = jnp.exp(h * h * -0.5)
    poly = t * (
        0.254829592
        + t * (-0.284496736 + t * (1.421413741 + t * (-1.453152027 + t * 1.061405429)))
    )
    tail = 0.5 * poly * density
    below = jnp.where(h < 0, tail, 1.0 - tail)
    return below, density * 0.3989422804014327


def feed_kernel(second, cot, w_in, w_out, vectors, passed_in, passed_out, passed_vectors, act, grad_pre, *outs):
    if cot is None:
        second, cot = second.at[0], second.at[1]
    units = w_in.shape[1]
    width = w_in.shape[0]
    step = 256
    tokens = second[...]
    portion = cot[...]
    for side, lines in enumerate((vectors, passed_vectors)):
        for u in range(0, units, step):
            cols = slice(u, u + step)
            spot = slice(side * units + u, side * units + u + step)
            into = passed_in[:, cols] if side else w_in[:, cols]
            down = passed_out[u : u + step, :] if side else w_out[cols, :]
            pre = dot(tokens, into) + lines[6:7, cols]
            below, density = gelu_parts(pre)
            act[:, spot] = (pre * below).astype(BF16)
            grad_act = dot(portion, down, NT)
            grad_pre[:, spot] = (grad_act * (below + pre * density)).astype(BF16)
    out = dot(act[:, :units], w_out[...]) + dot(act[:, units:], passed_out[...])
    grad = dot(grad_pre[:, :units], w_in[...], NT) + dot(
        grad_pre[:, units:], passed_in[...], NT
    )
    half = out.shape[0] // 2
    outs[0][...] = out.astype(BF16)
    low = grad.astype(BF16)
    if len(outs) == 2:
        outs[1][...] = low
    else:
        outs[1][...] = low[:half]
        outs[2][...] = low[half:]


def feed_weights_kernel(count, *refs):
    near = count // 2
    seconds, cots, pairs = refs[:near], refs[near:count], refs[count : count + near]
    seconds = [*seconds, *(pair.at[0] for pair in pairs)]
    cots = [*cots, *(pair.at[1] for pair in pairs)]
    refs = refs[count + near :]
    acts, pres = refs[:count], refs[count : 2 * count]
    own, passed, own_bias, passed_bias, down, up = refs[2 * count :]
    units = own.shape[1]
    for k in range(count):
        pre = pres[k][...]
        part_down = dot(acts[k][...], cots[k][...], TN)
        part_up = dot(seconds[k][...], pre, TN)
        sums = jnp.sum(pre.astype(F32), axis=0, keepdims=True)
        if k == 0:
            down[...] = part_down
            up[...] = part_up
            added = sums
        else:
            down[...] += part_down
            up[...] += part_up
            added += sums
    own_bias[...] = added[:, :units]
    passed_bias[...] = jnp.broadcast_to(added[:, units:], passed_bias.shape)
    own[0] = down[:units, :].astype(BF16)
    own[1] = up[:, :units].astype(BF16)
    passed[0] = down[units:, :].astype(BF16)
    passed[1] = up[:, units:].astype(BF16)


def feed_slots_kernel(own, passed, own_bias, passed_bias, bias, *outs):
    piece = outs[0].shape[0] // 2
    spot = where_am_i()[2]
    bias[...] = own_bias[...] + passed_bias[0:1, :]
    for s, out in enumerate(outs):
        span = pl.ds(pl.multiple_of((spot ^ s) * piece, piece), piece)
        for bank in range(2):
            total = own[bank, span, :].astype(F32) + passed[bank, span, :].astype(F32)
            out[bank * piece : (bank + 1) * piece, :] = total.astype(BF16)


def middle_back_kernel(chips, own, *rest):
    chip, rest = rest[:chips], rest[chips:]
    middle, cot, vectors = rest[:3]
    weights, outs = rest[3:7], rest[7:]
    grad_middle, grad_branch, sums = outs[0], outs[1], outs[5]
    heads = (outs[2], outs[3], outs[4].at[0], outs[4].at[1])
    across = jnp.concatenate([part[...] for part in chip], axis=0) if chips > 1 else chip[0][...]
    grad_second = own[...].astype(F32) + across.astype(F32)
    scaled, inverse = normalize(middle[...])
    grad_out = cot[...].astype(F32)
    total = grad_out + normalize_back(grad_second, scaled, inverse, vectors[3:4, :])
    low = total.astype(BF16)
    grad_middle[...] = total
    grad_branch[...] = low
    for w, out in zip(weights, heads):
        out[...] = dot(w[...], low, NT).astype(BF16)
    sums[0:1, :] = jnp.sum(grad_second * scaled, axis=0, keepdims=True)
    sums[1:2, :] = jnp.sum(grad_second, axis=0, keepdims=True)
    sums[2:3, :] = jnp.sum(grad_out, axis=0, keepdims=True)
    sums[3:4, :] = jnp.sum(low.astype(F32), axis=0, keepdims=True)
    sums[4:, :] = jnp.zeros((4, sums.shape[1]), F32)


def out_weight_kernel(rows, *refs):
    attended, grads, outs = refs[: 3 * rows], refs[3 * rows : 4 * rows], refs[4 * rows :]
    attended = [four(attended[3 * r : 3 * r + 3]) for r in range(rows)]
    own, across, sent = outs
    for s, out in enumerate((own, sent.at[0], across, sent.at[1])):
        total = dot(attended[0][s][...], grads[0][...])
        for r in range(1, rows):
            total = total + dot(attended[r][s][...], grads[r][...])
        out[...] = total.astype(BF16)


def project_weights_kernel(rows, *refs):
    projs, near, refs = refs[:rows], refs[rows], refs[rows + 1 :]
    beside, far, refs = refs[: 2 * rows], refs[2 * rows : 4 * rows], refs[4 * rows :]
    own, swapped, chip = refs[:3]
    outs, (bias, total) = refs[3:7], refs[7:]
    block = near.shape[1]
    me, _, spot = where_am_i()
    size = projs[0].shape[0]
    local = size // 3
    ones = jnp.ones((8, projs[0].shape[1]), BF16)
    bias[...] = jnp.zeros_like(bias)
    for c in range(3):
        part = slice(c * local, (c + 1) * local)
        sums = dot(ones, projs[0][part, :], NT)
        for r in range(1, rows):
            sums += dot(ones, projs[r][part, :], NT)
        bias[:, 256 * c : 256 * c + local] = sums
    for r in range(rows):
        for s in range(4):
            span = pl.ds(pl.multiple_of((me ^ s) * block, block), block)
            if s == 0:
                tokens = near[r]
            elif s == 1:
                tokens = jnp.concatenate([beside[2 * r][...], beside[2 * r + 1][...]], axis=0)
            else:
                tokens = far[2 * r + s - 2][...]
            product = dot(projs[r][:, span], tokens)
            if r + s == 0:
                total[:size, :] = product
            else:
                total[:size, :] += product
    total[size:, :] = own[...].astype(F32) + swapped[0].astype(F32) + chip[...].astype(F32)
    piece = outs[0].shape[0]
    for s, out in enumerate(outs):
        at = pl.multiple_of((spot ^ s) * piece, piece)
        out[...] = total[pl.ds(at, piece), :].astype(BF16)


def finish_kernel(*refs):
    spot = where_am_i()[2]
    slots, outs = refs[:4], refs[4:]
    for s, slot in enumerate(slots):
        piece = slot.shape[0] // 2
        span = pl.ds(pl.multiple_of((spot ^ s) * piece, piece), piece)
        for k, out in enumerate(outs):
            out[span, :] = slot[k * piece : (k + 1) * piece, :].astype(F32)


def finish_project_kernel(*refs):
    spot = where_am_i()[2]
    slots, (big, small) = refs[:4], refs[4:]
    piece = small.shape[0]
    for s, slot in enumerate(slots):
        at = spot ^ s

        @pl.when(at < 3)
        def _():
            big[pl.ds(pl.multiple_of(at * piece, piece), piece), :] = slot[...].astype(F32)

        @pl.when(at == 3)
        def _():
            small[...] = slot[...].astype(F32)


def first_back_kernel(row, kept, chip, hid, grad_middle, vectors, grad_in, sums):
    width = vectors.shape[1]
    grad_first = sum(part[...].astype(F32) for part in kept) + chip[...].astype(F32)
    scaled, inverse = normalize(hid[:, row * width : (row + 1) * width].astype(F32))
    grad_in[...] = grad_middle[...] + normalize_back(grad_first, scaled, inverse, vectors[0:1, :])
    sums[0:1, :] = jnp.sum(grad_first * scaled, axis=0, keepdims=True)
    sums[1:2, :] = jnp.sum(grad_first, axis=0, keepdims=True)
    sums[2:, :] = jnp.zeros((6, width), F32)


def small_kernel(firsts, middles, out):
    rows = len(firsts)
    out[...] = jnp.zeros_like(out)
    out[0:2, :] = sum(ref[0:2, :] for ref in firsts)
    out[2:6, :] = sum(ref[0:4, :] for ref in middles)


def small_extra_kernel(one, two, in_bias, proj_bias, out):
    out[...] = one[...] + two[...]
    out[6:7, :] = in_bias[...]
    out[7:8, :] = proj_bias[0:1, :]


def finish_small_kernel(one, two, *outs):
    *lines, proj_bias, total = outs
    total[...] = one[...] + two[...]
    width = total.shape[1]
    for k, line in enumerate(lines):
        line[...] = total[k : k + 1, :].reshape(width)
    local = proj_bias.shape[1]
    for c in range(3):
        proj_bias[c : c + 1, :] = total[7:8, 256 * c : 256 * c + local]


def block_out_kernel(own, middle, across, vectors, out):
    total = own[...].astype(F32) + across[...].astype(F32)
    out[...] = (middle[...] + (total + vectors[5:6, :])).astype(BF16)


def swap(values, axis, size, bit):
    return lax.ppermute(values, axis, [(i, i ^ bit) for i in range(size)])


def core_swap(values):
    return swap(values, "tp", 4, 1)


def chip_swap(values):
    return swap(values, "tp", 4, 2)


class Bank:
    def __init__(self, line, slots, size):
        self.line, self.own, self.size = line, slots[0], size
        self.moved = [swap(slots[s], "dp", size, s) for s in range(1, 4)]
        self.bit = 2

    def advance(self):
        (self.own,) = self.line.add([(self.own,), *((v,) for v in self.moved)])
        self.bit *= 2
        if self.bit < self.size:
            self.moved = [swap(self.own, "dp", self.size, self.bit)]
            return
        self.slots = [self.own] + [swap(self.own, "dp", self.size, s) for s in range(1, 4)]

    @property
    def done(self):
        return self.bit >= self.size


def on_device(
    size,
    hidden_in,
    segment_ids,
    cotangent,
    norm1_gain,
    norm1_bias,
    qkv_weight,
    qkv_bias,
    out_weight,
    out_bias,
    norm2_gain,
    norm2_bias,
    ffn_in_weight,
    ffn_in_bias,
    ffn_out_weight,
    ffn_out_bias,
):
    block, rows, width = hidden_in.shape
    length = segment_ids.shape[1]
    local = qkv_weight.shape[2]
    heads = local // HEAD_DIM
    units = ffn_in_weight.shape[1]
    line = Line()
    each, last = range(rows), rows - 1
    full, half, both = shape((block, width)), shape((block // 2, width)), shape((rows, block, width))
    hid = hidden_in.reshape(block, rows * width)
    cots = cotangent.reshape(block, rows * width)
    vector, anywhere = pl.BlockSpec(memory_space=pltpu.VMEM), pl.BlockSpec(memory_space=pltpu.HBM)
    params = [norm1_gain, norm1_bias, out_bias, norm2_gain, norm2_bias, ffn_out_bias, ffn_in_bias]
    vectors, first, alone, *parts = line.run(
        partial(first_norm_kernel, rows, width),
        "first_norm",
        [],
        [hid, *params],
        [shape((8, width), F32), both, full] + [half] * (2 * rows),
        [pltpu.VMEM((width,), BF16)] * 7 + [pltpu.SemaphoreType.DMA((7,))],
        inputs=[vector] + [anywhere] * 7,
    )
    first_across = [chip_swap(alone)]
    first_beside = [core_swap(v) for v in parts]
    passed_in, passed_out = core_swap(ffn_in_weight), core_swap(ffn_out_weight)
    passed_vectors = core_swap(vectors)

    rates = np.power(10000.0, -2.0 * np.arange(HALF) / HEAD_DIM).astype(np.float32)
    windows, marks, waves, proj_bias = line.run(
        partial(table_kernel, block),
        "tables",
        [],
        [segment_ids, jnp.asarray(rates.reshape(HALF, 1)), qkv_bias],
        [
            shape((rows, 2, 16, length)),
            shape((rows, 2, HALF, length), F32),
            shape((3 * local, 1), F32),
        ],
        numbers=[shape((rows * 2 * (length // block),), jnp.int32)],
    )
    proj_weight = jnp.transpose(qkv_weight, (0, 2, 1)).reshape(3 * local, width)

    def project(far, picked, one, *two):
        return line.run(
            partial(project_kernel, far, picked),
            "project",
            [],
            [one, *two, proj_weight, proj_bias, waves],
            [shape((len(picked), 3 * local, 2 * block))],
        )[0]

    def attend(r):
        *outs, log_norm = line.run(
            partial(attend_kernel, r),
            "attend",
            [windows],
            [near, far[r], marks],
            [shape((local, block))] * 2
            + [shape((2, local, block)), shape((8, length), F32)],
            [
                pltpu.VMEM((heads * KEY_ROWS, length), BF16),
                pltpu.VMEM((heads, length, KEY_ROWS), BF16),
                pltpu.VMEM((local, length), BF16),
                pltpu.VMEM((local, length), BF16),
            ],
            vmem=14,
        )
        logs.append(log_norm)
        return [outs[0], outs[1], chip_swap(outs[2])]

    def feed(*tokens):
        tokens = list(tokens)

        def body(*refs):
            feed_kernel(*(refs if len(tokens) == 2 else (refs[0], None, *refs[1:])))

        act, pre, *outs = line.run(
            body,
            "feed",
            [],
            tokens + [ffn_in_weight, ffn_out_weight, vectors, passed_in, passed_out, passed_vectors],
            [shape((block, 2 * units))] * 2 + [full, full],
            vmem=12,
        )
        acts.append(act)
        pres.append(pre)
        return outs

    def pick(values, r):
        def body(values, out):
            out[...] = values[r]

        return line.run(body, "pick", [], [values], [shape(values.shape[1:])])[0]

    near = project(0, tuple(each), first, *first_beside)
    cots = line.run(partial(split_kernel, width), "split", [], [cots], [full] * rows)
    far, far_slots = [], []
    logs, attended = [], []
    for r in each:
        (arrived,) = line.keep(first_across[r])
        far_slots += [arrived, core_swap(arrived)]
        if r < last:
            first_across.append(chip_swap(pick(first, r + 1)))
        if r == last:
            (ready,) = line.keep(out_weight)
            out_across = chip_swap(ready)
            out_beside = core_swap(ready)
        far.append(project(1, (r,), *far_slots[-2:]))
        attended.append(attend(r))

    middles, seconds, pairs = [], [], []
    acts, pres, feeds, feed_grads = [], [], [], []
    for r in each:
        if r == 0:
            (out_far,) = line.keep(out_across)
            out_slots = [out_weight, out_beside, out_far, core_swap(out_far)]
        one, two = line.split(attended[r][1], attended[r][2])
        attended[r][1:] = [one, two]
        middle, second, pair = line.run(
            partial(middle_kernel, r),
            "middle",
            [],
            [hid, *attended[r], *out_slots, vectors, cots[r]],
            [shape((block, width), F32), full, shape((2, block, width))],
        )
        middles.append(middle)
        seconds.append(second)
        pairs.append(chip_swap(pair))
        out, grad = feed(second, cots[r])
        feeds.append([out])
        feed_grads.append([grad])
    for r in each:
        out, grad = feed(pairs[r])
        feeds[r].append(out)
        feed_grads[r].append(chip_swap(grad))

    grad_middles, grad_branches, head_grads, norm_sums = [], [], [], []

    def middle_back(r):
        own, *across = feed_grads[r]
        grad_middle, grad_branch, *parts, sums = line.run(
            partial(middle_back_kernel, len(across)),
            "middle_back",
            [],
            [own, *across, middles[r], cots[r], vectors, *out_slots],
            [shape((block, width), F32), full]
            + [shape((local, block))] * 2
            + [shape((2, local, block)), shape((8, width), F32)],
        )
        grad_middles.append(grad_middle)
        grad_branches.append(grad_branch)
        head_grads.append([parts[0], parts[1], chip_swap(parts[2])])
        norm_sums.append(sums)

    own_sums, passed_sums, own_bias, passed_bias = line.run(
        partial(feed_weights_kernel, 2 * rows),
        "feed_weights",
        [],
        [*seconds, *cots, *pairs, *acts, *pres],
        [
            shape((2, units, width)),
            shape((2, units, width)),
            shape((1, units), F32),
            shape((8, units), F32),
        ],
        [pltpu.VMEM((2 * units, width), F32), pltpu.VMEM((width, 2 * units), F32)],
        vmem=22,
    )
    for r in range(last):
        middle_back(r)
    (passed_sums,) = line.keep(passed_sums)
    passed_sums = core_swap(passed_sums)
    passed_bias = core_swap(passed_bias)
    in_bias_sum, *slots = line.run(
        feed_slots_kernel,
        "feed_slots",
        [],
        [own_sums, passed_sums, own_bias, passed_bias],
        [shape((1, units), F32)] + [shape((units // 2, width))] * 4,
    )
    feed_bank = Bank(line, slots, size)
    middle_back(last)
    head_grads[0][1:] = line.split(*head_grads[0][1:])
    blocks_across = [chip_swap(line.keep(feeds[r][1])[0]) for r in range(last)]

    def block_out(r):
        return line.run(
            block_out_kernel,
            "block_out",
            [],
            [feeds[r][0], middles[r], blocks_across[r], vectors],
            [full],
        )[0]

    def attend_back(r, picked, before):
        final = picked[-1] == heads - 1
        some = len(picked)
        made = local if final else some * HEAD_DIM
        grad_proj, *parts = line.run(
            partial(attend_back_kernel, r, picked),
            "attend_back",
            [windows],
            [near, far[r], marks, logs[r], waves, *head_grads[r]]
            + before
            + ([proj_weight] if final else []),
            [shape((3 * made, length))]
            + ([full, full] if final else [])
            + ([full, full] if final and r == last else [])
            + ([shape((2, block, width))] if final and r < last else []),
            [
                pltpu.VMEM((some * KEY_ROWS, length), BF16),
                pltpu.VMEM((some, length, KEY_ROWS), BF16),
                pltpu.VMEM((some * HEAD_DIM, length), BF16),
                pltpu.VMEM((some, length, HEAD_DIM), BF16),
                pltpu.VMEM((some * HEAD_DIM, length), BF16),
                pltpu.VMEM((some * HEAD_DIM, length), F32),
                pltpu.VMEM((some * HEAD_DIM, length), F32),
                pltpu.VMEM((some * HEAD_DIM, length), F32),
            ],
            vmem=20,
        )
        if not final:
            return [grad_proj]
        projs.append(grad_proj)
        first_grads.append([parts[0], parts[1], *(core_swap(v) for v in parts[2:])])

    projs, first_grads, kepts, backs = [], [], [], []
    for r in each:
        if r > 0:
            head_grads[r][1:] = line.split(*head_grads[r][1:])
        if r == last:
            feed_bank.advance()
            blocks_out = [block_out(k) for k in range(last)]
            out_parts = line.run(
                partial(out_weight_kernel, rows),
                "out_weight",
                [],
                [*sum(attended, []), *grad_branches],
                [shape((local, width))] * 2 + [shape((2, local, width))],
            )
            out_beside = core_swap(out_parts[2])
            (back,) = line.add([(out_parts[1],), (out_beside, 1)])
            out_sums = [out_parts[0], out_beside, chip_swap(back)]
            blocks_across.append(chip_swap(line.keep(feeds[last][1])[0]))
            for k in range(last):
                kept, back = line.add(
                    [(first_grads[k][0],), (first_grads[k][2], 0)],
                    [(first_grads[k][1],), (first_grads[k][2], 1)],
                )
                kepts.append([kept])
                backs.append(back)
        attend_back(r, tuple(range(heads)), [])
    grads_in, first_sums = [], []

    def first_back(r):
        grad_in, sums = line.run(
            lambda *refs: first_back_kernel(r, refs[: len(kepts[r])], *refs[len(kepts[r]) :]),
            "first_back",
            [],
            [*kepts[r], first_across_back[r], hid, grad_middles[r], vectors],
            [shape((block, width), F32), shape((8, width), F32)],
        )
        grads_in.append(grad_in)
        first_sums.append(sums)

    *slots, proj_bias_sum = line.run(
        partial(project_weights_kernel, rows),
        "project_weights",
        [],
        [*projs, first, *first_beside, *far_slots, *out_sums],
        [shape((local, width))] * 4 + [shape((8, width), F32)],
        [pltpu.VMEM((4 * local, width), F32)],
        vmem=10,
    )
    head_bank = Bank(line, slots, size)
    blocks_out.append(block_out(last))
    blocks_out = jnp.stack(blocks_out, axis=1)
    first_across_back = [chip_swap(v) for v in line.keep(*backs)]
    own, across, beside, sent = first_grads[last]
    kepts.append([own, beside])
    (back,) = line.add([(across,), (sent,)])
    first_across_back.append(chip_swap(back))
    while not feed_bank.done:
        feed_bank.advance()
    head_bank.advance()
    for r in each:
        first_back(r)
    input_grad = jnp.stack(grads_in, axis=1)
    (small,) = line.run(
        lambda *refs: small_kernel(refs[:rows], refs[rows : 2 * rows], refs[2 * rows]),
        "small",
        [],
        [*first_sums, *norm_sums],
        [shape((8, width), F32)],
    )
    (small,) = line.add([(small,), (core_swap(small),)])
    (small,) = line.run(
        small_extra_kernel,
        "small_extra",
        [],
        [small, chip_swap(small), in_bias_sum, proj_bias_sum],
        [shape((8, width), F32)],
    )
    while not head_bank.done:
        head_bank.advance()
    bit = 1
    while 2 * bit < size:
        (small,) = line.add([(small,), (swap(small, "dp", size, bit),)])
        bit *= 2
    *lines, grad_proj_bias = line.run(
        finish_small_kernel,
        "finish_small",
        [],
        [small, swap(small, "dp", size, bit)],
        [shape((width,), F32)] * 7 + [shape((3, local), F32)],
        [pltpu.VMEM((8, width), F32)],
    )
    grad_down_weight, grad_in_weight = line.run(
        finish_kernel,
        "finish",
        [],
        feed_bank.slots,
        [shape((units, width), F32), shape((width, units), F32)],
    )
    grad_qkv_weight, grad_out_weight = line.run(
        finish_project_kernel,
        "finish_project",
        [],
        head_bank.slots,
        [shape((3 * local, width), F32), shape((local, width), F32)],
    )
    grad_qkv_weight = jnp.transpose(grad_qkv_weight.reshape(3, local, width), (0, 2, 1))
    return (
        blocks_out,
        input_grad,
        lines[0],
        lines[1],
        grad_qkv_weight,
        grad_proj_bias,
        grad_out_weight,
        lines[5],
        lines[2],
        lines[3],
        grad_in_weight,
        lines[6],
        grad_down_weight,
        lines[4],
    )


def solution(mesh):
    sharded = P("tp", "dp", None)
    return jax.shard_map(
        partial(on_device, mesh.shape["dp"]),
        mesh=mesh,
        in_specs=(
            sharded,
            P("dp", None),
            sharded,
            P(),
            P(),
            P(None, None, "tp"),
            P(None, "tp"),
            P("tp", None),
            P(),
            P(),
            P(),
            P(None, "tp"),
            P("tp"),
            P("tp", None),
            P(),
        ),
        out_specs=(
            sharded,
            sharded,
            P(),
            P(),
            P(None, None, "tp"),
            P(None, "tp"),
            P("tp", None),
            P(),
            P(),
            P(),
            P(None, "tp"),
            P("tp"),
            P("tp", None),
            P(),
        ),
        check_vma=False,
    )
```

```python
from functools import partial

import jax
import jax.numpy as jnp
import numpy as np
from jax import lax
from jax.experimental import pallas as pl
from jax.experimental.pallas import tpu as pltpu
from jax.sharding import PartitionSpec as P

HEAD_DIM = 64
HALF = HEAD_DIM // 2
KEY_ROWS = 128
EPSILON = 1e-05
APART = -1e30
F32 = jnp.float32
BF16 = jnp.bfloat16

NN = (((1,), (0,)), ((), ()))
NT = (((1,), (1,)), ((), ()))
TN = (((0,), (0,)), ((), ()))


def dot(a, b, dims=NN):
    return lax.dot_general(a, b, dims, preferred_element_type=F32)


def shape(dims, dtype=BF16):
    return jax.ShapeDtypeStruct(dims, dtype)


class Line:
    def __init__(self):
        self.tile = None

    def run(
        self, body, name, scalars, arrays, outs, scratch=(), vmem=8, inputs=None, numbers=(), places=None
    ):
        before = [] if self.tile is None else [self.tile]
        count, extra, made = len(scalars) + len(arrays), len(before), len(outs)
        made += len(numbers)

        def whole(*refs):
            tile = refs[count + extra + made]
            tile[...] = jnp.zeros_like(tile)
            body(
                *refs[:count],
                *refs[count + extra : count + extra + made],
                *refs[count + extra + made + 1 :],
            )

        vector = pl.BlockSpec(memory_space=pltpu.VMEM)
        scalar = pl.BlockSpec(memory_space=pltpu.SMEM)
        *results, self.tile = pl.pallas_call(
            whole,
            out_shape=(*numbers, *outs, shape((8, 128), F32)),
            in_specs=[scalar] * len(scalars)
            + (inputs or [vector] * len(arrays))
            + [vector] * extra,
            out_specs=(scalar,) * len(numbers)
            + (tuple(places) if places else (vector,) * len(outs))
            + (vector,),
            scratch_shapes=list(scratch),
            compiler_params=pltpu.CompilerParams(vmem_limit_bytes=vmem * 1024 * 1024),
            cost_estimate=pl.CostEstimate(flops=1, bytes_accessed=1, transcendentals=0),
            name=name,
        )(*scalars, *arrays, *before)
        return results

    def keep(self, *arrays):
        def body(*refs):
            for k in range(len(arrays)):
                refs[len(arrays) + k][...] = refs[k][...]

        return self.run(body, "keep", [], arrays, [shape(v.shape, v.dtype) for v in arrays])

    def split(self, near, pair):
        def body(near, pair, one, two):
            one[...] = pair[0]
            two[0] = near[...]
            two[1] = pair[1]

        made = [shape(near.shape), shape((2, *near.shape))]
        one, two = self.run(body, "split", [], [near, pair], made)
        return [one, core_swap(two)]

    def merge(self, one, two, cuts):
        def body(one, two, *outs):
            total = one[...].astype(F32) + two[...].astype(F32)
            size = total.shape[0] // cuts
            for k, out in enumerate(outs):
                out[...] = total[k * size : (k + 1) * size].astype(out.dtype)

        made = [shape((one.shape[0] // cuts, *one.shape[1:]))] * cuts
        return self.run(body, "merge", [], [one, two], made)

    def join(self, *arrays):
        def body(*refs):
            for k in range(len(arrays)):
                refs[len(arrays)][k] = refs[k][...]

        first = arrays[0]
        made = [shape((len(arrays), *first.shape), first.dtype)]
        return self.run(body, "join", [], arrays, made, vmem=8)[0]

    def add_rows(self, ones, twos):
        count = len(ones)

        def body(*refs):
            for r in range(count):
                total = refs[r][...].astype(F32) + refs[count + r][1].astype(F32)
                refs[2 * count][r] = total.astype(BF16)

        made = [shape((count, *ones[0].shape))]
        return self.run(body, "add_rows", [], [*ones, *twos], made)[0]

    def add_pair(self, one, two):
        def body(a, b, c, d, out):
            out[0] = (a[...].astype(F32) + b[...].astype(F32)).astype(out.dtype)
            out[1] = (c[...].astype(F32) + d[...].astype(F32)).astype(out.dtype)

        made = [shape((2, *one[0].shape), one[0].dtype)]
        return self.run(body, "add_pair", [], [*one, *two], made)[0]

    def add(self, *sums):
        arrays = [term[0] for terms in sums for term in terms]
        parts = [[term[1:] for term in terms] for terms in sums]
        outs = []
        for terms in sums:
            first = terms[0][0]
            outs.append(shape(first.shape[len(terms[0]) - 1 :], first.dtype))

        def body(*refs):
            at = 0
            for k, terms in enumerate(parts):
                total = None
                for index in terms:
                    value = refs[at][index[0]] if index else refs[at][...]
                    value = value.astype(F32)
                    total = value if total is None else total + value
                    at += 1
                out = refs[len(arrays) + k]
                out[...] = total.astype(out.dtype)

        return self.run(body, "add", [], arrays, outs)


def normalize(values):
    average = jnp.mean(values, axis=-1, keepdims=True)
    centered = values - average
    variance = jnp.mean(centered * centered, axis=-1, keepdims=True)
    inverse = lax.rsqrt(variance + EPSILON)
    return centered * inverse, inverse


def normalize_back(gradient, scaled, inverse, gain):
    grad_scaled = gradient * gain
    return inverse * (
        grad_scaled
        - jnp.mean(grad_scaled, axis=-1, keepdims=True)
        - scaled * jnp.mean(grad_scaled * scaled, axis=-1, keepdims=True)
    )


def where_am_i():
    me = lax.axis_index("tp")
    return me, me // 2, lax.axis_index("dp") & 3


def first_norm_kernel(rows, width, hid, *refs):
    lines, (vectors, first, alone) = refs[:7], refs[7:10]
    parts, lands, sems = refs[10 : 10 + 2 * rows], refs[10 + 2 * rows : 17 + 2 * rows], refs[-1]
    copies = [
        pltpu.make_async_copy(line, land, sems.at[k])
        for k, (line, land) in enumerate(zip(lines, lands))
    ]
    for copy in copies:
        copy.start()
    normed = []
    for r in range(rows):
        values = hid[:, r * width : (r + 1) * width].astype(F32)
        normed.append(normalize(values)[0])
    for copy in copies:
        copy.wait()
    for k, land in enumerate(lands):
        vectors[k : k + 1, :] = land[...].astype(F32).reshape(1, width)
    vectors[7:8, :] = jnp.zeros((1, width), F32)
    for r in range(rows):
        low = (normed[r] * vectors[0:1, :] + vectors[1:2, :]).astype(BF16)
        first[r] = low
        half = low.shape[0] // 2
        parts[2 * r][...] = low[:half]
        parts[2 * r + 1][...] = low[half:]
        if r == 0:
            alone[...] = low


def table_kernel(block, segments, rates, bias, windows, marks, waves, column):
    rows, length = segments.shape
    ids = lax.broadcasted_iota(jnp.int32, (16, length), 0)
    spots = lax.broadcasted_iota(jnp.int32, (1, length), 1)
    for r in range(rows):
        row = segments[r : r + 1, :]
        same = row == ids
        before = jnp.sum((row < ids).astype(F32), axis=1, keepdims=True)
        begins = jnp.sum(jnp.where(same, before, 0.0), axis=0, keepdims=True)
        ends = jnp.sum((row <= ids).astype(F32), axis=1, keepdims=True)
        closes = jnp.sum(jnp.where(same, ends, 0.0), axis=0, keepdims=True)
        marks[r, 0] = same.astype(F32).astype(BF16)
        marks[r, 1] = jnp.where(same | (ids >= 8), 0.0, APART).astype(BF16)
        angles = rates[...] * (spots.astype(F32) - begins)
        waves[r, 0] = jnp.cos(angles)
        waves[r, 1] = jnp.sin(angles)
        blocks = length // block
        for q in range(blocks):
            inside = slice(q * block, (q + 1) * block)
            least = jnp.min(begins[:, inside]).astype(jnp.int32)
            past = jnp.max(closes[:, inside]).astype(jnp.int32)
            start = (least // 128) * 128
            count = (past - start + block - 1) // block
            windows[2 * blocks * r + q] = jnp.minimum(start, length - count * block)
            windows[2 * blocks * r + blocks + q] = count
    local = bias.shape[1]
    tall = jnp.concatenate([bias[...].astype(F32), jnp.zeros((5, local), F32)], axis=0)
    tall = jnp.transpose(tall)
    for c in range(3):
        column[c * local : (c + 1) * local, :] = tall[:, c : c + 1]


def split_kernel(width, whole, *outs):
    for r, out in enumerate(outs):
        out[...] = whole[:, r * width : (r + 1) * width]


def project_kernel(far, picked, one, *refs):
    two, (weight, bias, waves, out) = refs[:-4], refs[-4:]
    block = one.shape[-2]
    local = weight.shape[0] // 3
    me, chip, _ = where_am_i()
    half = chip ^ far
    for at, r in enumerate(picked):
        for k, tokens in enumerate((one, two)):
            spot = pl.multiple_of(((me & 1) ^ k) * block, block)
            span = pl.ds(spot, block)
            table = pl.ds(pl.multiple_of(half * (2 * block) + spot, block), block)
            if k == 0:
                values = tokens[at] if len(tokens.shape) == 3 else tokens[...]
            elif len(tokens) == 1:
                values = tokens[0][...]
            else:
                values = jnp.concatenate([tokens[2 * at][...], tokens[2 * at + 1][...]], axis=0)
            turned = dot(weight[...], values, NT) + bias[...]
            cs = waves[r, 0, :, table]
            sn = waves[r, 1, :, table]
            for c in range(2):
                for base in range(c * local, (c + 1) * local, HEAD_DIM):
                    a = turned[base : base + HALF]
                    b = turned[base + HALF : base + HEAD_DIM]
                    new_a = a * cs - b * sn
                    new_b = b * cs + a * sn
                    if c == 0:
                        new_a = new_a * HEAD_DIM**-0.5
                        new_b = new_b * HEAD_DIM**-0.5
                    out[at, base : base + HALF, span] = new_a.astype(BF16)
                    out[at, base + HALF : base + HEAD_DIM, span] = new_b.astype(BF16)
            out[at, 2 * local :, span] = turned[2 * local :].astype(BF16)


def turn_over(values):
    return jnp.transpose(values)


def sides(r, near, far):
    chip = where_am_i()[1]
    width = near.shape[-1]
    return [
        (source, pl.ds(pl.multiple_of(at, width), width))
        for source, at in ((near.at[r], chip * width), (far.at[0], (1 - chip) * width))
    ]


def lay_out(r, picked, near, far, marked, queries, keys):
    mine = marked[r, 0]
    width = near.shape[-1]
    local = near.shape[1] // 3
    marks = mine.shape[0]
    for source, span in sides(r, near, far):
        for at, h in enumerate(picked):
            queries[at * KEY_ROWS : at * KEY_ROWS + HEAD_DIM, span] = source[
                h * HEAD_DIM : (h + 1) * HEAD_DIM, :
            ]
            column = jnp.concatenate(
                [
                    source[local + h * HEAD_DIM : local + (h + 1) * HEAD_DIM, :],
                    marked[r, 1, :, span],
                    jnp.zeros((KEY_ROWS - HEAD_DIM - marks, width), BF16),
                ],
                axis=0,
            )
            keys[at, span, :] = turn_over(column)
    for at in range(len(picked)):
        base = at * KEY_ROWS + HEAD_DIM
        queries[base : base + marks, :] = mine
        queries[base + marks : (at + 1) * KEY_ROWS, :] = jnp.zeros(
            (KEY_ROWS - HEAD_DIM - marks, queries.shape[1]), BF16
        )


def attend_kernel(r, windows, near, far, marked, *rest):
    outs, (log_norm, queries, keys, values, attended) = rest[:3], rest[3:]
    block = near.shape[-1] // 2
    local = near.shape[1] // 3
    heads = local // HEAD_DIM
    me = where_am_i()[0]
    lay_out(r, range(heads), near, far, marked, queries, keys)
    for source, span in sides(r, near, far):
        values[:, span] = source[2 * local :, :]

    @pl.loop(0, 4)
    def _(quarter):
        span = pl.ds(pl.multiple_of(quarter * block, block), block)
        start = pl.multiple_of(windows[8 * r + quarter], 128)
        count = windows[8 * r + 4 + quarter]

        def work(blocks):
            window = pl.ds(start, blocks * block)

            @pl.loop(0, heads)
            def _(h):
                part = pl.ds(pl.multiple_of(h * HEAD_DIM, HEAD_DIM), HEAD_DIM)
                rows = pl.ds(pl.multiple_of(h * KEY_ROWS, KEY_ROWS), KEY_ROWS)
                scores = dot(keys[h, window, :], queries[rows, span])
                peak = jnp.max(scores, axis=0, keepdims=True)
                weights = jnp.exp(scores - peak)
                total = jnp.sum(weights, axis=0, keepdims=True)
                out = dot(values[part, window], weights.astype(BF16))
                attended[part, span] = (out * (1.0 / total)).astype(BF16)
                log_norm[pl.ds(h, 1), span] = peak + jnp.log(total)

        for blocks in range(1, 5):
            pl.when(count == blocks)(partial(work, blocks))

    for s, out in enumerate((outs[0], outs[1], outs[2].at[0], outs[2].at[1])):
        out[...] = attended[:, pl.ds(pl.multiple_of((me ^ s) * block, block), block)]


def attend_back_kernel(r, picked, windows, near, far, marked, log_norm, waves, *rest):
    grads = (rest[0], rest[2].at[0], rest[1], rest[2].at[1])
    scratch, rest = rest[-8:], rest[3:-8]
    queries, keys, key_rows, value_cols, grad_rows, dk, dv, dq = scratch
    block = near.shape[-1] // 2
    local = near.shape[1] // 3
    heads = local // HEAD_DIM
    me = where_am_i()[0]
    if len(rest) == 1:
        before, weight, grad_proj, partials = None, None, rest[0], ()
    else:
        before = rest[0] if rest[0].shape[0] < rest[1].shape[0] else None
        weight, grad_proj, own, across, *sent = rest[1:] if before is not None else rest
        if len(sent) == 1:
            sent = (sent[0].at[0], sent[0].at[1])
        partials = (own, sent[0], across, sent[1])
    stride = grad_proj.shape[0] // 3
    first = picked[0] if weight is None else 0
    lay_out(r, picked, near, far, marked, queries, keys)
    for source, span in sides(r, near, far):
        for at, h in enumerate(picked):
            part = slice(at * HEAD_DIM, (at + 1) * HEAD_DIM)
            key_rows[part, span] = source[local + h * HEAD_DIM : local + (h + 1) * HEAD_DIM, :]
            value_cols[at, span, :] = turn_over(
                source[2 * local + h * HEAD_DIM : 2 * local + (h + 1) * HEAD_DIM, :]
            )
    for s, grad in enumerate(grads):
        span = pl.ds(pl.multiple_of((me ^ s) * block, block), block)
        for at, h in enumerate(picked):
            rows = grad[h * HEAD_DIM : (h + 1) * HEAD_DIM, :]
            grad_rows[at * HEAD_DIM : (at + 1) * HEAD_DIM, span] = rows
    dk[...] = jnp.zeros_like(dk)
    dv[...] = jnp.zeros_like(dv)

    @pl.loop(0, 4)
    def _(quarter):
        span = pl.ds(pl.multiple_of(quarter * block, block), block)
        start = pl.multiple_of(windows[8 * r + quarter], 128)
        count = windows[8 * r + 4 + quarter]

        def work(blocks):
            window = pl.ds(start, blocks * block)
            for at, h in enumerate(picked):
                part = slice(at * HEAD_DIM, (at + 1) * HEAD_DIM)
                scores = dot(
                    keys[at, window, :], queries[at * KEY_ROWS : (at + 1) * KEY_ROWS, span]
                )
                probs = jnp.exp(scores - log_norm[h : h + 1, span])
                grad_probs = dot(value_cols[at, window, :], grad_rows[part, span])
                inner = jnp.sum(probs * grad_probs, axis=0, keepdims=True)
                grad_scores = (probs * (grad_probs - inner)).astype(BF16)
                dv[part, window] += dot(grad_rows[part, span], probs.astype(BF16), NT)
                asked = slice(at * KEY_ROWS, at * KEY_ROWS + HEAD_DIM)
                dk[part, window] += dot(queries[asked, span], grad_scores, NT)
                dq[part, span] = dot(key_rows[part, window], grad_scores)

        for blocks in range(1, 5):
            pl.when(count == blocks)(partial(work, blocks))

    cs = waves[r, 0]
    sn = waves[r, 1]

    def turn_back(rows, base):
        a = rows[:HALF]
        b = rows[HALF:]
        grad_proj[base : base + HALF, :] = (a * cs + b * sn).astype(BF16)
        grad_proj[base + HALF : base + HEAD_DIM, :] = (b * cs - a * sn).astype(BF16)

    for at, h in enumerate(picked):
        base = (h - first) * HEAD_DIM
        turn_back(dq[at * HEAD_DIM : (at + 1) * HEAD_DIM, :] * HEAD_DIM**-0.5, base)
        part = slice(at * HEAD_DIM, (at + 1) * HEAD_DIM)
        turn_back(dk[part, :], stride + base)
        base += 2 * stride
        grad_proj[base : base + HEAD_DIM, :] = dv[part, :].astype(BF16)
    if before is not None:
        had = before.shape[0] // 3
        for c in range(3):
            grad_proj[c * stride : c * stride + had, :] = before[c * had : (c + 1) * had, :]
    for s, partial_out in enumerate(partials):
        span = pl.ds(pl.multiple_of((me ^ s) * block, block), block)
        partial_out[...] = dot(grad_proj[:, span], weight[...], TN).astype(BF16)


def four(parts):
    return (parts[0], parts[2].at[0], parts[1], parts[2].at[1])


def middle_kernel(row, hid, *rest):
    attended, weights = four(rest[:3]), rest[3:7]
    vectors, cot, middle, second, pair = rest[7:12]
    width = vectors.shape[1]
    branch = vectors[2:3, :]
    for a, w in zip(attended, weights):
        branch = branch + dot(a[...], w[...], TN)
    values = hid[:, row * width : (row + 1) * width].astype(F32) + branch
    middle[...] = values
    scaled, _ = normalize(values)
    low = (scaled * vectors[3:4, :] + vectors[4:5, :]).astype(BF16)
    second[...] = low
    pair[0] = low
    pair[1] = cot[...]


def gelu_parts(h):
    size = jnp.abs(h)
    t = 1.0 / (1.0 + size * (0.3275911 * 0.5**0.5))
    density = jnp.exp(h * h * -0.5)
    poly = t * (
        0.254829592
        + t * (-0.284496736 + t * (1.421413741 + t * (-1.453152027 + t * 1.061405429)))
    )
    tail = 0.5 * poly * density
    below = jnp.where(h < 0, tail, 1.0 - tail)
    return below, density * 0.3989422804014327


def feed_kernel(second, cot, w_in, w_out, vectors, passed_in, passed_out, passed_vectors, act, grad_pre, *outs):
    if cot is None:
        second, cot = second.at[0], second.at[1]
    units = w_in.shape[1]
    width = w_in.shape[0]
    step = 256
    tokens = second[...]
    portion = cot[...]
    for side, lines in enumerate((vectors, passed_vectors)):
        for u in range(0, units, step):
            cols = slice(u, u + step)
            spot = slice(side * units + u, side * units + u + step)
            into = passed_in[:, cols] if side else w_in[:, cols]
            down = passed_out[u : u + step, :] if side else w_out[cols, :]
            pre = dot(tokens, into) + lines[6:7, cols]
            below, density = gelu_parts(pre)
            act[:, spot] = (pre * below).astype(BF16)
            grad_act = dot(portion, down, NT)
            grad_pre[:, spot] = (grad_act * (below + pre * density)).astype(BF16)
    out = dot(act[:, :units], w_out[...]) + dot(act[:, units:], passed_out[...])
    grad = dot(grad_pre[:, :units], w_in[...], NT) + dot(
        grad_pre[:, units:], passed_in[...], NT
    )
    half = out.shape[0] // 2
    outs[0][...] = out.astype(BF16)
    low = grad.astype(BF16)
    if len(outs) == 2:
        outs[1][...] = low
    else:
        outs[1][...] = low[:half]
        outs[2][...] = low[half:]


def feed_weights_kernel(count, *refs):
    near = count // 2
    seconds, cots, pairs = refs[:near], refs[near:count], refs[count : count + near]
    seconds = [*seconds, *(pair.at[0] for pair in pairs)]
    cots = [*cots, *(pair.at[1] for pair in pairs)]
    refs = refs[count + near :]
    acts, pres = refs[:count], refs[count : 2 * count]
    own, passed, own_bias, passed_bias, down, up = refs[2 * count :]
    units = own.shape[1]
    for k in range(count):
        pre = pres[k][...]
        part_down = dot(acts[k][...], cots[k][...], TN)
        part_up = dot(seconds[k][...], pre, TN)
        sums = jnp.sum(pre.astype(F32), axis=0, keepdims=True)
        if k == 0:
            down[...] = part_down
            up[...] = part_up
            added = sums
        else:
            down[...] += part_down
            up[...] += part_up
            added += sums
    own_bias[...] = added[:, :units]
    passed_bias[...] = jnp.broadcast_to(added[:, units:], passed_bias.shape)
    own[0] = down[:units, :].astype(BF16)
    own[1] = up[:, :units].astype(BF16)
    passed[0] = down[units:, :].astype(BF16)
    passed[1] = up[:, units:].astype(BF16)


def feed_slots_kernel(own, passed, own_bias, passed_bias, bias, *outs):
    piece = outs[0].shape[0] // 2
    spot = where_am_i()[2]
    bias[...] = own_bias[...] + passed_bias[0:1, :]
    for s, out in enumerate(outs):
        span = pl.ds(pl.multiple_of((spot ^ s) * piece, piece), piece)
        for bank in range(2):
            total = own[bank, span, :].astype(F32) + passed[bank, span, :].astype(F32)
            out[bank * piece : (bank + 1) * piece, :] = total.astype(BF16)


def middle_back_kernel(chips, own, *rest):
    chip, rest = rest[:chips], rest[chips:]
    middle, cot, vectors = rest[:3]
    weights, outs = rest[3:7], rest[7:]
    grad_middle, grad_branch, sums = outs[0], outs[1], outs[5]
    heads = (outs[2], outs[3], outs[4].at[0], outs[4].at[1])
    across = jnp.concatenate([part[...] for part in chip], axis=0) if chips > 1 else chip[0][...]
    grad_second = own[...].astype(F32) + across.astype(F32)
    scaled, inverse = normalize(middle[...])
    grad_out = cot[...].astype(F32)
    total = grad_out + normalize_back(grad_second, scaled, inverse, vectors[3:4, :])
    low = total.astype(BF16)
    grad_middle[...] = total
    grad_branch[...] = low
    for w, out in zip(weights, heads):
        out[...] = dot(w[...], low, NT).astype(BF16)
    sums[0:1, :] = jnp.sum(grad_second * scaled, axis=0, keepdims=True)
    sums[1:2, :] = jnp.sum(grad_second, axis=0, keepdims=True)
    sums[2:3, :] = jnp.sum(grad_out, axis=0, keepdims=True)
    sums[3:4, :] = jnp.sum(low.astype(F32), axis=0, keepdims=True)
    sums[4:, :] = jnp.zeros((4, sums.shape[1]), F32)


def out_weight_kernel(rows, *refs):
    attended, grads, outs = refs[: 3 * rows], refs[3 * rows : 4 * rows], refs[4 * rows :]
    attended = [four(attended[3 * r : 3 * r + 3]) for r in range(rows)]
    own, across, sent = outs
    for s, out in enumerate((own, sent.at[0], across, sent.at[1])):
        total = dot(attended[0][s][...], grads[0][...])
        for r in range(1, rows):
            total = total + dot(attended[r][s][...], grads[r][...])
        out[...] = total.astype(BF16)


def project_weights_kernel(rows, *refs):
    projs, near, refs = refs[:rows], refs[rows], refs[rows + 1 :]
    beside, far, refs = refs[: 2 * rows], refs[2 * rows : 4 * rows], refs[4 * rows :]
    own, swapped, chip = refs[:3]
    outs, (bias, total) = refs[3:7], refs[7:]
    block = near.shape[1]
    me, _, spot = where_am_i()
    size = projs[0].shape[0]
    local = size // 3
    ones = jnp.ones((8, projs[0].shape[1]), BF16)
    bias[...] = jnp.zeros_like(bias)
    for c in range(3):
        part = slice(c * local, (c + 1) * local)
        sums = dot(ones, projs[0][part, :], NT)
        for r in range(1, rows):
            sums += dot(ones, projs[r][part, :], NT)
        bias[:, 256 * c : 256 * c + local] = sums
    for r in range(rows):
        for s in range(4):
            span = pl.ds(pl.multiple_of((me ^ s) * block, block), block)
            if s == 0:
                tokens = near[r]
            elif s == 1:
                tokens = jnp.concatenate([beside[2 * r][...], beside[2 * r + 1][...]], axis=0)
            else:
                tokens = far[2 * r + s - 2][...]
            product = dot(projs[r][:, span], tokens)
            if r + s == 0:
                total[:size, :] = product
            else:
                total[:size, :] += product
    total[size:, :] = own[...].astype(F32) + swapped[0].astype(F32) + chip[...].astype(F32)
    piece = outs[0].shape[0]
    for s, out in enumerate(outs):
        at = pl.multiple_of((spot ^ s) * piece, piece)
        out[...] = total[pl.ds(at, piece), :].astype(BF16)


def finish_kernel(*refs):
    spot = where_am_i()[2]
    slots, outs = refs[:4], refs[4:]
    for s, slot in enumerate(slots):
        piece = slot.shape[0] // 2
        span = pl.ds(pl.multiple_of((spot ^ s) * piece, piece), piece)
        for k, out in enumerate(outs):
            out[span, :] = slot[k * piece : (k + 1) * piece, :].astype(F32)


def finish_project_kernel(*refs):
    spot = where_am_i()[2]
    slots, (big, small) = refs[:4], refs[4:]
    piece = small.shape[0]
    for s, slot in enumerate(slots):
        at = spot ^ s

        @pl.when(at < 3)
        def _():
            big[pl.ds(pl.multiple_of(at * piece, piece), piece), :] = slot[...].astype(F32)

        @pl.when(at == 3)
        def _():
            small[...] = slot[...].astype(F32)


def first_back_kernel(row, kept, chip, hid, grad_middle, vectors, grad_in, sums):
    width = vectors.shape[1]
    grad_first = sum(part[...].astype(F32) for part in kept) + chip[...].astype(F32)
    scaled, inverse = normalize(hid[:, row * width : (row + 1) * width].astype(F32))
    grad_in[...] = grad_middle[...] + normalize_back(grad_first, scaled, inverse, vectors[0:1, :])
    sums[0:1, :] = jnp.sum(grad_first * scaled, axis=0, keepdims=True)
    sums[1:2, :] = jnp.sum(grad_first, axis=0, keepdims=True)
    sums[2:, :] = jnp.zeros((6, width), F32)


def small_kernel(firsts, middles, out):
    rows = len(firsts)
    out[...] = jnp.zeros_like(out)
    out[0:2, :] = sum(ref[0:2, :] for ref in firsts)
    out[2:6, :] = sum(ref[0:4, :] for ref in middles)


def small_extra_kernel(one, two, in_bias, proj_bias, out):
    out[...] = one[...] + two[...]
    out[6:7, :] = in_bias[...]
    out[7:8, :] = proj_bias[0:1, :]


def finish_small_kernel(one, two, *outs):
    *lines, proj_bias, total = outs
    total[...] = one[...] + two[...]
    width = total.shape[1]
    for k, line in enumerate(lines):
        line[...] = total[k : k + 1, :].reshape(width)
    local = proj_bias.shape[1]
    for c in range(3):
        proj_bias[c : c + 1, :] = total[7:8, 256 * c : 256 * c + local]


def block_out_kernel(own, middle, across, vectors, out):
    total = own[...].astype(F32) + across[...].astype(F32)
    out[...] = (middle[...] + (total + vectors[5:6, :])).astype(BF16)


def swap(values, axis, size, bit):
    return lax.ppermute(values, axis, [(i, i ^ bit) for i in range(size)])


def core_swap(values):
    return swap(values, "tp", 4, 1)


def chip_swap(values):
    return swap(values, "tp", 4, 2)


class Bank:
    def __init__(self, line, slots, size):
        self.line, self.own, self.size = line, slots[0], size
        self.moved = [swap(slots[s], "dp", size, s) for s in range(1, 4)]
        self.bit = 2

    def advance(self):
        (self.own,) = self.line.add([(self.own,), *((v,) for v in self.moved)])
        self.bit *= 2
        if self.bit < self.size:
            self.moved = [swap(self.own, "dp", self.size, self.bit)]
            return
        self.slots = [self.own] + [swap(self.own, "dp", self.size, s) for s in range(1, 4)]

    @property
    def done(self):
        return self.bit >= self.size


def on_device(
    size,
    hidden_in,
    segment_ids,
    cotangent,
    norm1_gain,
    norm1_bias,
    qkv_weight,
    qkv_bias,
    out_weight,
    out_bias,
    norm2_gain,
    norm2_bias,
    ffn_in_weight,
    ffn_in_bias,
    ffn_out_weight,
    ffn_out_bias,
):
    block, rows, width = hidden_in.shape
    length = segment_ids.shape[1]
    local = qkv_weight.shape[2]
    heads = local // HEAD_DIM
    units = ffn_in_weight.shape[1]
    line = Line()
    each, last = range(rows), rows - 1
    full, half, both = shape((block, width)), shape((block // 2, width)), shape((rows, block, width))
    hid = hidden_in.reshape(block, rows * width)
    cots = cotangent.reshape(block, rows * width)
    vector, anywhere = pl.BlockSpec(memory_space=pltpu.VMEM), pl.BlockSpec(memory_space=pltpu.HBM)
    params = [norm1_gain, norm1_bias, out_bias, norm2_gain, norm2_bias, ffn_out_bias, ffn_in_bias]
    vectors, first, alone, *parts = line.run(
        partial(first_norm_kernel, rows, width),
        "first_norm",
        [],
        [hid, *params],
        [shape((8, width), F32), both, full] + [half] * (2 * rows),
        [pltpu.VMEM((width,), BF16)] * 7 + [pltpu.SemaphoreType.DMA((7,))],
        inputs=[vector] + [anywhere] * 7,
    )
    first_across = [chip_swap(alone)]
    first_beside = [core_swap(v) for v in parts]
    passed_in, passed_out = core_swap(ffn_in_weight), core_swap(ffn_out_weight)
    passed_vectors = core_swap(vectors)

    rates = np.power(10000.0, -2.0 * np.arange(HALF) / HEAD_DIM).astype(np.float32)
    windows, marks, waves, proj_bias = line.run(
        partial(table_kernel, block),
        "tables",
        [],
        [segment_ids, jnp.asarray(rates.reshape(HALF, 1)), qkv_bias],
        [
            shape((rows, 2, 16, length)),
            shape((rows, 2, HALF, length), F32),
            shape((3 * local, 1), F32),
        ],
        numbers=[shape((rows * 2 * (length // block),), jnp.int32)],
    )
    proj_weight = jnp.transpose(qkv_weight, (0, 2, 1)).reshape(3 * local, width)

    def project(far, picked, one, *two):
        return line.run(
            partial(project_kernel, far, picked),
            "project",
            [],
            [one, *two, proj_weight, proj_bias, waves],
            [shape((len(picked), 3 * local, 2 * block))],
        )[0]

    def attend(r):
        *outs, log_norm = line.run(
            partial(attend_kernel, r),
            "attend",
            [windows],
            [near, far[r], marks],
            [shape((local, block))] * 2
            + [shape((2, local, block)), shape((8, length), F32)],
            [
                pltpu.VMEM((heads * KEY_ROWS, length), BF16),
                pltpu.VMEM((heads, length, KEY_ROWS), BF16),
                pltpu.VMEM((local, length), BF16),
                pltpu.VMEM((local, length), BF16),
            ],
            vmem=14,
        )
        logs.append(log_norm)
        return [outs[0], outs[1], chip_swap(outs[2])]

    def feed(*tokens):
        tokens = list(tokens)

        def body(*refs):
            feed_kernel(*(refs if len(tokens) == 2 else (refs[0], None, *refs[1:])))

        act, pre, *outs = line.run(
            body,
            "feed",
            [],
            tokens + [ffn_in_weight, ffn_out_weight, vectors, passed_in, passed_out, passed_vectors],
            [shape((block, 2 * units))] * 2 + [full, full],
            vmem=12,
        )
        acts.append(act)
        pres.append(pre)
        return outs

    def pick(values, r):
        def body(values, out):
            out[...] = values[r]

        return line.run(body, "pick", [], [values], [shape(values.shape[1:])])[0]

    near = project(0, tuple(each), first, *first_beside)
    cots = line.run(partial(split_kernel, width), "split", [], [cots], [full] * rows)
    far, far_slots = [], []
    logs, attended = [], []
    for r in each:
        (arrived,) = line.keep(first_across[r])
        far_slots += [arrived, core_swap(arrived)]
        if r < last:
            first_across.append(chip_swap(pick(first, r + 1)))
        if r == last:
            (ready,) = line.keep(out_weight)
            out_across = chip_swap(ready)
            out_beside = core_swap(ready)
        far.append(project(1, (r,), *far_slots[-2:]))
        attended.append(attend(r))

    middles, seconds, pairs = [], [], []
    acts, pres, feeds, feed_grads = [], [], [], []
    for r in each:
        if r == 0:
            (out_far,) = line.keep(out_across)
            out_slots = [out_weight, out_beside, out_far, core_swap(out_far)]
        one, two = line.split(attended[r][1], attended[r][2])
        attended[r][1:] = [one, two]
        middle, second, pair = line.run(
            partial(middle_kernel, r),
            "middle",
            [],
            [hid, *attended[r], *out_slots, vectors, cots[r]],
            [shape((block, width), F32), full, shape((2, block, width))],
        )
        middles.append(middle)
        seconds.append(second)
        pairs.append(chip_swap(pair))
        out, grad = feed(second, cots[r])
        feeds.append([out])
        feed_grads.append([grad])
    for r in each:
        out, grad = feed(pairs[r])
        feeds[r].append(out)
        feed_grads[r].append(chip_swap(grad))

    grad_middles, grad_branches, head_grads, norm_sums = [], [], [], []

    def middle_back(r):
        own, *across = feed_grads[r]
        grad_middle, grad_branch, *parts, sums = line.run(
            partial(middle_back_kernel, len(across)),
            "middle_back",
            [],
            [own, *across, middles[r], cots[r], vectors, *out_slots],
            [shape((block, width), F32), full]
            + [shape((local, block))] * 2
            + [shape((2, local, block)), shape((8, width), F32)],
        )
        grad_middles.append(grad_middle)
        grad_branches.append(grad_branch)
        head_grads.append([parts[0], parts[1], chip_swap(parts[2])])
        norm_sums.append(sums)

    own_sums, passed_sums, own_bias, passed_bias = line.run(
        partial(feed_weights_kernel, 2 * rows),
        "feed_weights",
        [],
        [*seconds, *cots, *pairs, *acts, *pres],
        [
            shape((2, units, width)),
            shape((2, units, width)),
            shape((1, units), F32),
            shape((8, units), F32),
        ],
        [pltpu.VMEM((2 * units, width), F32), pltpu.VMEM((width, 2 * units), F32)],
        vmem=22,
    )
    for r in range(last):
        middle_back(r)
    (passed_sums,) = line.keep(passed_sums)
    passed_sums = core_swap(passed_sums)
    passed_bias = core_swap(passed_bias)
    in_bias_sum, *slots = line.run(
        feed_slots_kernel,
        "feed_slots",
        [],
        [own_sums, passed_sums, own_bias, passed_bias],
        [shape((1, units), F32)] + [shape((units // 2, width))] * 4,
    )
    feed_bank = Bank(line, slots, size)
    middle_back(last)
    head_grads[0][1:] = line.split(*head_grads[0][1:])
    blocks_across = [chip_swap(line.keep(feeds[r][1])[0]) for r in range(last)]

    def block_out(r):
        return line.run(
            block_out_kernel,
            "block_out",
            [],
            [feeds[r][0], middles[r], blocks_across[r], vectors],
            [full],
        )[0]

    def attend_back(r, picked, before):
        final = picked[-1] == heads - 1
        some = len(picked)
        made = local if final else some * HEAD_DIM
        grad_proj, *parts = line.run(
            partial(attend_back_kernel, r, picked),
            "attend_back",
            [windows],
            [near, far[r], marks, logs[r], waves, *head_grads[r]]
            + before
            + ([proj_weight] if final else []),
            [shape((3 * made, length))]
            + ([full, full] if final else [])
            + ([full, full] if final and r == last else [])
            + ([shape((2, block, width))] if final and r < last else []),
            [
                pltpu.VMEM((some * KEY_ROWS, length), BF16),
                pltpu.VMEM((some, length, KEY_ROWS), BF16),
                pltpu.VMEM((some * HEAD_DIM, length), BF16),
                pltpu.VMEM((some, length, HEAD_DIM), BF16),
                pltpu.VMEM((some * HEAD_DIM, length), BF16),
                pltpu.VMEM((some * HEAD_DIM, length), F32),
                pltpu.VMEM((some * HEAD_DIM, length), F32),
                pltpu.VMEM((some * HEAD_DIM, length), F32),
            ],
            vmem=20,
        )
        if not final:
            return [grad_proj]
        projs.append(grad_proj)
        first_grads.append([parts[0], parts[1], *(core_swap(v) for v in parts[2:])])

    projs, first_grads, kepts, backs = [], [], [], []
    for r in each:
        if r > 0:
            head_grads[r][1:] = line.split(*head_grads[r][1:])
        if r == last:
            feed_bank.advance()
            blocks_out = [block_out(k) for k in range(last)]
            out_parts = line.run(
                partial(out_weight_kernel, rows),
                "out_weight",
                [],
                [*sum(attended, []), *grad_branches],
                [shape((local, width))] * 2 + [shape((2, local, width))],
            )
            out_beside = core_swap(out_parts[2])
            (back,) = line.add([(out_parts[1],), (out_beside, 1)])
            out_sums = [out_parts[0], out_beside, chip_swap(back)]
            blocks_across.append(chip_swap(line.keep(feeds[last][1])[0]))
            for k in range(last):
                kept, back = line.add(
                    [(first_grads[k][0],), (first_grads[k][2], 0)],
                    [(first_grads[k][1],), (first_grads[k][2], 1)],
                )
                kepts.append([kept])
                backs.append(back)
        attend_back(r, tuple(range(heads)), [])
    grads_in, first_sums = [], []

    def first_back(r):
        grad_in, sums = line.run(
            lambda *refs: first_back_kernel(r, refs[: len(kepts[r])], *refs[len(kepts[r]) :]),
            "first_back",
            [],
            [*kepts[r], first_across_back[r], hid, grad_middles[r], vectors],
            [shape((block, width), F32), shape((8, width), F32)],
        )
        grads_in.append(grad_in)
        first_sums.append(sums)

    *slots, proj_bias_sum = line.run(
        partial(project_weights_kernel, rows),
        "project_weights",
        [],
        [*projs, first, *first_beside, *far_slots, *out_sums],
        [shape((local, width))] * 4 + [shape((8, width), F32)],
        [pltpu.VMEM((4 * local, width), F32)],
        vmem=10,
    )
    head_bank = Bank(line, slots, size)
    blocks_out.append(block_out(last))
    blocks_out = jnp.stack(blocks_out, axis=1)
    first_across_back = [chip_swap(v) for v in line.keep(*backs)]
    own, across, beside, sent = first_grads[last]
    kepts.append([own, beside])
    (back,) = line.add([(across,), (sent,)])
    first_across_back.append(chip_swap(back))
    while not feed_bank.done:
        feed_bank.advance()
    head_bank.advance()
    for r in each:
        first_back(r)
    input_grad = jnp.stack(grads_in, axis=1)
    (small,) = line.run(
        lambda *refs: small_kernel(refs[:rows], refs[rows : 2 * rows], refs[2 * rows]),
        "small",
        [],
        [*first_sums, *norm_sums],
        [shape((8, width), F32)],
    )
    (small,) = line.add([(small,), (core_swap(small),)])
    (small,) = line.run(
        small_extra_kernel,
        "small_extra",
        [],
        [small, chip_swap(small), in_bias_sum, proj_bias_sum],
        [shape((8, width), F32)],
    )
    while not head_bank.done:
        head_bank.advance()
    bit = 1
    while 2 * bit < size:
        (small,) = line.add([(small,), (swap(small, "dp", size, bit),)])
        bit *= 2
    *lines, grad_proj_bias = line.run(
        finish_small_kernel,
        "finish_small",
        [],
        [small, swap(small, "dp", size, bit)],
        [shape((width,), F32)] * 7 + [shape((3, local), F32)],
        [pltpu.VMEM((8, width), F32)],
    )
    grad_down_weight, grad_in_weight = line.run(
        finish_kernel,
        "finish",
        [],
        feed_bank.slots,
        [shape((units, width), F32), shape((width, units), F32)],
    )
    grad_qkv_weight, grad_out_weight = line.run(
        finish_project_kernel,
        "finish_project",
        [],
        head_bank.slots,
        [shape((3 * local, width), F32), shape((local, width), F32)],
    )
    grad_qkv_weight = jnp.transpose(grad_qkv_weight.reshape(3, local, width), (0, 2, 1))
    return (
        blocks_out,
        input_grad,
        lines[0],
        lines[1],
        grad_qkv_weight,
        grad_proj_bias,
        grad_out_weight,
        lines[5],
        lines[2],
        lines[3],
        grad_in_weight,
        lines[6],
        grad_down_weight,
        lines[4],
    )


def solution(mesh):
    sharded = P("tp", "dp", None)
    return jax.shard_map(
        partial(on_device, mesh.shape["dp"]),
        mesh=mesh,
        in_specs=(
            sharded,
            P("dp", None),
            sharded,
            P(),
            P(),
            P(None, None, "tp"),
            P(None, "tp"),
            P("tp", None),
            P(),
            P(),
            P(),
            P(None, "tp"),
            P("tp"),
            P("tp", None),
            P(),
        ),
        out_specs=(
            sharded,
            sharded,
            P(),
            P(),
            P(None, None, "tp"),
            P(None, "tp"),
            P("tp", None),
            P(),
            P(),
            P(),
            P(None, "tp"),
            P("tp"),
            P("tp", None),
            P(),
        ),
        check_vma=False,
    )
```
